128 devices in a mesh: fsdp: 32 (over y, x, core), tp: 4 (over z).
Axes of the slice: x: 4, y: 4, z: 4, core: 2. Of those that a mesh axis runs over, the one named last changes fastest.
Arguments:
- roll_rows: bfloat16 [1024, 72, 3584], P('fsdp', None, 'tp'), may hold values from -60 to 60
- dest: int32 [1024], P('fsdp'), may hold values from 0 to 1023, as said below
- lengths: int32 [32, 32], P('fsdp'), may hold values from 1 to 72, 768 in all within a row
- clusters: int32 [1024], P('fsdp'), may hold values from 0 to 3
- log_prob_grad: bfloat16 [24576, 3584], P('fsdp', 'tp'), may hold values from -6 to 6
- gain: bfloat16 [3584], replicated, may hold values from 0.5 to 1.5
- w_q: bfloat16 [3584, 2048], P('fsdp', 'tp'), may hold values from -1 to 1
- w_k: bfloat16 [3584, 512], P('fsdp', 'tp'), may hold values from -1 to 1
- w_v: bfloat16 [3584, 512], P('fsdp', 'tp'), may hold values from -0.09375 to 0.09375
- w_o_t: bfloat16 [3584, 2048], P('fsdp', 'tp'), may hold values from -0.125 to 0.125
Outputs:
- input_grad: bfloat16 [24576, 3584], P('fsdp', 'tp')
- grad_q: bfloat16 [3584, 2048], P('fsdp', 'tp')
- grad_k: bfloat16 [3584, 512], P('fsdp', 'tp')
- grad_v: bfloat16 [3584, 512], P('fsdp', 'tp')
- grad_o_t: bfloat16 [3584, 2048], P('fsdp', 'tp')
The draws below stay inside these ranges and needn't reach their ends.
Inputs may be any that keep to these rules, and one draw needn't show every extreme that they name: dest is a permutation; every rollout replica hands exactly 1 completions to every learner, and every learner trains 32 completions. Each learner's 32 lengths sum to 768.
All inputs are finite; a program needn't handle non-finite values.
Results may differ from the reference program's by a relative error of at most 0.03.
Values may be sent and summed in bfloat16 or wider, within the bound.
A program may use at most 128 MiB of HBM per device.

```python
import math
import jax
import jax.numpy as jnp
import numpy as np
from jax import lax

D = 3584
KEY_VALUE_HEADS = 4
HD = 128
QUERY_HEADS = 16
TOK_DEV = 768
SEQ_DEV = 32
GSIZE = 16
NCLUST = 4
TOKENS = 24576
SEQS = 1024
MAXLEN = 72
SEQ_PAIR = 1
QW = 2048
KW = 512
N_FSDP = 32
N_TP = 4


def draw_roll_rows(key, part):
    shape_all = (SEQS, MAXLEN, D)
    row_scale = jnp.exp(jax.random.uniform(jax.random.fold_in(key, 2), (SEQS, MAXLEN, 1), jnp.float32, math.log(0.3), math.log(3.0)))
    col_scale = jnp.exp(jax.random.uniform(jax.random.fold_in(key, 3), (D,), jnp.float32, math.log(0.3), math.log(3.0)))
    noise = jnp.clip(jax.random.normal(jax.random.fold_in(key, 1), shape_all, jnp.float32), -6.0, 6.0)
    values = noise * row_scale * col_scale
    return values.astype(jnp.bfloat16)


def draw_w_q(key, part):
    values = jnp.clip(jax.random.normal(jax.random.fold_in(key, 11), (D, QW), jnp.float32), -6.0, 6.0)
    return (values * D ** (-0.5)).astype(jnp.bfloat16)


def draw_w_k(key, part):
    values = jnp.clip(jax.random.normal(jax.random.fold_in(key, 12), (D, KW), jnp.float32), -6.0, 6.0)
    return (values * D ** (-0.5)).astype(jnp.bfloat16)


def draw_dest(key, part):
    seq_order = jax.random.permutation(jax.random.fold_in(key, 21), SEQ_DEV).astype(jnp.int32)
    residue = seq_order % N_FSDP
    seq_index = jnp.arange(SEQ_DEV, dtype=jnp.int32)
    same_residue = residue[:, None] == residue[None, :]
    rank_of = jnp.sum((same_residue & (seq_index[None, :] < seq_index[:, None])).astype(jnp.int32), axis=1)
    learner = jnp.arange(N_FSDP, dtype=jnp.int32)[:, None]
    replica = (learner + residue[None, :]) % N_FSDP
    local_slot = learner * SEQ_PAIR + rank_of[None, :]
    shuffle_key = jax.random.fold_in(key, 22)
    shuffles = jax.vmap(lambda replica_number: jax.random.permutation(jax.random.fold_in(shuffle_key, replica_number), SEQ_DEV))(jnp.arange(N_FSDP, dtype=jnp.int32)).astype(jnp.int32)
    roll_slot = replica * SEQ_DEV + shuffles[replica, local_slot]
    return jnp.zeros((SEQS,), jnp.int32).at[roll_slot.reshape(SEQS)].set(jnp.arange(SEQS, dtype=jnp.int32))


def plant(values, stream_key, smallest, high):
    place = [jax.random.randint(jax.random.fold_in(stream_key, axis), (), 0, length) for axis, length in enumerate(values.shape)]
    longest = values.shape.index(max(values.shape))
    next_to = place[:longest] + [(place[longest] + 1) % values.shape[longest]] + place[longest + 1:]
    return values.at[tuple(place)].set(smallest).at[tuple(next_to)].set(high)


def level_of(own_key, extent, pieces, smallest, largest):
    level = 1.0
    for dim, shards_of in pieces:
        steps = jax.random.uniform(jax.random.fold_in(jax.random.fold_in(own_key, 6), dim), (shards_of,), jnp.float32, smallest / len(pieces), largest / len(pieces))
        level = level * jnp.repeat(jnp.exp(steps), extent[dim] // shards_of).reshape((-1,) + (1,) * (len(extent) - 1 - dim))
    return level


def rank_table(number_of, lean):
    portions = [(1 << 20) // math.isqrt(grade ** lean) + 1 for grade in range(1, number_of + 1)]
    scale = 1 + sum(portions) // (1 << 30)
    return np.cumsum(np.array([max(1, weight // scale) for weight in portions]))


def skewed_ids(rng, dims, amount, lean):
    grid = rank_table(amount, lean)
    ticket = jax.random.randint(jax.random.fold_in(rng, 1), dims, 0, int(grid[amount - 1]))
    standing = jnp.searchsorted(jnp.asarray(grid, jnp.int32), ticket, side="right")
    return jax.random.permutation(jax.random.fold_in(rng, 2), amount)[standing].astype(jnp.int32)


def split_up(count, total, bound, slope):
    weights = [(1 << 20) // math.isqrt(grade ** slope) + 1 for grade in range(2, count + 1)]
    spare, counts = total - bound - (count - 1), [1] * (count - 1)
    while spare > 0:
        candidates = [i for i in range(count - 1) if counts[i] < bound]
        whole, remaining = sum([weights[i] for i in candidates]), spare
        for i in candidates:
            more = min(bound - counts[i], max(1, remaining * weights[i] // whole), spare)
            counts[i] = counts[i] + more
            spare = spare - more
    return np.array([bound] + counts)


def uneven_parts(own_key, amount, total, limit, skew):
    if amount == 2:
        one = jax.random.randint(own_key, (), max(1, total - limit), min(limit, total - 1) + 1)
        return jnp.stack([one, total - one])
    sizes = jnp.asarray(split_up(amount, total, limit, skew), jnp.int32)
    twos = (amount - 1) // 2
    donor, sink = sizes[1:1 + 2 * twos:2], sizes[2:2 + 2 * twos:2]
    room = jnp.minimum(donor - 1, limit - sink)
    moved = jax.random.randint(jax.random.fold_in(own_key, 1), (twos,), 0, 1 << 20) % (room + 1)
    sizes = sizes.at[1:1 + 2 * twos:2].set(donor - moved).at[2:2 + 2 * twos:2].set(sink + moved)
    return sizes[jax.random.permutation(jax.random.fold_in(own_key, 2), amount)]


def normal_values(rng, shape, scale, most, pieces=(), kind=jnp.bfloat16):
    array = scale * jax.random.normal(rng, shape, jnp.float32)
    if pieces:
        array = array * level_of(rng, shape, pieces, -0.22, 0.18)
    return jnp.clip(array, -most, most).astype(kind)


def setup_inputs(seed: int = 0) -> dict:
    arg_keys = jax.random.split(jax.random.key(seed), 11)
    return {
        "roll_rows": draw_roll_rows(jax.random.fold_in(arg_keys[10], 71), 0),
        "dest": draw_dest(jax.random.fold_in(arg_keys[10], 71), 0),
        "lengths": jax.vmap(lambda own: uneven_parts(own, SEQ_DEV, TOK_DEV, MAXLEN, 2))(jax.random.split(arg_keys[2], N_FSDP)).reshape((N_FSDP, SEQ_DEV)).astype(jnp.int32),
        "clusters": plant(skewed_ids(arg_keys[3], (SEQS,), NCLUST, 2), jax.random.fold_in(arg_keys[3], 3), 0, NCLUST - 1).astype(jnp.int32),
        "log_prob_grad": normal_values(arg_keys[4], (TOKENS, D), 1.0, 6.0, ((0, 32), (1, 4))),
        "gain": jnp.clip(1.0 + 0.1 * jax.random.normal(arg_keys[5], (D,), jnp.float32), 0.5, 1.5).astype(jnp.bfloat16),
        "w_q": draw_w_q(jax.random.fold_in(arg_keys[10], 71), 0),
        "w_k": draw_w_k(jax.random.fold_in(arg_keys[10], 71), 0),
        "w_v": normal_values(arg_keys[8], (D, KW), D ** -0.5, 0.09375, ((0, 32), (1, 4))),
        "w_o_t": normal_values(arg_keys[9], (D, QW), QW ** -0.5, 0.125, ((0, 32), (1, 4))),
    }


ROPE_BASE = 1000000.0
NORM_EPSILON = 1e-06

def wire_round(values):
    return lax.optimization_barrier(values.astype(jnp.bfloat16)).astype(jnp.float32)

def contract_rows(left, right):
    return lax.dot_general(left, right, (((0,), (0,)), ((), ())), preferred_element_type=jnp.float32)

def times_trans(left, right):
    return lax.dot_general(left, right, (((1,), (1,)), ((), ())), preferred_element_type=jnp.float32)

def rotary_tables(position):
    half_width = HD // 2
    frequency = ROPE_BASE ** (-(2.0 * jnp.arange(half_width, dtype=jnp.float32)) / HD)
    angles = position.astype(jnp.float32)[:, None] * frequency[None, :]
    return (jnp.cos(angles)[:, None, :], jnp.sin(angles)[:, None, :])

def rotate(values, rope_cos, rope_sin):
    half_width = values.shape[-1] // 2
    first_half = values[..., :half_width]
    second_half = values[..., half_width:]
    return jnp.concatenate([first_half * rope_cos - second_half * rope_sin, second_half * rope_cos + first_half * rope_sin], axis=-1)

def inverse_rotate(values, rope_cos, rope_sin):
    half_width = values.shape[-1] // 2
    first_half = values[..., :half_width]
    second_half = values[..., half_width:]
    return jnp.concatenate([first_half * rope_cos + second_half * rope_sin, second_half * rope_cos - first_half * rope_sin], axis=-1)

def packed_layout(lengths_row):
    sequence_ends = jnp.cumsum(lengths_row).astype(jnp.int32)
    sequence_starts = sequence_ends - lengths_row
    row_index = jnp.arange(TOK_DEV, dtype=jnp.int32)
    segment = lax.optimization_barrier(jnp.sum((sequence_ends[None, :] <= row_index[:, None]).astype(jnp.int32), axis=1))
    one_hot = segment[:, None] == jnp.arange(SEQ_DEV, dtype=jnp.int32)[None, :]
    position = row_index - lax.optimization_barrier(jnp.sum(jnp.where(one_hot, sequence_starts[None, :], 0), axis=1)).astype(jnp.int32)
    return (segment, position, one_hot)

def group_pass(normed, unit_rows, inverse_norm, gain_float, grad_round, rope_cos, rope_sin, allowed, weight_q, weight_k, weight_v, weight_o):
    row_count = normed.shape[0]
    key_heads = weight_k.shape[1] // HD
    queries_per_group = QUERY_HEADS // KEY_VALUE_HEADS
    query_lin = jnp.dot(normed, weight_q, preferred_element_type=jnp.float32)
    key_lin = jnp.dot(normed, weight_k, preferred_element_type=jnp.float32)
    value_lin = jnp.dot(normed, weight_v, preferred_element_type=jnp.float32)
    query_rot = rotate(query_lin.reshape(row_count, key_heads * queries_per_group, HD), rope_cos, rope_sin).astype(jnp.bfloat16).reshape(row_count, key_heads, queries_per_group, HD)
    key_rot = rotate(key_lin.reshape(row_count, key_heads, HD), rope_cos, rope_sin).astype(jnp.bfloat16)
    value_b = value_lin.reshape(row_count, key_heads, HD).astype(jnp.bfloat16)
    scores = jnp.einsum('ighd,jgd->ghij', query_rot.astype(jnp.float32), key_rot.astype(jnp.float32)) * HD ** (-0.5)
    scores = jnp.where(allowed, scores, -1e+30)
    row_max = lax.optimization_barrier(jnp.max(scores, axis=-1, keepdims=True))
    exp_scores = jnp.where(allowed, jnp.exp(scores - row_max), 0.0)
    attn_prob = exp_scores / lax.optimization_barrier(jnp.sum(exp_scores, axis=-1, keepdims=True))
    attn_prob_b = attn_prob.astype(jnp.bfloat16)
    attn_out = jnp.einsum('ghij,jgd->ighd', attn_prob_b.astype(jnp.float32), value_b.astype(jnp.float32))
    attn_out = attn_out.reshape(row_count, key_heads * queries_per_group * HD).astype(jnp.bfloat16)
    grad_wo = contract_rows(grad_round, attn_out)
    grad_attn = jnp.dot(grad_round, weight_o, preferred_element_type=jnp.float32).astype(jnp.bfloat16)
    grad_attn = grad_attn.reshape(row_count, key_heads, queries_per_group, HD)
    grad_prob = jnp.einsum('ighd,jgd->ghij', grad_attn.astype(jnp.float32), value_b.astype(jnp.float32))
    grad_value_f = jnp.einsum('ghij,ighd->jgd', attn_prob_b.astype(jnp.float32), grad_attn.astype(jnp.float32))
    row_delta = lax.optimization_barrier(jnp.sum(attn_prob * grad_prob, axis=-1, keepdims=True))
    grad_score = (attn_prob * (grad_prob - row_delta) * HD ** (-0.5)).astype(jnp.bfloat16)
    grad_qrot = jnp.einsum('ghij,jgd->ighd', grad_score.astype(jnp.float32), key_rot.astype(jnp.float32))
    grad_qrot = grad_qrot.reshape(row_count, key_heads * queries_per_group, HD)
    grad_krot = jnp.einsum('ghij,ighd->jgd', grad_score.astype(jnp.float32), query_rot.astype(jnp.float32))
    grad_query = inverse_rotate(grad_qrot, rope_cos, rope_sin).astype(jnp.bfloat16).reshape(row_count, -1)
    grad_key = inverse_rotate(grad_krot, rope_cos, rope_sin).astype(jnp.bfloat16).reshape(row_count, -1)
    grad_value = grad_value_f.astype(jnp.bfloat16).reshape(row_count, -1)
    grads = (contract_rows(normed, grad_query), contract_rows(normed, grad_key), contract_rows(normed, grad_value), grad_wo)
    grad_normed = times_trans(grad_query, weight_q) + times_trans(grad_key, weight_k) + times_trans(grad_value, weight_v)
    grad_hat = grad_normed * gain_float
    grad_in = inverse_norm * (grad_hat - unit_rows * lax.optimization_barrier(jnp.mean(grad_hat * unit_rows, axis=1, keepdims=True)))
    return (grad_in, grads)

def reference(roll_rows, dest, lengths, clusters, log_prob_grad, gain, w_q, w_k, w_v, w_o_t):
    slot_of = jnp.zeros((SEQS,), jnp.int32).at[dest].set(jnp.arange(SEQS, dtype=jnp.int32))
    ballots = clusters.reshape(SEQS // GSIZE, GSIZE)
    vote_share = lax.optimization_barrier(jnp.mean((ballots[:, :, None] == ballots[:, None, :]).astype(jnp.float32), axis=2))
    advantage = (vote_share - lax.optimization_barrier(jnp.mean(vote_share, axis=1, keepdims=True))).reshape(SEQS).astype(jnp.bfloat16)
    flat_rows = roll_rows.reshape(SEQS * MAXLEN, D)
    gain_float = gain.astype(jnp.float32)
    q_cols = QW // N_TP
    k_cols = KW // N_TP

    def learner(totals, inputs):
        lengths_row, slots_row, cotangent = inputs
        segment, position, one_hot = packed_layout(lengths_row)
        slot_rows = lax.optimization_barrier(jnp.sum(jnp.where(one_hot, slots_row[None, :], 0), axis=1)).astype(jnp.int32)
        packed = jnp.take(flat_rows, slot_rows * MAXLEN + position, axis=0)
        row_advantage = jnp.take(advantage, slot_rows).astype(jnp.float32)
        inputs_float = packed.astype(jnp.float32)
        inverse_norm = lax.rsqrt(lax.optimization_barrier(jnp.mean(inputs_float * inputs_float, axis=1, keepdims=True)) + NORM_EPSILON)
        unit_rows = inputs_float * inverse_norm
        normed = (unit_rows * gain_float).astype(jnp.bfloat16)
        rope_cos, rope_sin = rotary_tables(position)
        allowed = (segment[:, None] == segment[None, :]) & (position[None, :] <= position[:, None])
        grad_out = row_advantage[:, None] * cotangent.astype(jnp.float32)
        grad_round = grad_out.astype(jnp.bfloat16)
        input_sum = grad_out
        stores = ([], [], [], [])
        for member in range(N_TP):
            q_span = slice(member * q_cols, (member + 1) * q_cols)
            k_span = slice(member * k_cols, (member + 1) * k_cols)
            grad_in, grads = group_pass(normed, unit_rows, inverse_norm, gain_float, grad_round, rope_cos, rope_sin, allowed, w_q[:, q_span], w_k[:, k_span], w_v[:, k_span], w_o_t[:, q_span])
            input_sum = input_sum + wire_round(grad_in)
            for store, term in zip(stores, grads):
                store.append(term)
        learner_terms = tuple((wire_round(jnp.concatenate(store, axis=1)) for store in stores))
        totals = tuple((running + term for running, term in zip(totals, learner_terms)))
        return (totals, input_sum.astype(jnp.bfloat16))
    initial = (jnp.zeros((D, QW), jnp.float32), jnp.zeros((D, KW), jnp.float32), jnp.zeros((D, KW), jnp.float32), jnp.zeros((D, QW), jnp.float32))
    totals, input_rows = lax.scan(learner, initial, (lengths, slot_of.reshape(N_FSDP, SEQ_DEV), log_prob_grad.reshape(N_FSDP, TOK_DEV, D)))
    return (input_rows.reshape(TOKENS, D), totals[0].astype(jnp.bfloat16), totals[1].astype(jnp.bfloat16), totals[2].astype(jnp.bfloat16), totals[3].astype(jnp.bfloat16))
```

```python
import jax
import jax.numpy as jnp
import numpy as np
from jax import lax
from jax.experimental import pallas as pl
from jax.experimental.pallas import tpu as pltpu
from jax.sharding import PartitionSpec as P

HD = 128
GSIZE = 16
ROPE_BASE = 1000000.0
NORM_EPSILON = 1e-06
MESH = pl.DeviceIdType.MESH
BF = jnp.bfloat16
F32 = jnp.float32
HBM = pl.BlockSpec(memory_space=pl.ANY)
VMEM = pl.BlockSpec(memory_space=pltpu.VMEM)
SMEM = pl.BlockSpec(memory_space=pltpu.SMEM)
DMA = pltpu.SemaphoreType.DMA
LIMIT = 56 * 2**20

N_F = 32
N_Z = 4
SEQ = 32
MAXLEN = 72
TOK = 768
HALF = TOK // 2
FB = 896
D = 3584
QC = 512
KC = 128
TB = 128

CHIPS = [(0, 1), (1, 0), (0, 3), (3, 0), (1, 1), (3, 3), (1, 3), (3, 1),
         (0, 2), (2, 0), (1, 2), (2, 1), (3, 2), (2, 3), (2, 2)]
OFFSETS = [(0, 0, 1)] + [(a, b, c) for c in range(2) for a, b in CHIPS]


def nt(a, b):
    return lax.dot_general(a, b, (((1,), (1,)), ((), ())), preferred_element_type=F32)


def tn(a, b):
    return lax.dot_general(a, b, (((0,), (0,)), ((), ())), preferred_element_type=F32)


def nn(a, b):
    return lax.dot_general(a, b, (((1,), (0,)), ((), ())), preferred_element_type=F32)


def iota(shape, dim):
    return lax.broadcasted_iota(jnp.int32, shape, dim)


def stage_kernel(dest_s, dest_r, clus_r, clus_c, roll, send, meta, sem):
    def start(s, c):
        t = dest_s[s] // SEQ
        pltpu.make_async_copy(roll.at[s], send.at[t], sem.at[s]).start()
        return c

    lax.fori_loop(0, SEQ, start, 0)
    same = (clus_c[...] == clus_r[...]) & (iota((SEQ, SEQ), 0) // GSIZE == iota((SEQ, SEQ), 1) // GSIZE)
    group = iota((SEQ, SEQ), 0) // GSIZE == iota((SEQ, SEQ), 1) // GSIZE
    same = jnp.where(same, 1.0 / GSIZE, 0.0)
    share_c = jnp.sum(same, axis=1, keepdims=True)
    share_r = jnp.sum(same, axis=0, keepdims=True)
    mean_r = jnp.sum(jnp.where(group, share_c, 0.0), axis=0, keepdims=True) * (1.0 / GSIZE)
    adv_r = (share_r - mean_r).astype(BF).astype(F32)
    rows = iota((SEQ * 8, SEQ), 0)
    dest_v = dest_r[...]
    hit = dest_v // SEQ == rows // 8
    what = jnp.where(rows % 8 < 4, (dest_v % SEQ).astype(F32), adv_r)
    meta[...] = jnp.broadcast_to(jnp.sum(jnp.where(hit, what, 0.0), axis=1, keepdims=True), (SEQ * 8, 128))

    def wait(s, c):
        t = dest_s[s] // SEQ
        pltpu.make_async_copy(roll.at[s], send.at[t], sem.at[s]).wait()
        return c

    lax.fori_loop(0, SEQ, wait, 0)


def ring_copy(src, dst, blk, half, to, ss, rs, i):
    sl = pl.ds(half * HALF, HALF)
    return pltpu.make_async_remote_copy(
        src_ref=src.at[sl], dst_ref=dst.at[blk, sl], send_sem=ss.at[i], recv_sem=rs.at[i],
        device_id={"tp": to}, device_id_type=MESH)


def ring_start(own, dst, z, ss, rs):
    right, left = lax.rem(z + 1, N_Z), lax.rem(z + 3, N_Z)
    c = [ring_copy(own, dst, z, 0, right, ss, rs, 0), ring_copy(own, dst, z, 1, left, ss, rs, 1),
         ring_copy(own, dst, z, 1, right, ss, rs, 2), ring_copy(own, dst, z, 0, left, ss, rs, 3)]
    for x in c:
        x.start()
    return c


def ring_end(own, dst, z, ss, rs, c):
    right, left, far = lax.rem(z + 1, N_Z), lax.rem(z + 3, N_Z), lax.rem(z + 2, N_Z)
    ring_copy(own, dst, left, 0, right, ss, rs, 0).wait_recv()
    f0 = ring_copy(dst.at[left], dst, left, 0, right, ss, rs, 4)
    f0.start()
    ring_copy(own, dst, right, 1, left, ss, rs, 1).wait_recv()
    f1 = ring_copy(dst.at[right], dst, right, 1, left, ss, rs, 5)
    f1.start()
    ring_copy(own, dst, left, 1, right, ss, rs, 2).wait_recv()
    ring_copy(own, dst, right, 0, left, ss, rs, 3).wait_recv()
    ring_copy(own, dst, far, 0, right, ss, rs, 4).wait_recv()
    ring_copy(own, dst, far, 1, left, ss, rs, 5).wait_recv()
    for x in c + [f0, f1]:
        x.wait_send()


def hand_kernel(send, meta, cot, out, meta_out, cot_full, lsem, ss, rs, ms, mr, zs, zr):
    me = lax.axis_index("fsdp")
    z = lax.axis_index("tp")
    y, x, c = me // 8, (me // 2) % 4, me % 2

    def peer(o, s):
        return lax.rem(y + s * o[0] + 4, 4) * 8 + lax.rem(x + s * o[1] + 4, 4) * 2 + lax.rem(c + s * o[2] + 2, 2)

    barrier = pltpu.get_barrier_semaphore()
    for o in OFFSETS:
        pl.semaphore_signal(barrier, inc=1, device_id={"fsdp": peer(o, 1)}, device_id_type=MESH)
    for d in (1, 3):
        pl.semaphore_signal(barrier, inc=1, device_id={"tp": lax.rem(z + d, N_Z)}, device_id_type=MESH)
    pl.semaphore_wait(barrier, len(OFFSETS) + 2)
    mine = [pltpu.make_async_copy(send.at[me], out.at[me], lsem.at[0]),
            pltpu.make_async_copy(meta.at[pl.ds(8 * me, 8)], meta_out.at[pl.ds(8 * me, 8)], lsem.at[1]),
            pltpu.make_async_copy(cot, cot_full.at[z], lsem.at[2])]
    ring = ring_start(cot, cot_full, z, zs, zr)

    def slab(i, frm, to, who):
        return pltpu.make_async_remote_copy(
            src_ref=send.at[frm], dst_ref=out.at[to], send_sem=ss.at[i], recv_sem=rs.at[i],
            device_id={"fsdp": who}, device_id_type=MESH)

    def note(i, frm, to, who):
        return pltpu.make_async_remote_copy(
            src_ref=meta.at[pl.ds(8 * frm, 8)], dst_ref=meta_out.at[pl.ds(8 * to, 8)],
            send_sem=ms.at[i], recv_sem=mr.at[i], device_id={"fsdp": who}, device_id_type=MESH)

    for i, o in enumerate(OFFSETS):
        t = peer(o, 1)
        slab(i, t, me, t).start()
        note(i, t, me, t).start()
    for m in mine:
        m.start()
    ring_end(cot, cot_full, z, zs, zr, ring)
    for i, o in enumerate(OFFSETS):
        t, f = peer(o, 1), peer(o, -1)
        slab(i, t, f, t).wait_recv()
        note(i, t, f, t).wait_recv()
        slab(i, t, me, t).wait_send()
        note(i, t, me, t).wait_send()
    for m in mine:
        m.wait()


def pack_kernel(rows, meta, len_c, gain, table, packed, scaled, squares, rope, pos_b, adv_b, keys):
    lane = iota((SEQ, 128), 1)
    sub = iota((SEQ, 128), 0)
    lens = len_c[...].astype(F32)
    ends = jnp.sum(jnp.where(sub <= lane, lens, 0.0), axis=0, keepdims=True)
    starts = jnp.sum(jnp.where(sub < lane, lens, 0.0), axis=0, keepdims=True)
    place = meta[pl.ds(0, SEQ, 8), :]
    share = meta[pl.ds(4, SEQ, 8), :]
    one = iota((1, 128), 1)
    place_r = jnp.where(one < SEQ, jnp.sum(jnp.where(sub == lane, place, 0.0), axis=0, keepdims=True), -1.0)
    share_r = jnp.sum(jnp.where(sub == lane, share, 0.0), axis=0, keepdims=True)
    column = iota((SEQ, SEQ * MAXLEN), 1)
    source = iota((SEQ, SEQ * MAXLEN), 0)
    here = (column >= source * MAXLEN) & (column < (source + 1) * MAXLEN)
    key = place[:, :1] * 128.0 + (column - source * MAXLEN).astype(F32)
    keys[...] = jnp.sum(jnp.where(here, key, 0.0), axis=0, keepdims=True)

    def block(b, c):
        at = pl.ds(pl.multiple_of(b * TB, TB), TB)
        i = (iota((TB, 128), 0) + b * TB).astype(F32)
        lane_f = iota((TB, 128), 1).astype(F32)
        hit = (i >= starts) & (i < ends)
        seg = jnp.sum(jnp.where(hit, lane_f, 0.0), axis=1, keepdims=True)
        start = jnp.sum(jnp.where(hit, starts, 0.0), axis=1, keepdims=True)
        pos = i - start
        pos_b[at, :] = pos
        adv_b[at, :] = jnp.broadcast_to(
            jnp.sum(jnp.where(place_r == seg, share_r, 0.0), axis=1, keepdims=True), (TB, 128))
        rope[at, :] = lax.dot_general(
            jnp.where(pos == lane_f, 1.0, 0.0), table[...], (((1,), (0,)), ((), ())),
            precision=lax.Precision.HIGHEST, preferred_element_type=F32)
        pick = jnp.where(seg * 128.0 + pos[:, :1] == keys[...], 1.0, 0.0).astype(BF)
        took = nn(pick, rows[...])
        packed[at, :] = took.astype(BF)
        scaled[at, :] = (took * gain[...].astype(F32)).astype(BF)
        square = jnp.sum(took * took, axis=1, keepdims=True)
        squares[:, at] = jnp.transpose(jnp.broadcast_to(square, (TB, 128)))[:8, :]
        return c

    lax.fori_loop(0, TOK // TB, block, 0)


def gather_kernel(own, sq, full, sq_full, lsem, zs, zr, qs, qr):
    z = lax.axis_index("tp")
    barrier = pltpu.get_barrier_semaphore()
    for d in (1, 2, 3):
        pl.semaphore_signal(barrier, inc=1, device_id={"tp": lax.rem(z + d, N_Z)}, device_id_type=MESH)
    pl.semaphore_wait(barrier, 3)
    mine = [pltpu.make_async_copy(own, full.at[z], lsem.at[0]), pltpu.make_async_copy(sq, sq_full.at[z], lsem.at[1])]
    ring = ring_start(own, full, z, zs, zr)

    def note(d, blk):
        return pltpu.make_async_remote_copy(
            src_ref=sq, dst_ref=sq_full.at[blk], send_sem=qs.at[d], recv_sem=qr.at[d],
            device_id={"tp": lax.rem(z + d, N_Z)}, device_id_type=MESH)

    for d in (1, 2, 3):
        note(d, z).start()
    for m in mine:
        m.start()
    ring_end(own, full, z, zs, zr, ring)
    for d in (1, 2, 3):
        note(d, lax.rem(z + N_Z - d, N_Z)).wait_recv()
        note(d, z).wait_send()
    for m in mine:
        m.wait()


def unstack(v):
    return jnp.concatenate([v[h * TB:(h + 1) * TB] for h in range(4)], axis=1)


def stack(v):
    return jnp.concatenate([v[:, h * HD:(h + 1) * HD] for h in range(4)], axis=0)


def turn(v, cos, sin):
    return v * cos + jnp.concatenate([v[:, HD // 2:], v[:, :HD // 2]], axis=1) * sin


def turn_back(v, cos, sin):
    return v * cos - jnp.concatenate([v[:, HD // 2:], v[:, :HD // 2]], axis=1) * sin


def block_kernel(xf, cf, wf, sq, rope, pos_b, adv_b, grads, outs, inv_b, dots,
                 xv, cv, wv, sem, lin, ga, qrot, kbuf, vbuf, gab, dk, dv, mq):
    copies = []
    for b in range(N_Z):
        copies.append([pltpu.make_async_copy(xf.at[b], xv.at[b], sem.at[b, 0]),
                       pltpu.make_async_copy(cf.at[b], cv.at[b], sem.at[b, 1]),
                       pltpu.make_async_copy(wf.at[b], wv.at[b], sem.at[b, 2])])
        for k in copies[-1]:
            k.start()
    total = sq[0] + sq[1] + sq[2] + sq[3]
    inv_t = lax.rsqrt(total * (1.0 / D) + NORM_EPSILON)
    for b in range(TOK // TB):
        inv_b[b * TB:(b + 1) * TB, :] = jnp.transpose(jnp.broadcast_to(inv_t[:1, b * TB:(b + 1) * TB], (128, TB)))
    kbuf[...] = jnp.zeros_like(kbuf)
    vbuf[...] = jnp.zeros_like(vbuf)
    dk[...] = jnp.zeros_like(dk)
    dv[...] = jnp.zeros_like(dv)
    lin[...] = jnp.zeros_like(lin)
    ga[...] = jnp.zeros_like(ga)
    for b in range(N_Z):
        for k in copies[b]:
            k.wait()
    def project(b, c):
        for n in range(3):
            lin[:, n * 256:(n + 1) * 256] += nn(xv[b], wv[b, :, n * 256:(n + 1) * 256])
        for n in range(2):
            ga[:, n * 256:(n + 1) * 256] += nn(cv[b], wv[b, :, 768 + n * 256:768 + (n + 1) * 256])
        return c

    lax.fori_loop(0, N_Z, project, 0)

    def ready(b, c):
        at = pl.ds(pl.multiple_of(b * TB, TB), TB)
        up = pl.ds(pl.multiple_of(b * TB + TB, TB), TB)
        inv = inv_b[at, :]
        cos, sin = rope[at, :HD], rope[at, HD:]
        for h in range(4):
            qrot[at, h * HD:(h + 1) * HD] = turn(lin[at, h * HD:(h + 1) * HD] * inv, cos, sin).astype(BF)
            gab[at, h * HD:(h + 1) * HD] = (ga[at, h * HD:(h + 1) * HD] * adv_b[at, :]).astype(BF)
        kbuf[up, :] = turn(lin[at, QC:QC + KC] * inv, cos, sin).astype(BF)
        vbuf[up, :] = (lin[at, QC + KC:] * inv).astype(BF)
        return c

    lax.fori_loop(0, TOK // TB, ready, 0)
    scale = HD ** (-0.5)

    def attend(b, c):
        at = pl.ds(pl.multiple_of(b * TB, TB), TB)
        win = pl.ds(pl.multiple_of(b * TB, TB), 2 * TB)
        q = stack(qrot[at, :])
        g = stack(gab[at, :])
        k, v = kbuf[win, :], vbuf[win, :]
        back = iota((TB, 2 * TB), 0) + TB - iota((TB, 2 * TB), 1)
        ok = (back >= 0) & (back.astype(F32) <= pos_b[at, :1])
        ok = jnp.concatenate([ok] * 4, axis=0)
        s = jnp.where(ok, nt(q, k) * scale, -1e30)
        e = jnp.where(ok, jnp.exp(s - jnp.max(s, axis=1, keepdims=True)), 0.0)
        p = e / jnp.sum(e, axis=1, keepdims=True)
        pb = p.astype(BF)
        o = unstack(nn(pb, v))
        dp = nt(g, v)
        ds = (p * (dp - jnp.sum(p * dp, axis=1, keepdims=True)) * scale).astype(BF)
        dq = nn(ds, k)
        dk[win, :] += tn(ds, q)
        dv[win, :] += tn(pb, g)
        prod = dq * q.astype(F32)
        mq[at, :] = prod[:TB] + prod[TB:2 * TB] + prod[2 * TB:3 * TB] + prod[3 * TB:]
        dq = unstack(dq)
        inv = inv_b[at, :]
        cos, sin = rope[at, :HD], rope[at, HD:]
        for h in range(4):
            col = slice(h * HD, (h + 1) * HD)
            grads[at, col] = (turn_back(dq[:, col], cos, sin) * inv).astype(BF)
            outs[at, col] = (o[:, col] * adv_b[at, :]).astype(BF)
        return c

    lax.fori_loop(0, TOK // TB, attend, 0)

    def finish(b, c):
        at = pl.ds(pl.multiple_of(b * TB, TB), TB)
        up = pl.ds(pl.multiple_of(b * TB + TB, TB), TB)
        inv = inv_b[at, :]
        cos, sin = rope[at, :HD], rope[at, HD:]
        gk, gv = dk[up, :], dv[up, :]
        grads[at, QC:QC + KC] = (turn_back(gk, cos, sin) * inv).astype(BF)
        grads[at, QC + KC:] = (gv * inv).astype(BF)
        m = mq[at, :] + gk * kbuf[up, :].astype(F32) + gv * vbuf[up, :].astype(F32)
        m = jnp.sum(m, axis=1, keepdims=True) * inv
        dots[:, at] = jnp.transpose(m)[:8, :]
        return c

    lax.fori_loop(0, TOK // TB, finish, 0)


def input_kernel(grads, wf, dots, packed, lpg, gain, inv_b, adv_b, result,
                 wv, dots_all, sbuf, rbuf, own, wsem, zs, zr, ds_, dr):
    z = lax.axis_index("tp")
    right, left, far = lax.rem(z + 1, N_Z), lax.rem(z + 3, N_Z), lax.rem(z + 2, N_Z)
    order = [far, right, left, z]
    loads = [pltpu.make_async_copy(wf.at[t, :, pl.ds(0, QC + 2 * KC)], wv.at[i], wsem.at[i]) for i, t in enumerate(order)]
    for k in loads:
        k.start()
    barrier = pltpu.get_barrier_semaphore()
    for d in (1, 2, 3):
        pl.semaphore_signal(barrier, inc=1, device_id={"tp": lax.rem(z + d, N_Z)}, device_id_type=MESH)
    pl.semaphore_wait(barrier, 3)

    def note(d, blk):
        return pltpu.make_async_remote_copy(
            src_ref=dots, dst_ref=dots_all.at[d - 1], send_sem=ds_.at[d], recv_sem=dr.at[d],
            device_id={"tp": lax.rem(z + d, N_Z)}, device_id_type=MESH)

    for d in (1, 2, 3):
        note(d, z).start()

    def ship(i, to):
        return pltpu.make_async_remote_copy(
            src_ref=sbuf.at[i], dst_ref=rbuf.at[i], send_sem=zs.at[i], recv_sem=zr.at[i],
            device_id={"tp": to}, device_id_type=MESH)

    def share(i, h):
        return nt(grads[h * HALF:(h + 1) * HALF, :], wv[i])

    loads[0].wait()
    sbuf[0] = share(0, 0).astype(BF)
    ship(0, right).start()
    sbuf[1] = share(0, 1).astype(BF)
    ship(1, left).start()
    loads[1].wait()
    sbuf[2] = share(1, 1).astype(BF)
    ship(2, right).start()
    loads[2].wait()
    sbuf[3] = share(2, 0).astype(BF)
    ship(3, left).start()
    a = share(1, 0)
    ship(0, right).wait_recv()
    sbuf[4] = (a + rbuf[0].astype(F32)).astype(BF)
    ship(4, right).start()
    a = share(2, 1)
    ship(1, left).wait_recv()
    sbuf[5] = (a + rbuf[1].astype(F32)).astype(BF)
    ship(5, left).start()
    loads[3].wait()
    own[:HALF] = share(3, 0)
    own[HALF:] = share(3, 1)
    for d in (1, 2, 3):
        note(d, z).wait_recv()
        note(d, z).wait_send()
    m = (dots[...] + dots_all[0] + dots_all[1] + dots_all[2]) * (1.0 / D)
    ship(2, right).wait_recv()
    ship(3, left).wait_recv()
    ship(4, right).wait_recv()
    ship(5, left).wait_recv()
    for b in range(TOK // TB):
        h, r = divmod(b * TB, HALF)
        at = slice(b * TB, (b + 1) * TB)
        hs = slice(r, r + TB)
        one, two = (4, 3) if h == 0 else (2, 5)
        s = own[at, :] + rbuf[one, hs, :].astype(F32) + rbuf[two, hs, :].astype(F32)
        mc = jnp.transpose(jnp.broadcast_to(m[:1, at], (128, TB)))[:, :1]
        inv = inv_b[at, :1]
        result[at, :] = (adv_b[at, :1] * lpg[at, :].astype(F32) + s * gain[...].astype(F32)
                         - packed[at, :].astype(F32) * (inv * mc)).astype(BF)
    for i in range(6):
        ship(i, right if i % 2 == 0 else left).wait_send()


def sds(shape, dtype=BF):
    return jax.ShapeDtypeStruct(shape, dtype)


def params(**kw):
    return pltpu.CompilerParams(vmem_limit_bytes=LIMIT, has_side_effects=True, **kw)


def rope_table():
    i = np.arange(HD // 2, dtype=np.float32)
    frequency = np.float32(ROPE_BASE) ** (-(np.float32(2.0) * i) / np.float32(HD))
    angle = np.arange(128, dtype=np.float32)[:, None] * frequency[None, :]
    c, s = np.cos(angle), np.sin(angle)
    return np.concatenate([c, c, -s, s], axis=1).astype(np.float32)


def per_device(roll_rows, dest, lengths, clusters, log_prob_grad, gain, w_q, w_k, w_v, w_o_t):
    z = lax.axis_index("tp")
    weights = lax.all_gather(jnp.concatenate([w_q, w_k, w_v, w_o_t], axis=1), "fsdp", axis=0, tiled=True)
    weights = weights.reshape(N_Z, FB, QC * 2 + KC * 2)
    gain_own = lax.dynamic_slice(gain, (z * FB,), (FB,)).reshape(1, FB)
    send, meta = pl.pallas_call(
        stage_kernel, out_shape=(sds((SEQ, MAXLEN, FB)), sds((SEQ * 8, 128), F32)),
        in_specs=[SMEM, VMEM, VMEM, VMEM, HBM], out_specs=(HBM, VMEM),
        scratch_shapes=[DMA((SEQ,))], compiler_params=params(),
    )(dest, dest.reshape(1, SEQ), clusters.reshape(1, SEQ), clusters.reshape(SEQ, 1), roll_rows)
    n_o = len(OFFSETS)
    arrived, meta_in, cot = pl.pallas_call(
        hand_kernel, out_shape=(sds((SEQ, MAXLEN, FB)), sds((SEQ * 8, 128), F32), sds((N_Z, TOK, FB))),
        in_specs=[HBM, HBM, HBM], out_specs=(HBM, HBM, HBM),
        scratch_shapes=[DMA((3,)), DMA((n_o,)), DMA((n_o,)), DMA((n_o,)), DMA((n_o,)), DMA((6,)), DMA((6,))],
        compiler_params=params(collective_id=0),
    )(send, meta, log_prob_grad)
    packed, scaled, squares, rope, pos_b, adv_b = pl.pallas_call(
        pack_kernel,
        out_shape=(sds((TOK, FB)), sds((TOK, FB)), sds((8, TOK), F32), sds((TOK, 2 * HD), F32),
                   sds((TOK, 128), F32), sds((TOK, 128), F32)),
        in_specs=[VMEM] * 5, out_specs=(VMEM,) * 6,
        scratch_shapes=[pltpu.VMEM((1, SEQ * MAXLEN), F32)], compiler_params=params(),
    )(arrived.reshape(SEQ * MAXLEN, FB), meta_in, lengths.reshape(SEQ, 1), gain_own, jnp.asarray(rope_table()))
    rows, sq = pl.pallas_call(
        gather_kernel, out_shape=(sds((N_Z, TOK, FB)), sds((N_Z, 8, TOK), F32)),
        in_specs=[HBM, HBM], out_specs=(HBM, HBM),
        scratch_shapes=[DMA((2,)), DMA((6,)), DMA((6,)), DMA((4,)), DMA((4,))],
        compiler_params=params(collective_id=1),
    )(scaled, squares)
    grads, outs, inv_b, dots = pl.pallas_call(
        block_kernel,
        out_shape=(sds((TOK, QC + 2 * KC)), sds((TOK, QC)), sds((TOK, 128), F32), sds((8, TOK), F32)),
        in_specs=[HBM, HBM, HBM] + [VMEM] * 4, out_specs=(VMEM,) * 4,
        scratch_shapes=[
            pltpu.VMEM((N_Z, TOK, FB), BF), pltpu.VMEM((N_Z, TOK, FB), BF),
            pltpu.VMEM((N_Z, FB, 2 * QC + 2 * KC), BF), DMA((N_Z, 3)),
            pltpu.VMEM((TOK, QC + 2 * KC), F32), pltpu.VMEM((TOK, QC), F32),
            pltpu.VMEM((TOK, QC), BF), pltpu.VMEM((TOK + TB, HD), BF), pltpu.VMEM((TOK + TB, HD), BF),
            pltpu.VMEM((TOK, QC), BF), pltpu.VMEM((TOK + TB, HD), F32), pltpu.VMEM((TOK + TB, HD), F32),
            pltpu.VMEM((TOK, HD), F32)],
        compiler_params=params(),
    )(rows, cot, weights, sq, rope, pos_b, adv_b)
    def terms(left, right):
        t = lax.dot_general(left, right, (((1,), (0,)), ((), ())), preferred_element_type=F32)
        return t.astype(BF).reshape(D, right.shape[1])

    total = lax.psum_scatter(
        jnp.concatenate([terms(rows, grads), terms(cot, outs)], axis=1), "fsdp", scatter_dimension=0, tiled=True)
    input_grad = pl.pallas_call(
        input_kernel, out_shape=sds((TOK, FB)),
        in_specs=[VMEM, HBM] + [VMEM] * 6, out_specs=VMEM,
        scratch_shapes=[
            pltpu.VMEM((N_Z, FB, QC + 2 * KC), BF), pltpu.VMEM((3, 8, TOK), F32),
            pltpu.VMEM((6, HALF, FB), BF), pltpu.VMEM((6, HALF, FB), BF), pltpu.VMEM((TOK, FB), F32),
            DMA((N_Z,)), DMA((6,)), DMA((6,)), DMA((4,)), DMA((4,))],
        compiler_params=params(collective_id=2),
    )(grads, weights, dots, packed, log_prob_grad, gain_own, inv_b, adv_b)
    a, b, c = QC, QC + KC, QC + 2 * KC
    return (input_grad, total[:, :a], total[:, a:b], total[:, b:c], total[:, c:])


def solution(mesh):
    in_specs = (
        P("fsdp", None, "tp"), P("fsdp"), P("fsdp", None), P("fsdp"), P("fsdp", "tp"), P(),
        P("fsdp", "tp"), P("fsdp", "tp"), P("fsdp", "tp"), P("fsdp", "tp"),
    )
    out_specs = (P("fsdp", "tp"),) * 5
    return jax.shard_map(per_device, mesh=mesh, in_specs=in_specs, out_specs=out_specs, check_vma=False)
```

```python
import jax
import jax.numpy as jnp
import numpy as np
from jax import lax
from jax.experimental import pallas as pl
from jax.experimental.pallas import tpu as pltpu
from jax.sharding import PartitionSpec as P

HD = 128
GSIZE = 16
ROPE_BASE = 1000000.0
NORM_EPSILON = 1e-06
MESH = pl.DeviceIdType.MESH
BF = jnp.bfloat16
F32 = jnp.float32
HBM = pl.BlockSpec(memory_space=pl.ANY)
VMEM = pl.BlockSpec(memory_space=pltpu.VMEM)
SMEM = pl.BlockSpec(memory_space=pltpu.SMEM)
DMA = pltpu.SemaphoreType.DMA
LIMIT = 56 * 2**20

N_F = 32
N_Z = 4
SEQ = 32
MAXLEN = 72
TOK = 768
HALF = TOK // 2
FB = 896
D = 3584
QC = 512
KC = 128
TB = 128

CHIPS = [(0, 1), (1, 0), (0, 3), (3, 0), (1, 1), (3, 3), (1, 3), (3, 1),
         (0, 2), (2, 0), (1, 2), (2, 1), (3, 2), (2, 3), (2, 2)]
OFFSETS = [(0, 0, 1)] + [(a, b, c) for c in range(2) for a, b in CHIPS]


def nt(a, b):
    return lax.dot_general(a, b, (((1,), (1,)), ((), ())), preferred_element_type=F32)


def tn(a, b):
    return lax.dot_general(a, b, (((0,), (0,)), ((), ())), preferred_element_type=F32)


def nn(a, b):
    return lax.dot_general(a, b, (((1,), (0,)), ((), ())), preferred_element_type=F32)


def iota(shape, dim):
    return lax.broadcasted_iota(jnp.int32, shape, dim)


def diagonal(row, n):
    return jnp.sum(jnp.where(iota((n, n), 0) == iota((n, n), 1), row, 0.0), axis=1, keepdims=True)


def stage_kernel(dest_s, dest_r, clus_r, roll, send, meta, sem):
    def start(s, c):
        t = dest_s[s] // SEQ
        pltpu.make_async_copy(roll.at[s], send.at[t], sem.at[s]).start()
        return c

    lax.fori_loop(0, SEQ, start, 0)
    clus = clus_r[...].astype(F32)
    group = iota((SEQ, SEQ), 0) // GSIZE == iota((SEQ, SEQ), 1) // GSIZE
    same = jnp.where((diagonal(clus, SEQ) == clus) & group, 1.0 / GSIZE, 0.0)
    share_c = jnp.sum(same, axis=1, keepdims=True)
    share_r = jnp.sum(same, axis=0, keepdims=True)
    mean_r = jnp.sum(jnp.where(group, share_c, 0.0), axis=0, keepdims=True) * (1.0 / GSIZE)
    adv_r = (share_r - mean_r).astype(BF).astype(F32)
    rows = iota((SEQ * 8, SEQ), 0)
    dest_v = dest_r[...]
    hit = dest_v // SEQ == rows // 8
    what = jnp.where(rows % 8 < 4, (dest_v % SEQ).astype(F32), adv_r)
    meta[...] = jnp.broadcast_to(jnp.sum(jnp.where(hit, what, 0.0), axis=1, keepdims=True), (SEQ * 8, 128))

    def wait(s, c):
        t = dest_s[s] // SEQ
        pltpu.make_async_copy(roll.at[s], send.at[t], sem.at[s]).wait()
        return c

    lax.fori_loop(0, SEQ, wait, 0)


def ring_copy(src, dst, blk, half, to, ss, rs, i):
    sl = pl.ds(half * HALF, HALF)
    return pltpu.make_async_remote_copy(
        src_ref=src.at[sl], dst_ref=dst.at[blk, sl], send_sem=ss.at[i], recv_sem=rs.at[i],
        device_id={"tp": to}, device_id_type=MESH)


def ring_start(own, dst, z, ss, rs):
    right, left = lax.rem(z + 1, N_Z), lax.rem(z + 3, N_Z)
    c = [ring_copy(own, dst, z, 0, right, ss, rs, 0), ring_copy(own, dst, z, 1, left, ss, rs, 1),
         ring_copy(own, dst, z, 1, right, ss, rs, 2), ring_copy(own, dst, z, 0, left, ss, rs, 3)]
    for x in c:
        x.start()
    return c


def ring_end(own, dst, z, ss, rs, c):
    right, left, far = lax.rem(z + 1, N_Z), lax.rem(z + 3, N_Z), lax.rem(z + 2, N_Z)
    ring_copy(own, dst, left, 0, right, ss, rs, 0).wait_recv()
    f0 = ring_copy(dst.at[left], dst, left, 0, right, ss, rs, 4)
    f0.start()
    ring_copy(own, dst, right, 1, left, ss, rs, 1).wait_recv()
    f1 = ring_copy(dst.at[right], dst, right, 1, left, ss, rs, 5)
    f1.start()
    ring_copy(own, dst, left, 1, right, ss, rs, 2).wait_recv()
    ring_copy(own, dst, right, 0, left, ss, rs, 3).wait_recv()
    ring_copy(own, dst, far, 0, right, ss, rs, 4).wait_recv()
    ring_copy(own, dst, far, 1, left, ss, rs, 5).wait_recv()
    for x in c + [f0, f1]:
        x.wait_send()


def hand_kernel(send, meta, cot, out, meta_out, cot_full, lsem, ss, rs, ms, mr, zs, zr):
    me = lax.axis_index("fsdp")
    z = lax.axis_index("tp")
    y, x, c = me // 8, (me // 2) % 4, me % 2

    def peer(o, s):
        return lax.rem(y + s * o[0] + 4, 4) * 8 + lax.rem(x + s * o[1] + 4, 4) * 2 + lax.rem(c + s * o[2] + 2, 2)

    barrier = pltpu.get_barrier_semaphore()
    for o in OFFSETS:
        pl.semaphore_signal(barrier, inc=1, device_id={"fsdp": peer(o, 1)}, device_id_type=MESH)
    for d in (1, 3):
        pl.semaphore_signal(barrier, inc=1, device_id={"tp": lax.rem(z + d, N_Z)}, device_id_type=MESH)
    pl.semaphore_wait(barrier, len(OFFSETS) + 2)
    mine = [pltpu.make_async_copy(send.at[me], out.at[me], lsem.at[0]),
            pltpu.make_async_copy(meta.at[pl.ds(8 * me, 8)], meta_out.at[pl.ds(8 * me, 8)], lsem.at[1])]
    ring = ring_start(cot, cot_full, z, zs, zr)

    def slab(i, frm, to, who):
        return pltpu.make_async_remote_copy(
            src_ref=send.at[frm], dst_ref=out.at[to], send_sem=ss.at[i], recv_sem=rs.at[i],
            device_id={"fsdp": who}, device_id_type=MESH)

    def note(i, frm, to, who):
        return pltpu.make_async_remote_copy(
            src_ref=meta.at[pl.ds(8 * frm, 8)], dst_ref=meta_out.at[pl.ds(8 * to, 8)],
            send_sem=ms.at[i], recv_sem=mr.at[i], device_id={"fsdp": who}, device_id_type=MESH)

    for i, o in enumerate(OFFSETS):
        t = peer(o, 1)
        slab(i, t, me, t).start()
        note(i, t, me, t).start()
    for m in mine:
        m.start()
    ring_end(cot, cot_full, z, zs, zr, ring)
    for i, o in enumerate(OFFSETS):
        t, f = peer(o, 1), peer(o, -1)
        slab(i, t, f, t).wait_recv()
        note(i, t, f, t).wait_recv()
        slab(i, t, me, t).wait_send()
        note(i, t, me, t).wait_send()
    for m in mine:
        m.wait()


def pack_kernel(rows, meta, len_r, gain, table, packed, scaled, squares, rope, pos_b, adv_b, keys):
    lane = iota((SEQ, 128), 1)
    sub = iota((SEQ, 128), 0)
    lens = diagonal(len_r[...].astype(F32), SEQ)
    at_own = pl.ds(pl.multiple_of(lax.axis_index("tp") * FB, 128), FB)
    gain_own = gain[:, at_own].astype(F32)
    ends = jnp.sum(jnp.where(sub <= lane, lens, 0.0), axis=0, keepdims=True)
    starts = jnp.sum(jnp.where(sub < lane, lens, 0.0), axis=0, keepdims=True)
    place = meta[pl.ds(0, SEQ, 8), :]
    share = meta[pl.ds(4, SEQ, 8), :]
    one = iota((1, 128), 1)
    place_r = jnp.where(one < SEQ, jnp.sum(jnp.where(sub == lane, place, 0.0), axis=0, keepdims=True), -1.0)
    share_r = jnp.sum(jnp.where(sub == lane, share, 0.0), axis=0, keepdims=True)
    column = iota((SEQ, SEQ * MAXLEN), 1)
    source = iota((SEQ, SEQ * MAXLEN), 0)
    here = (column >= source * MAXLEN) & (column < (source + 1) * MAXLEN)
    key = place[:, :1] * 128.0 + (column - source * MAXLEN).astype(F32)
    keys[...] = jnp.sum(jnp.where(here, key, 0.0), axis=0, keepdims=True)

    def block(b, c):
        at = pl.ds(pl.multiple_of(b * TB, TB), TB)
        i = (iota((TB, 128), 0) + b * TB).astype(F32)
        lane_f = iota((TB, 128), 1).astype(F32)
        hit = (i >= starts) & (i < ends)
        seg = jnp.sum(jnp.where(hit, lane_f, 0.0), axis=1, keepdims=True)
        start = jnp.sum(jnp.where(hit, starts, 0.0), axis=1, keepdims=True)
        pos = i - start
        pos_b[at, :] = pos
        adv_b[at, :] = jnp.broadcast_to(
            jnp.sum(jnp.where(place_r == seg, share_r, 0.0), axis=1, keepdims=True), (TB, 128))
        rope[at, :] = lax.dot_general(
            jnp.where(pos == lane_f, 1.0, 0.0), table[...], (((1,), (0,)), ((), ())),
            precision=lax.Precision.HIGHEST, preferred_element_type=F32)
        pick = jnp.where(seg * 128.0 + pos[:, :1] == keys[...], 1.0, 0.0).astype(BF)
        took = nn(pick, rows[...])
        packed[at, :] = took.astype(BF)
        scaled[at, :] = (took * gain_own).astype(BF)
        square = jnp.sum(took * took, axis=1, keepdims=True)
        squares[:, at] = jnp.transpose(jnp.broadcast_to(square, (TB, 128)))[:8, :]
        return c

    lax.fori_loop(0, TOK // TB, block, 0)


def gather_kernel(own, sq, full, sq_full, lsem, zs, zr, qs, qr):
    z = lax.axis_index("tp")
    barrier = pltpu.get_barrier_semaphore()
    for d in (1, 2, 3):
        pl.semaphore_signal(barrier, inc=1, device_id={"tp": lax.rem(z + d, N_Z)}, device_id_type=MESH)
    pl.semaphore_wait(barrier, 3)
    mine = [pltpu.make_async_copy(sq, sq_full.at[z], lsem.at[0])]
    ring = ring_start(own, full, z, zs, zr)

    def note(d, blk):
        return pltpu.make_async_remote_copy(
            src_ref=sq, dst_ref=sq_full.at[blk], send_sem=qs.at[d], recv_sem=qr.at[d],
            device_id={"tp": lax.rem(z + d, N_Z)}, device_id_type=MESH)

    for d in (1, 2, 3):
        note(d, z).start()
    for m in mine:
        m.start()
    ring_end(own, full, z, zs, zr, ring)
    for d in (1, 2, 3):
        note(d, lax.rem(z + N_Z - d, N_Z)).wait_recv()
        note(d, z).wait_send()
    for m in mine:
        m.wait()


def unstack(v):
    return jnp.concatenate([v[h * TB:(h + 1) * TB] for h in range(4)], axis=1)


def stack(v):
    return jnp.concatenate([v[:, h * HD:(h + 1) * HD] for h in range(4)], axis=0)


def turn(v, cos, sin):
    return v * cos + jnp.concatenate([v[:, HD // 2:], v[:, :HD // 2]], axis=1) * sin


def turn_back(v, cos, sin):
    return v * cos - jnp.concatenate([v[:, HD // 2:], v[:, :HD // 2]], axis=1) * sin


def block_kernel(own_x, own_c, xf, cf, wf, sq, rope, pos_b, adv_b, grads, outs, inv_b, dots,
                 xv, cv, wv, sem, lin, ga, qrot, kbuf, vbuf, gab, dk, dv, mq):
    z = lax.axis_index("tp")

    def loads(d):
        blk = lax.rem(z + d, N_Z)
        first = isinstance(d, int) and d == 0
        return [pltpu.make_async_copy(own_x if first else xf.at[blk], xv.at[d], sem.at[d, 0]),
                pltpu.make_async_copy(own_c if first else cf.at[blk], cv.at[d], sem.at[d, 1]),
                pltpu.make_async_copy(wf.at[blk], wv.at[d], sem.at[d, 2])]

    for d in range(N_Z):
        for k in loads(d):
            k.start()
    total = sq[0] + sq[1] + sq[2] + sq[3]
    inv_t = lax.rsqrt(total * (1.0 / D) + NORM_EPSILON)
    for b in range(TOK // TB):
        inv_b[b * TB:(b + 1) * TB, :] = jnp.transpose(jnp.broadcast_to(inv_t[:1, b * TB:(b + 1) * TB], (128, TB)))
    kbuf[...] = jnp.zeros_like(kbuf)
    vbuf[...] = jnp.zeros_like(vbuf)
    dk[...] = jnp.zeros_like(dk)
    dv[...] = jnp.zeros_like(dv)
    lin[...] = jnp.zeros_like(lin)
    ga[...] = jnp.zeros_like(ga)

    def project(d, c):
        for k in loads(d):
            k.wait()
        for n in range(3):
            lin[:, n * 256:(n + 1) * 256] += nn(xv[d], wv[d, :, n * 256:(n + 1) * 256])
        for n in range(2):
            ga[:, n * 256:(n + 1) * 256] += nn(cv[d], wv[d, :, 768 + n * 256:768 + (n + 1) * 256])
        return c

    lax.fori_loop(0, N_Z, project, 0)

    def ready(b, c):
        at = pl.ds(pl.multiple_of(b * TB, TB), TB)
        up = pl.ds(pl.multiple_of(b * TB + TB, TB), TB)
        inv = inv_b[at, :]
        cos, sin = rope[at, :HD], rope[at, HD:]
        for h in range(4):
            qrot[at, h * HD:(h + 1) * HD] = turn(lin[at, h * HD:(h + 1) * HD] * inv, cos, sin).astype(BF)
            gab[at, h * HD:(h + 1) * HD] = (ga[at, h * HD:(h + 1) * HD] * adv_b[at, :]).astype(BF)
        kbuf[up, :] = turn(lin[at, QC:QC + KC] * inv, cos, sin).astype(BF)
        vbuf[up, :] = (lin[at, QC + KC:] * inv).astype(BF)
        return c

    lax.fori_loop(0, TOK // TB, ready, 0)
    scale = HD ** (-0.5)

    def attend(b, c):
        at = pl.ds(pl.multiple_of(b * TB, TB), TB)
        win = pl.ds(pl.multiple_of(b * TB, TB), 2 * TB)
        q = stack(qrot[at, :])
        g = stack(gab[at, :])
        k, v = kbuf[win, :], vbuf[win, :]
        back = iota((TB, 2 * TB), 0) + TB - iota((TB, 2 * TB), 1)
        ok = (back >= 0) & (back.astype(F32) <= pos_b[at, :1])
        ok = jnp.concatenate([ok] * 4, axis=0)
        s = jnp.where(ok, nt(q, k) * scale, -1e30)
        e = jnp.where(ok, jnp.exp(s - jnp.max(s, axis=1, keepdims=True)), 0.0)
        p = e / jnp.sum(e, axis=1, keepdims=True)
        pb = p.astype(BF)
        o = unstack(nn(pb, v))
        dp = nt(g, v)
        ds = (p * (dp - jnp.sum(p * dp, axis=1, keepdims=True)) * scale).astype(BF)
        dq = nn(ds, k)
        dk[win, :] += tn(ds, q)
        dv[win, :] += tn(pb, g)
        prod = dq * q.astype(F32)
        mq[at, :] = prod[:TB] + prod[TB:2 * TB] + prod[2 * TB:3 * TB] + prod[3 * TB:]
        dq = unstack(dq)
        inv = inv_b[at, :]
        cos, sin = rope[at, :HD], rope[at, HD:]
        for h in range(4):
            col = slice(h * HD, (h + 1) * HD)
            grads[at, col] = (turn_back(dq[:, col], cos, sin) * inv).astype(BF)
            outs[at, col] = (o[:, col] * adv_b[at, :]).astype(BF)
        return c

    lax.fori_loop(0, TOK // TB, attend, 0)

    def finish(b, c):
        at = pl.ds(pl.multiple_of(b * TB, TB), TB)
        up = pl.ds(pl.multiple_of(b * TB + TB, TB), TB)
        inv = inv_b[at, :]
        cos, sin = rope[at, :HD], rope[at, HD:]
        gk, gv = dk[up, :], dv[up, :]
        grads[at, QC:QC + KC] = (turn_back(gk, cos, sin) * inv).astype(BF)
        grads[at, QC + KC:] = (gv * inv).astype(BF)
        m = mq[at, :] + gk * kbuf[up, :].astype(F32) + gv * vbuf[up, :].astype(F32)
        m = jnp.sum(m, axis=1, keepdims=True) * inv
        dots[:, at] = jnp.transpose(m)[:8, :]
        return c

    lax.fori_loop(0, TOK // TB, finish, 0)


def grad_kernel(grads, outs, own_x, own_c, xf, cf, wf, dots, packed, gain, inv_b, adv_b,
                result, res_q, res_k, res_v, res_o,
                wv, xv, cv, dots_all, sbuf, rbuf, dw, pair, r1, s1, r2, s2, fin,
                wsem, zs, zr, ds_, dr, ps, pr, s1s, s1r, s2s, s2r, fs, fr):
    z = lax.axis_index("tp")
    me = lax.axis_index("fsdp")
    y, x, c = me // 8, (me // 2) % 4, me % 2
    right, left, far = lax.rem(z + 1, N_Z), lax.rem(z + 3, N_Z), lax.rem(z + 2, N_Z)
    other = 1 - c
    sib = {"fsdp": y * 8 + x * 2 + other}
    width = QC + 2 * KC

    def on_x(d):
        return {"fsdp": y * 8 + lax.rem(x + d, 4) * 2 + c}

    def on_y(d):
        return {"fsdp": lax.rem(y + d, 4) * 8 + x * 2 + c}

    order = [far, right, left, z]
    wl = [pltpu.make_async_copy(wf.at[t, :, pl.ds(0, width)], wv.at[i], wsem.at[i, 0]) for i, t in enumerate(order)]
    for k in wl:
        k.start()
    rows = [pltpu.make_async_copy(own_x, xv.at[z], wsem.at[0, 1]), pltpu.make_async_copy(own_c, cv.at[z], wsem.at[0, 2])]
    for d in (1, 2, 3):
        t = lax.rem(z + d, N_Z)
        rows += [pltpu.make_async_copy(xf.at[t], xv.at[t], wsem.at[d, 1]),
                 pltpu.make_async_copy(cf.at[t], cv.at[t], wsem.at[d, 2])]
    for k in rows:
        k.start()
    barrier = pltpu.get_barrier_semaphore()
    for d in (1, 2, 3):
        for who in ({"tp": lax.rem(z + d, N_Z)}, on_x(d), on_y(d)):
            pl.semaphore_signal(barrier, inc=1, device_id=who, device_id_type=MESH)
    pl.semaphore_signal(barrier, inc=1, device_id=sib, device_id_type=MESH)
    pl.semaphore_wait(barrier, 10)

    def remote(src, dst, ss, rs, who):
        return pltpu.make_async_remote_copy(
            src_ref=src, dst_ref=dst, send_sem=ss, recv_sem=rs, device_id=who, device_id_type=MESH)

    def note(d):
        return remote(dots, dots_all.at[d - 1], ds_.at[d], dr.at[d], {"tp": lax.rem(z + d, N_Z)})

    for d in (1, 2, 3):
        note(d).start()

    def ship(i):
        return remote(sbuf.at[i], rbuf.at[i], zs.at[i], zr.at[i], {"tp": right if i % 2 == 0 else left})

    def share(i, h):
        return nt(grads[h * HALF:(h + 1) * HALF, :], wv[i])

    for i, (w, h) in enumerate([(0, 0), (0, 1), (1, 1), (2, 0)]):
        if i != 1:
            wl[w].wait()
        sbuf[i] = share(w, h).astype(BF)
        ship(i).start()
    for k in rows:
        k.wait()

    def swap(i):
        b = lax.rem(y + 1 + i, 4)
        return remote(dw.at[other, b], pair.at[b], ps.at[i], pr.at[i], sib)

    def terms(i, carry):
        b = lax.rem(y + 1 + i, 4)
        lo = tn(xv[b], grads[:, :QC + KC]).astype(BF)
        mid = tn(xv[b], grads[:, QC + KC:]).astype(BF)
        hi = tn(cv[b], outs[...]).astype(BF)
        for j in range(8):
            at = slice(112 * j, 112 * (j + 1))
            dw[0, b, j // 2, j % 2] = lo[at]
            dw[1, b, j // 2, j % 2, :, :KC] = mid[at]
            dw[1, b, j // 2, j % 2, :, KC:] = hi[at]
        swap(i).start()
        return carry

    lax.fori_loop(0, 4, terms, 0)
    for i, w in ((4, 1), (5, 2)):
        a = share(w, i % 2)
        ship(i - 4).wait_recv()
        sbuf[i] = (a + rbuf[i - 4].astype(F32)).astype(BF)
        ship(i).start()

    def hop_y(d):
        return remote(dw.at[c, lax.rem(y + d, 4), :, 1], r1.at[1, d - 1], s1s.at[1, d - 1], s1r.at[1, d - 1], on_y(d))

    def hop_x(d):
        return remote(dw.at[c, :, lax.rem(x + d, 4), 0], r1.at[0, d - 1], s1s.at[0, d - 1], s1r.at[0, d - 1], on_x(d))

    def chip_sum(i, carry):
        b = lax.rem(y + 1 + i, 4)
        swap(i).wait_recv()
        for j in range(4):
            dw[c, b, j] = (dw[c, b, j].astype(F32) + pair[b, j].astype(F32)).astype(BF)

        @pl.when(i < 3)
        def _():
            hop_y(i + 1).start()

        return carry

    lax.fori_loop(0, 4, chip_sum, 0)
    for d in (1, 2, 3):
        hop_x(d).start()
    wl[3].wait()
    own = share(3, 0)
    sbuf[6] = own.astype(BF)
    own = share(3, 1)
    sbuf[7] = own.astype(BF)
    for d in (1, 2, 3):
        note(d).wait()
    m = (dots[...] + dots_all[0] + dots_all[1] + dots_all[2]) * (1.0 / D)

    for d in (1, 2, 3):
        hop_y(d).wait_recv()
        hop_x(d).wait_recv()
    for j in range(4):
        s1[1, j] = (dw[c, y, j, 1].astype(F32) + r1[1, 0, j].astype(F32) + r1[1, 1, j].astype(F32)
                    + r1[1, 2, j].astype(F32)).astype(BF)
        s1[0, j] = (dw[c, j, x, 0].astype(F32) + r1[0, 0, j].astype(F32) + r1[0, 1, j].astype(F32)
                    + r1[0, 2, j].astype(F32)).astype(BF)

    def last_x(d):
        return remote(s1.at[1, lax.rem(x + d, 4)], r2.at[1, d - 1], s2s.at[1, d - 1], s2r.at[1, d - 1], on_x(d))

    def last_y(d):
        return remote(s1.at[0, lax.rem(y + d, 4)], r2.at[0, d - 1], s2s.at[0, d - 1], s2r.at[0, d - 1], on_y(d))

    for d in (1, 2, 3):
        last_x(d).start()
        last_y(d).start()
    for d in (1, 2, 3):
        last_x(d).wait_recv()
        last_y(d).wait_recv()
    for p, own in ((0, s1[0, y]), (1, s1[1, x])):
        s2[p] = (own.astype(F32) + r2[p, 0].astype(F32) + r2[p, 1].astype(F32) + r2[p, 2].astype(F32)).astype(BF)
    trade = remote(s2.at[other], fin.at[c], fs.at[0], fr.at[0], sib)
    trade.start()
    for i in (2, 3, 4, 5):
        ship(i).wait_recv()
    gain_own = gain[:, pl.ds(pl.multiple_of(z * FB, 128), FB)].astype(F32)
    for b in range(TOK // TB):
        h, r = divmod(b * TB, HALF)
        at = slice(b * TB, (b + 1) * TB)
        hs = slice(r, r + TB)
        one, two = (4, 3) if h == 0 else (2, 5)
        s = sbuf[6 + h, hs, :].astype(F32) + rbuf[one, hs, :].astype(F32) + rbuf[two, hs, :].astype(F32)
        mc = jnp.transpose(jnp.broadcast_to(m[:1, at], (128, TB)))[:, :1]
        inv = inv_b[at, :1]
        result[at, :] = (adv_b[at, :1] * cv[z, at, :].astype(F32) + s * gain_own
                         - packed[at, :].astype(F32) * (inv * mc)).astype(BF)
    trade.wait()
    mine = s2[c]
    got = fin[other]
    low = jnp.where(c == 0, mine, got)
    high = jnp.where(c == 0, got, mine)
    res_q[...] = low[:, :QC]
    res_k[...] = low[:, QC:]
    res_v[...] = high[:, :KC]
    res_o[...] = high[:, KC:]
    for i in range(6):
        ship(i).wait_send()
    for i in range(4):
        swap(i).wait_send()
    for d in (1, 2, 3):
        hop_x(d).wait_send()
        hop_y(d).wait_send()
        last_x(d).wait_send()
        last_y(d).wait_send()


def sds(shape, dtype=BF):
    return jax.ShapeDtypeStruct(shape, dtype)


def params(**kw):
    return pltpu.CompilerParams(vmem_limit_bytes=LIMIT, has_side_effects=True, **kw)


def rope_table():
    i = np.arange(HD // 2, dtype=np.float32)
    frequency = np.float32(ROPE_BASE) ** (-(np.float32(2.0) * i) / np.float32(HD))
    angle = np.arange(128, dtype=np.float32)[:, None] * frequency[None, :]
    c, s = np.cos(angle), np.sin(angle)
    return np.concatenate([c, c, -s, s], axis=1).astype(np.float32)


def per_device(roll_rows, dest, lengths, clusters, log_prob_grad, gain, w_q, w_k, w_v, w_o_t):
    weights = lax.all_gather(jnp.concatenate([w_q, w_k, w_v, w_o_t], axis=1), "fsdp", axis=0, tiled=True)
    weights = weights.reshape(N_Z, FB, QC * 2 + KC * 2)
    gain = gain.reshape(1, D)
    send, meta = pl.pallas_call(
        stage_kernel, out_shape=(sds((SEQ, MAXLEN, FB)), sds((SEQ * 8, 128), F32)),
        in_specs=[SMEM, VMEM, VMEM, HBM], out_specs=(VMEM, VMEM),
        scratch_shapes=[DMA((SEQ,))], compiler_params=params(),
    )(dest, dest.reshape(1, SEQ), clusters.reshape(1, SEQ), roll_rows)
    n_o = len(OFFSETS)
    arrived, meta_in, cot = pl.pallas_call(
        hand_kernel, out_shape=(sds((SEQ, MAXLEN, FB)), sds((SEQ * 8, 128), F32), sds((N_Z, TOK, FB))),
        in_specs=[HBM, HBM, HBM], out_specs=(HBM, HBM, HBM),
        scratch_shapes=[DMA((2,)), DMA((n_o,)), DMA((n_o,)), DMA((n_o,)), DMA((n_o,)), DMA((6,)), DMA((6,))],
        compiler_params=params(collective_id=0),
    )(send, meta, log_prob_grad)
    packed, scaled, squares, rope, pos_b, adv_b = pl.pallas_call(
        pack_kernel,
        out_shape=(sds((TOK, FB)), sds((TOK, FB)), sds((8, TOK), F32), sds((TOK, 2 * HD), F32),
                   sds((TOK, 128), F32), sds((TOK, 128), F32)),
        in_specs=[VMEM] * 5, out_specs=(VMEM,) * 6,
        scratch_shapes=[pltpu.VMEM((1, SEQ * MAXLEN), F32)], compiler_params=params(),
    )(arrived.reshape(SEQ * MAXLEN, FB), meta_in, lengths, gain, jnp.asarray(rope_table()))
    rows, sq = pl.pallas_call(
        gather_kernel, out_shape=(sds((N_Z, TOK, FB)), sds((N_Z, 8, TOK), F32)),
        in_specs=[HBM, HBM], out_specs=(HBM, HBM),
        scratch_shapes=[DMA((1,)), DMA((6,)), DMA((6,)), DMA((4,)), DMA((4,))],
        compiler_params=params(collective_id=1),
    )(scaled, squares)
    width = QC + 2 * KC
    grads, outs, inv_b, dots = pl.pallas_call(
        block_kernel,
        out_shape=(sds((TOK, width)), sds((TOK, QC)), sds((TOK, 128), F32), sds((8, TOK), F32)),
        in_specs=[HBM] * 5 + [VMEM] * 4, out_specs=(VMEM,) * 4,
        scratch_shapes=[
            pltpu.VMEM((N_Z, TOK, FB), BF), pltpu.VMEM((N_Z, TOK, FB), BF),
            pltpu.VMEM((N_Z, FB, width + QC), BF), DMA((N_Z, 3)),
            pltpu.VMEM((TOK, width), F32), pltpu.VMEM((TOK, QC), F32),
            pltpu.VMEM((TOK, QC), BF), pltpu.VMEM((TOK + TB, HD), BF), pltpu.VMEM((TOK + TB, HD), BF),
            pltpu.VMEM((TOK, QC), BF), pltpu.VMEM((TOK + TB, HD), F32), pltpu.VMEM((TOK + TB, HD), F32),
            pltpu.VMEM((TOK, HD), F32)],
        compiler_params=params(),
    )(scaled, log_prob_grad, rows, cot, weights, sq, rope, pos_b, adv_b)
    half = (112, QC + KC)
    return pl.pallas_call(
        grad_kernel,
        out_shape=(sds((TOK, FB)), sds((112, QC)), sds((112, KC)), sds((112, KC)), sds((112, QC))),
        in_specs=[VMEM, VMEM] + [HBM] * 5 + [VMEM] * 5, out_specs=(VMEM,) * 5,
        scratch_shapes=[
            pltpu.VMEM((N_Z, FB, width), BF), pltpu.VMEM((N_Z, TOK, FB), BF), pltpu.VMEM((N_Z, TOK, FB), BF),
            pltpu.VMEM((3, 8, TOK), F32), pltpu.VMEM((8, HALF, FB), BF), pltpu.VMEM((6, HALF, FB), BF),
            pltpu.VMEM((2, 4, 4, 2) + half, BF), pltpu.VMEM((4, 4, 2) + half, BF),
            pltpu.VMEM((2, 3, 4) + half, BF), pltpu.VMEM((2, 4) + half, BF), pltpu.VMEM((2, 3) + half, BF),
            pltpu.VMEM((2,) + half, BF), pltpu.VMEM((2,) + half, BF),
            DMA((N_Z, 3)), DMA((6,)), DMA((6,)), DMA((4,)), DMA((4,)), DMA((4,)), DMA((4,)),
            DMA((2, 3)), DMA((2, 3)), DMA((2, 3)), DMA((2, 3)), DMA((1,)), DMA((1,))],
        compiler_params=params(collective_id=2),
    )(grads, outs, scaled, log_prob_grad, rows, cot, weights, dots, packed, gain, inv_b, adv_b)


def solution(mesh):
    in_specs = (
        P("fsdp", None, "tp"), P("fsdp"), P("fsdp", None), P("fsdp"), P("fsdp", "tp"), P(),
        P("fsdp", "tp"), P("fsdp", "tp"), P("fsdp", "tp"), P("fsdp", "tp"),
    )
    out_specs = (P("fsdp", "tp"),) * 5
    return jax.shard_map(per_device, mesh=mesh, in_specs=in_specs, out_specs=out_specs, check_vma=False)
```

```python
import jax
import jax.numpy as jnp
import numpy as np
from jax import lax
from jax.experimental import pallas as pl
from jax.experimental.pallas import tpu as pltpu
from jax.sharding import PartitionSpec as P

HD = 128
GSIZE = 16
ROPE_BASE = 1000000.0
NORM_EPSILON = 1e-06
MESH = pl.DeviceIdType.MESH
BF = jnp.bfloat16
F32 = jnp.float32
HBM = pl.BlockSpec(memory_space=pl.ANY)
VMEM = pl.BlockSpec(memory_space=pltpu.VMEM)
SMEM = pl.BlockSpec(memory_space=pltpu.SMEM)
DMA = pltpu.SemaphoreType.DMA
LIMIT = 60 * 2**20

N_F = 32
N_Z = 4
SEQ = 32
MAXLEN = 72
TOK = 768
HALF = TOK // 2
FB = 896
FA = 512
SLAB = 80
D = 3584
QC = 512
KC = 128
TB = 128

CHIPS = [(0, 1), (1, 0), (0, 3), (3, 0), (1, 1), (3, 3), (1, 3), (3, 1),
         (0, 2), (2, 0), (1, 2), (2, 1), (3, 2), (2, 3), (2, 2)]
OFFSETS = [(0, 0, 1)] + [(a, b, c) for c in range(2) for a, b in CHIPS]


def nt(a, b):
    return lax.dot_general(a, b, (((1,), (1,)), ((), ())), preferred_element_type=F32)


def tn(a, b):
    return lax.dot_general(a, b, (((0,), (0,)), ((), ())), preferred_element_type=F32)


def nn(a, b):
    return lax.dot_general(a, b, (((1,), (0,)), ((), ())), preferred_element_type=F32)


def iota(shape, dim):
    return lax.broadcasted_iota(jnp.int32, shape, dim)


def diagonal(row, n):
    return jnp.sum(jnp.where(iota((n, n), 0) == iota((n, n), 1), row, 0.0), axis=1, keepdims=True)


def stage_kernel(dest_s, dest_r, clus_r, roll, send_a, send_b, meta):
    def place(s, c):
        at = pl.ds(pl.multiple_of((dest_s[s] // SEQ) * SLAB, 16), SLAB)
        v = jnp.concatenate([roll[s], jnp.zeros((SLAB - MAXLEN, FB), BF)], axis=0)
        send_a[at, :] = v[:, :FA]
        send_b[at, :] = v[:, FA:]
        return c

    lax.fori_loop(0, SEQ, place, 0)
    clus = clus_r[...].astype(F32)
    group = iota((SEQ, SEQ), 0) // GSIZE == iota((SEQ, SEQ), 1) // GSIZE
    same = jnp.where((diagonal(clus, SEQ) == clus) & group, 1.0 / GSIZE, 0.0)
    share_c = jnp.sum(same, axis=1, keepdims=True)
    share_r = jnp.sum(same, axis=0, keepdims=True)
    mean_r = jnp.sum(jnp.where(group, share_c, 0.0), axis=0, keepdims=True) * (1.0 / GSIZE)
    adv_r = (share_r - mean_r).astype(BF).astype(F32)
    rows = iota((SEQ * 8, SEQ), 0)
    dest_v = dest_r[...]
    hit = dest_v // SEQ == rows // 8
    what = jnp.where(rows % 8 < 4, (dest_v % SEQ).astype(F32), adv_r)
    meta[...] = jnp.broadcast_to(jnp.sum(jnp.where(hit, what, 0.0), axis=1, keepdims=True), (SEQ * 8, 128))


def remote(src, dst, ss, rs, who):
    return pltpu.make_async_remote_copy(
        src_ref=src, dst_ref=dst, send_sem=ss, recv_sem=rs, device_id=who, device_id_type=MESH)


class Ring:
    def __init__(self, own, dst, cols, z, ss, rs):
        self.own, self.dst, self.cols, self.z, self.ss, self.rs = own, dst, cols, z, ss, rs
        self.right, self.left, self.far = (lax.rem(z + d, N_Z) for d in (1, 3, 2))

    def copy(self, i, blk, src=None):
        half = (0, 1, 1, 0, 0, 1)[i]
        at = pl.ds(half * HALF, HALF)
        to = self.right if i % 2 == 0 else self.left
        src = self.own if src is None else src
        return remote(src.at[at, self.cols], self.dst.at[blk, at, self.cols], self.ss.at[i], self.rs.at[i], {"tp": to})

    def start(self):
        for i in range(4):
            self.copy(i, self.z).start()

    def hand_on(self):
        for i, blk in ((0, self.left), (1, self.right)):
            self.copy(i, blk).wait_recv()
            self.copy(i + 4, blk, self.dst.at[blk]).start()

    def near(self):
        self.copy(2, self.left).wait_recv()
        self.copy(3, self.right).wait_recv()

    def end(self):
        self.copy(4, self.far).wait_recv()
        self.copy(5, self.far).wait_recv()

    def sent(self):
        for i in range(4):
            self.copy(i, self.z).wait_send()
        self.copy(4, self.left, self.dst.at[self.left]).wait_send()
        self.copy(5, self.right, self.dst.at[self.right]).wait_send()


def unstack(v):
    return jnp.concatenate([v[h * TB:(h + 1) * TB] for h in range(4)], axis=1)


def stack(v):
    return jnp.concatenate([v[:, h * HD:(h + 1) * HD] for h in range(4)], axis=0)


def turn(v, cos, sin):
    return v * cos + jnp.concatenate([v[:, HD // 2:], v[:, :HD // 2]], axis=1) * sin


def turn_back(v, cos, sin):
    return v * cos - jnp.concatenate([v[:, HD // 2:], v[:, :HD // 2]], axis=1) * sin


def front_kernel(send_a, send_b, meta, cot, len_r, gain, table, w_q, w_k, w_v, w_o,
                 x_out, c_out, w_out, packed, grads, outs, inv_b, adv_b, dots,
                 arr_a, arr_b, meta_in, pick, xv, cv, wsh, wv, sq, sq_all, sqc, rope, pos_b,
                 lin, ga, qrot, kbuf, vbuf, gab, dk, dv, mq,
                 lsem, osem, as_, ar, bs, br, ms, mr, zs, zr, us, ur, vs, vr, qs, qr,
                 w0s, w0r, w1s, w1r, w2s, w2r, w3s, w3r):
    me = lax.axis_index("fsdp")
    z = lax.axis_index("tp")
    y, x, c = me // 8, (me // 2) % 4, me % 2
    other = 1 - c
    sib = {"fsdp": y * 8 + x * 2 + other}

    def peer(o, s):
        return lax.rem(y + s * o[0] + 4, 4) * 8 + lax.rem(x + s * o[1] + 4, 4) * 2 + lax.rem(c + s * o[2] + 2, 2)

    def on_x(d):
        return {"fsdp": peer((0, d, 0), 1)}

    def on_y(d):
        return {"fsdp": peer((d, 0, 0), 1)}

    cot_own = pltpu.make_async_copy(cot, cv.at[z], lsem.at[0])
    cot_own.start()
    barrier = pltpu.get_barrier_semaphore()
    for o in OFFSETS:
        pl.semaphore_signal(barrier, inc=1, device_id={"fsdp": peer(o, 1)}, device_id_type=MESH)
    for d in (1, 2, 3):
        pl.semaphore_signal(barrier, inc=1, device_id={"tp": lax.rem(z + d, N_Z)}, device_id_type=MESH)
    pl.semaphore_wait(barrier, len(OFFSETS) + 3)

    ring_c = Ring(cot, cv, pl.ds(0, FB), z, zs, zr)
    ring_a = Ring(xv.at[z], xv, pl.ds(0, FA), z, us, ur)
    ring_b = Ring(xv.at[z], xv, pl.ds(FA, FB - FA), z, vs, vr)
    ring_c.start()

    def slab(k):
        return pl.ds(pl.multiple_of(k * SLAB, 16), SLAB)

    def eight(k):
        return pl.ds(pl.multiple_of(k * 8, 8), 8)

    def part_a(i, frm, to, who):
        return remote(send_a.at[slab(frm)], arr_a.at[slab(to)], as_.at[i], ar.at[i], {"fsdp": who})

    def part_b(i, frm, to, who):
        return remote(send_b.at[slab(frm)], arr_b.at[slab(to)], bs.at[i], br.at[i], {"fsdp": who})

    def note(i, frm, to, who):
        return remote(meta.at[eight(frm)], meta_in.at[eight(to)], ms.at[i], mr.at[i], {"fsdp": who})

    for kind in (note, part_a, part_b):
        for i, o in enumerate(OFFSETS):
            t = peer(o, 1)
            kind(i, t, me, t).start()
    mine = [pltpu.make_async_copy(send_a.at[slab(me)], arr_a.at[slab(me)], lsem.at[1]),
            pltpu.make_async_copy(send_b.at[slab(me)], arr_b.at[slab(me)], lsem.at[2]),
            pltpu.make_async_copy(meta.at[eight(me)], meta_in.at[eight(me)], lsem.at[3])]
    for k in mine:
        k.start()

    wsh[0, :, :QC] = w_q[...]
    wsh[0, :, QC:] = w_k[...]
    wsh[1, :, :KC] = w_v[...]
    wsh[1, :, KC:] = w_o[...]
    wv[0, y, x, c] = wsh[0]
    wv[1, y, x, c] = wsh[1]
    w_pair = remote(wsh.at[other], wv.at[other, y, x, c], w0s.at[0], w0r.at[0], sib)
    w_pair.start()

    def w_near(p, d):
        return remote(wv.at[c, y, x, p], wv.at[c, y, x, p], w1s.at[p, d - 1], w1r.at[p, d - 1], on_y(d) if p else on_x(d))

    def w_next(p, d):
        blk = wv.at[c, :, x, 1] if p else wv.at[c, y, :, 0]
        return remote(blk, blk, w2s.at[p, d - 1], w2r.at[p, d - 1], on_x(d) if p else on_y(d))

    def w_last(d):
        if d < 3:
            blk = wv.at[c, lax.rem(y + d + 1, 4)]
        elif d < 6:
            blk = wv.at[c, y, lax.rem(x + d - 2, 4)]
        else:
            blk = wv.at[c, y, x, c]
        return remote(blk, blk, w3s.at[d], w3r.at[d], sib)

    hops = [(p, d) for d in (1, 2, 3) for p in (0, 1)]
    w_pair.wait_recv()
    for p, d in hops:
        w_near(p, d).start()

    lens = diagonal(len_r[...].astype(F32), SEQ)
    gain_own = gain[:, pl.ds(pl.multiple_of(z * FB, 128), FB)].astype(F32)
    lane = iota((SEQ, 128), 1)
    sub = iota((SEQ, 128), 0)
    ends = jnp.sum(jnp.where(sub <= lane, lens, 0.0), axis=0, keepdims=True)
    starts = jnp.sum(jnp.where(sub < lane, lens, 0.0), axis=0, keepdims=True)
    for i, o in enumerate(OFFSETS):
        note(i, peer(o, 1), peer(o, -1), peer(o, 1)).wait_recv()
    mine[2].wait()
    place = meta_in[pl.ds(0, SEQ, 8), :]
    share = meta_in[pl.ds(4, SEQ, 8), :]
    place_r = jnp.where(iota((1, 128), 1) < SEQ, jnp.sum(jnp.where(sub == lane, place, 0.0), axis=0, keepdims=True), -1.0)
    share_r = jnp.sum(jnp.where(sub == lane, share, 0.0), axis=0, keepdims=True)
    column = iota((SEQ, SEQ * SLAB), 1) - iota((SEQ, SEQ * SLAB), 0) * SLAB
    here = (column >= 0) & (column < SLAB)
    key = jnp.sum(jnp.where(here, place[:, :1] * 128.0 + column.astype(F32), 0.0), axis=0, keepdims=True)

    def layout(b):
        at = pl.ds(b * TB, TB)
        i = (iota((TB, 128), 0) + b * TB).astype(F32)
        lane_f = iota((TB, 128), 1).astype(F32)
        hit = (i >= starts) & (i < ends)
        seg = jnp.sum(jnp.where(hit, lane_f, 0.0), axis=1, keepdims=True)
        pos = i - jnp.sum(jnp.where(hit, starts, 0.0), axis=1, keepdims=True)
        pos_b[at, :] = pos
        adv_b[at, :] = jnp.broadcast_to(
            jnp.sum(jnp.where(place_r == seg, share_r, 0.0), axis=1, keepdims=True), (TB, 128))
        rope[at, :] = lax.dot_general(
            jnp.where(pos == lane_f, 1.0, 0.0), table[...], (((1,), (0,)), ((), ())),
            precision=lax.Precision.HIGHEST, preferred_element_type=F32)
        pick[at, :] = jnp.where(seg * 128.0 + pos[:, :1] == key, 1.0, 0.0).astype(BF)

    for b in range(TOK // TB):
        layout(b)
    ring_c.hand_on()

    def pack(arr, lo, hi):
        def rows(b, carry):
            at = pl.ds(pl.multiple_of(b * 256, 256), 256)
            took = nn(pick[at, :], arr[...])
            packed[at, lo:hi] = took.astype(BF)
            xv[z, at, lo:hi] = (took * gain_own[:, lo:hi]).astype(BF)
            square = took * took
            lanes = sum(square[:, k:k + 128] for k in range(0, hi - lo, 128))
            sqc[at, :] = lanes if lo == 0 else sqc[at, :] + lanes
            return carry

        lax.fori_loop(0, TOK // 256, rows, 0)

    for i, o in enumerate(OFFSETS):
        part_a(i, peer(o, 1), peer(o, -1), peer(o, 1)).wait_recv()
    mine[0].wait()
    pack(arr_a, 0, FA)
    ring_a.start()
    ring_c.near()
    ring_c.end()
    cot_own.wait()
    keep = [pltpu.make_async_copy(cv, c_out, osem.at[0])]
    keep[0].start()
    ring_a.hand_on()
    for i, o in enumerate(OFFSETS):
        part_b(i, peer(o, 1), peer(o, -1), peer(o, 1)).wait_recv()
    mine[1].wait()
    for p, d in hops:
        w_near(p, d).wait_recv()
    for p, d in hops:
        w_next(p, d).start()
    pack(arr_b, FA, FB)
    ring_b.start()
    for b in range(TOK // TB):
        square = jnp.sum(sqc[b * TB:(b + 1) * TB, :], axis=1, keepdims=True)
        sq[:, b * TB:(b + 1) * TB] = jnp.transpose(jnp.broadcast_to(square, (TB, 128)))[:8, :]

    def tell(d):
        return remote(sq, sq_all.at[d - 1], qs.at[d], qr.at[d], {"tp": lax.rem(z + d, N_Z)})

    for d in (1, 2, 3):
        tell(d).start()
    kbuf[:TB, :] = jnp.zeros((TB, HD), BF)
    vbuf[:TB, :] = jnp.zeros((TB, HD), BF)
    dk[...] = jnp.zeros_like(dk)
    dv[...] = jnp.zeros_like(dv)
    ring_b.hand_on()
    ring_a.near()
    ring_a.end()
    for d in (1, 2, 3):
        tell(d).wait_recv()
    inv_t = lax.rsqrt((sq[...] + sq_all[0] + sq_all[1] + sq_all[2]) * (1.0 / D) + NORM_EPSILON)
    for b in range(TOK // TB):
        inv_b[b * TB:(b + 1) * TB, :] = jnp.transpose(jnp.broadcast_to(inv_t[:1, b * TB:(b + 1) * TB], (128, TB)))
    for p, d in hops:
        w_next(p, d).wait_recv()
    for d in range(7):
        w_last(d).start()
    for d in range(7):
        w_last(d).wait_recv()
    keep.append(pltpu.make_async_copy(wv, w_out, osem.at[1]))
    keep[1].start()

    def whole(h, blk):
        return wv[h, blk].reshape(FB, QC + KC)

    def project_c(d, carry):
        t = nn(cv[d], whole(1, d)[:, KC:])

        @pl.when(d == 0)
        def _():
            ga[...] = t

        @pl.when(d > 0)
        def _():
            ga[...] += t

        return carry

    lax.fori_loop(0, N_Z, project_c, 0)
    lin[...] = jnp.zeros_like(lin)

    def project_x(d, carry):
        blk = lax.rem(z + d, N_Z)
        lin[:, :QC + KC] += nn(xv[blk], whole(0, blk))
        lin[:, QC + KC:] += nn(xv[blk], whole(1, blk)[:, :KC])
        return carry

    project_x(0, 0)
    ring_b.near()
    lax.fori_loop(0, 2, lambda k, carry: project_x(1 + 2 * k, carry), 0)
    ring_b.end()
    keep.append(pltpu.make_async_copy(xv, x_out, osem.at[2]))
    keep[2].start()
    project_x(2, 0)

    def ready(b, carry):
        at = pl.ds(pl.multiple_of(b * TB, TB), TB)
        up = pl.ds(pl.multiple_of(b * TB + TB, TB), TB)
        inv = inv_b[at, :]
        cos, sin = rope[at, :HD], rope[at, HD:]
        for h in range(4):
            qrot[at, h * HD:(h + 1) * HD] = turn(lin[at, h * HD:(h + 1) * HD] * inv, cos, sin).astype(BF)
            gab[at, h * HD:(h + 1) * HD] = (ga[at, h * HD:(h + 1) * HD] * adv_b[at, :]).astype(BF)
        kbuf[up, :] = turn(lin[at, QC:QC + KC] * inv, cos, sin).astype(BF)
        vbuf[up, :] = (lin[at, QC + KC:] * inv).astype(BF)
        return carry

    lax.fori_loop(0, TOK // TB, ready, 0)
    scale = HD ** (-0.5)

    def attend(b, carry):
        at = pl.ds(pl.multiple_of(b * TB, TB), TB)
        win = pl.ds(pl.multiple_of(b * TB, TB), 2 * TB)
        q = stack(qrot[at, :])
        g = stack(gab[at, :])
        k, v = kbuf[win, :], vbuf[win, :]
        back = iota((TB, 2 * TB), 0) + TB - iota((TB, 2 * TB), 1)
        ok = (back >= 0) & (back.astype(F32) <= pos_b[at, :1])
        ok = jnp.concatenate([ok] * 4, axis=0)
        s = jnp.where(ok, nt(q, k) * scale, -1e30)
        e = jnp.where(ok, jnp.exp(s - jnp.max(s, axis=1, keepdims=True)), 0.0)
        p = e / jnp.sum(e, axis=1, keepdims=True)
        pb = p.astype(BF)
        o = unstack(nn(pb, v))
        dp = nt(g, v)
        ds = (p * (dp - jnp.sum(p * dp, axis=1, keepdims=True)) * scale).astype(BF)
        dq = nn(ds, k)
        dk[win, :] += tn(ds, q)
        dv[win, :] += tn(pb, g)
        prod = dq * q.astype(F32)
        mq[at, :] = prod[:TB] + prod[TB:2 * TB] + prod[2 * TB:3 * TB] + prod[3 * TB:]
        dq = unstack(dq)
        inv = inv_b[at, :]
        cos, sin = rope[at, :HD], rope[at, HD:]
        for h in range(4):
            col = slice(h * HD, (h + 1) * HD)
            grads[at, col] = (turn_back(dq[:, col], cos, sin) * inv).astype(BF)
            outs[at, col] = (o[:, col] * adv_b[at, :]).astype(BF)
        return carry

    lax.fori_loop(0, TOK // TB, attend, 0)

    def finish(b, carry):
        at = pl.ds(pl.multiple_of(b * TB, TB), TB)
        up = pl.ds(pl.multiple_of(b * TB + TB, TB), TB)
        inv = inv_b[at, :]
        cos, sin = rope[at, :HD], rope[at, HD:]
        gk, gv = dk[up, :], dv[up, :]
        grads[at, QC:QC + KC] = (turn_back(gk, cos, sin) * inv).astype(BF)
        grads[at, QC + KC:] = (gv * inv).astype(BF)
        m = mq[at, :] + gk * kbuf[up, :].astype(F32) + gv * vbuf[up, :].astype(F32)
        m = jnp.sum(m, axis=1, keepdims=True) * inv
        dots[:, at] = jnp.transpose(jnp.broadcast_to(m, (TB, 128)))[:8, :]
        return carry

    lax.fori_loop(0, TOK // TB, finish, 0)
    for ring in (ring_c, ring_a, ring_b):
        ring.sent()
    for kind in (note, part_a, part_b):
        for i, o in enumerate(OFFSETS):
            t = peer(o, 1)
            kind(i, t, me, t).wait_send()
    w_pair.wait_send()
    for p, d in hops:
        w_near(p, d).wait_send()
        w_next(p, d).wait_send()
    for d in range(7):
        w_last(d).wait_send()
    for d in (1, 2, 3):
        tell(d).wait_send()
    for k in keep:
        k.wait()


def grad_kernel(grads, outs, xf, cf, wf, dots, packed, gain, inv_b, adv_b, result, low_out, high_out,
                wv, wu, xv, cv, dots_all, sbuf, rbuf, dw, pair, r1, s1, r2, s2, fin,
                wsem, zs, zr, ds_, dr, ps, pr, s1s, s1r, s2s, s2r, fs, fr):
    z = lax.axis_index("tp")
    me = lax.axis_index("fsdp")
    y, x, c = me // 8, (me // 2) % 4, me % 2
    right, left, far = lax.rem(z + 1, N_Z), lax.rem(z + 3, N_Z), lax.rem(z + 2, N_Z)
    other = 1 - c
    sib = {"fsdp": y * 8 + x * 2 + other}

    def on_x(d):
        return {"fsdp": y * 8 + lax.rem(x + d, 4) * 2 + c}

    def on_y(d):
        return {"fsdp": lax.rem(y + d, 4) * 8 + x * 2 + c}

    order = [far, right, left, z]
    wl = [pltpu.make_async_copy(wf.at[0, t], wv.at[i], wsem.at[i, 0]) for i, t in enumerate(order)]
    ul = [pltpu.make_async_copy(wf.at[1, t, :, pl.ds(0, KC)], wu.at[i], wsem.at[i, 3]) for i, t in enumerate(order)]
    for k in wl + ul:
        k.start()
    rows = []
    for t in range(N_Z):
        rows += [pltpu.make_async_copy(xf.at[t], xv.at[t], wsem.at[t, 1]),
                 pltpu.make_async_copy(cf.at[t], cv.at[t], wsem.at[t, 2])]
    for k in rows:
        k.start()
    barrier = pltpu.get_barrier_semaphore()
    for d in (1, 2, 3):
        for who in ({"tp": lax.rem(z + d, N_Z)}, on_x(d), on_y(d)):
            pl.semaphore_signal(barrier, inc=1, device_id=who, device_id_type=MESH)
    pl.semaphore_signal(barrier, inc=1, device_id=sib, device_id_type=MESH)
    pl.semaphore_wait(barrier, 10)

    def note(d):
        return remote(dots, dots_all.at[d - 1], ds_.at[d], dr.at[d], {"tp": lax.rem(z + d, N_Z)})

    for d in (1, 2, 3):
        note(d).start()

    def ship(i):
        return remote(sbuf.at[i], rbuf.at[i], zs.at[i], zr.at[i], {"tp": right if i % 2 == 0 else left})

    def share(i, h):
        at = slice(h * HALF, (h + 1) * HALF)
        return nt(grads[at, :QC + KC], wv[i]) + nt(grads[at, QC + KC:], wu[i])

    def first(i, w, h):
        sbuf[i] = share(w, h).astype(BF)
        ship(i).start()

    wl[0].wait()
    ul[0].wait()
    first(0, 0, 0)
    first(1, 0, 1)
    for k in rows:
        k.wait()

    def swap(i):
        b = lax.rem(y + 1 + i, 4)
        return remote(dw.at[other, b], pair.at[b], ps.at[i], pr.at[i], sib)

    def terms(i, carry):
        b = lax.rem(y + 1 + i, 4)
        lo = tn(xv[b], grads[...]).astype(BF)
        hi = tn(cv[b], outs[...]).astype(BF)
        for j in range(8):
            at = slice(112 * j, 112 * (j + 1))
            dw[0, b, j // 2, j % 2] = lo[at, :QC + KC]
            dw[1, b, j // 2, j % 2, :, :KC] = lo[at, QC + KC:]
            dw[1, b, j // 2, j % 2, :, KC:] = hi[at]
        swap(i).start()
        return carry

    lax.fori_loop(0, 2, terms, 0)
    for k in (wl[1], ul[1], wl[2], ul[2]):
        k.wait()
    first(2, 1, 1)
    first(3, 2, 0)
    lax.fori_loop(2, 4, terms, 0)
    for i, w in ((4, 1), (5, 2)):
        a = share(w, i % 2)
        ship(i - 4).wait_recv()
        sbuf[i] = (a + rbuf[i - 4].astype(F32)).astype(BF)
        ship(i).start()

    def hop_y(d):
        return remote(dw.at[c, lax.rem(y + d, 4), :, 1], r1.at[1, d - 1], s1s.at[1, d - 1], s1r.at[1, d - 1], on_y(d))

    def hop_x(d):
        return remote(dw.at[c, :, lax.rem(x + d, 4), 0], r1.at[0, d - 1], s1s.at[0, d - 1], s1r.at[0, d - 1], on_x(d))

    def chip_sum(i, carry):
        b = lax.rem(y + 1 + i, 4)
        swap(i).wait_recv()
        for j in range(4):
            dw[c, b, j] = (dw[c, b, j].astype(F32) + pair[b, j].astype(F32)).astype(BF)

        @pl.when(i < 3)
        def _():
            hop_y(i + 1).start()

        return carry

    lax.fori_loop(0, 4, chip_sum, 0)
    for d in (1, 2, 3):
        hop_x(d).start()
    wl[3].wait()
    ul[3].wait()
    own = share(3, 0)
    sbuf[6] = own.astype(BF)
    own = share(3, 1)
    sbuf[7] = own.astype(BF)
    for d in (1, 2, 3):
        note(d).wait()
    m = (dots[...] + dots_all[0] + dots_all[1] + dots_all[2]) * (1.0 / D)

    for d in (1, 2, 3):
        hop_y(d).wait_recv()
        hop_x(d).wait_recv()
    for j in range(4):
        s1[1, j] = (dw[c, y, j, 1].astype(F32) + r1[1, 0, j].astype(F32) + r1[1, 1, j].astype(F32)
                    + r1[1, 2, j].astype(F32)).astype(BF)
        s1[0, j] = (dw[c, j, x, 0].astype(F32) + r1[0, 0, j].astype(F32) + r1[0, 1, j].astype(F32)
                    + r1[0, 2, j].astype(F32)).astype(BF)

    def last_x(d):
        return remote(s1.at[1, lax.rem(x + d, 4)], r2.at[1, d - 1], s2s.at[1, d - 1], s2r.at[1, d - 1], on_x(d))

    def last_y(d):
        return remote(s1.at[0, lax.rem(y + d, 4)], r2.at[0, d - 1], s2s.at[0, d - 1], s2r.at[0, d - 1], on_y(d))

    for d in (1, 2, 3):
        last_x(d).start()
        last_y(d).start()
    for d in (1, 2, 3):
        last_x(d).wait_recv()
        last_y(d).wait_recv()
    for p, own in ((0, s1[0, y]), (1, s1[1, x])):
        s2[p] = (own.astype(F32) + r2[p, 0].astype(F32) + r2[p, 1].astype(F32) + r2[p, 2].astype(F32)).astype(BF)
    trade = remote(s2.at[other], fin.at[c], fs.at[0], fr.at[0], sib)
    trade.start()
    for i in (2, 3, 4, 5):
        ship(i).wait_recv()
    gain_own = gain[:, pl.ds(pl.multiple_of(z * FB, 128), FB)].astype(F32)
    for b in range(TOK // TB):
        h, r = divmod(b * TB, HALF)
        at = slice(b * TB, (b + 1) * TB)
        hs = slice(r, r + TB)
        one, two = (4, 3) if h == 0 else (2, 5)
        s = sbuf[6 + h, hs, :].astype(F32) + rbuf[one, hs, :].astype(F32) + rbuf[two, hs, :].astype(F32)
        mc = jnp.transpose(jnp.broadcast_to(m[:1, at], (128, TB)))[:, :1]
        inv = inv_b[at, :1]
        result[at, :] = (adv_b[at, :1] * cv[z, at, :].astype(F32) + s * gain_own
                         - packed[at, :].astype(F32) * (inv * mc)).astype(BF)
    trade.wait()
    mine = s2[c]
    got = fin[other]
    low_out[...] = jnp.where(c == 0, mine, got)
    high_out[...] = jnp.where(c == 0, got, mine)
    for i in range(6):
        ship(i).wait_send()
    for i in range(4):
        swap(i).wait_send()
    for d in (1, 2, 3):
        hop_x(d).wait_send()
        hop_y(d).wait_send()
        last_x(d).wait_send()
        last_y(d).wait_send()


def split_kernel(result, low, high, res, res_q, res_k, res_v, res_o):
    res[...] = result[...]
    res_q[...] = low[:, :QC]
    res_k[...] = low[:, QC:]
    res_v[...] = high[:, :KC]
    res_o[...] = high[:, KC:]


def sds(shape, dtype=BF):
    return jax.ShapeDtypeStruct(shape, dtype)


def params(**kw):
    return pltpu.CompilerParams(vmem_limit_bytes=LIMIT, has_side_effects=True, **kw)


def rope_table():
    i = np.arange(HD // 2, dtype=np.float32)
    frequency = np.float32(ROPE_BASE) ** (-(np.float32(2.0) * i) / np.float32(HD))
    angle = np.arange(128, dtype=np.float32)[:, None] * frequency[None, :]
    c, s = np.cos(angle), np.sin(angle)
    return np.concatenate([c, c, -s, s], axis=1).astype(np.float32)


def per_device(roll_rows, dest, lengths, clusters, log_prob_grad, gain, w_q, w_k, w_v, w_o_t):
    gain = gain.reshape(1, D)
    send_a, send_b, meta = pl.pallas_call(
        stage_kernel, out_shape=(sds((SEQ * SLAB, FA)), sds((SEQ * SLAB, FB - FA)), sds((SEQ * 8, 128), F32)),
        in_specs=[SMEM, VMEM, VMEM, VMEM], out_specs=(VMEM,) * 3, compiler_params=params(),
    )(dest, dest.reshape(1, SEQ), clusters.reshape(1, SEQ), roll_rows)
    n_o = len(OFFSETS)
    width = QC + 2 * KC
    half = (112, QC + KC)
    v = pltpu.VMEM
    ring = [DMA((6,)), DMA((6,))]
    rows, cot, weights, packed, grads, outs, inv_b, adv_b, dots = pl.pallas_call(
        front_kernel,
        out_shape=(sds((N_Z, TOK, FB)), sds((N_Z, TOK, FB)), sds((2, 4, 4, 2) + half), sds((TOK, FB)),
                   sds((TOK, width)), sds((TOK, QC)), sds((TOK, 128), F32), sds((TOK, 128), F32), sds((8, TOK), F32)),
        in_specs=[HBM] * 4 + [VMEM] * 7, out_specs=(HBM,) * 3 + (VMEM,) * 6,
        scratch_shapes=[
            v((SEQ * SLAB, FA), BF), v((SEQ * SLAB, FB - FA), BF), v((SEQ * 8, 128), F32), v((TOK, SEQ * SLAB), BF),
            v((N_Z, TOK, FB), BF), v((N_Z, TOK, FB), BF), v((2,) + half, BF), v((2, 4, 4, 2) + half, BF),
            v((8, TOK), F32), v((3, 8, TOK), F32), v((TOK, 128), F32), v((TOK, 2 * HD), F32), v((TOK, 128), F32),
            v((TOK, width), F32), v((TOK, QC), F32),
            v((TOK, QC), BF), v((TOK + TB, HD), BF), v((TOK + TB, HD), BF),
            v((TOK, QC), BF), v((TOK + TB, HD), F32), v((TOK + TB, HD), F32), v((TOK, HD), F32),
            DMA((4,)), DMA((3,))] + [DMA((n_o,))] * 6 + ring * 3 + [DMA((4,)), DMA((4,)), DMA((1,)), DMA((1,))]
        + [DMA((2, 3))] * 4 + [DMA((7,))] * 2,
        compiler_params=params(collective_id=0),
    )(send_a, send_b, meta, log_prob_grad, lengths, gain, jnp.asarray(rope_table()), w_q, w_k, w_v, w_o_t)
    result, low, high = pl.pallas_call(
        grad_kernel,
        out_shape=(sds((TOK, FB)), sds(half), sds(half)),
        in_specs=[VMEM, VMEM] + [HBM] * 3 + [VMEM] * 5, out_specs=(VMEM,) * 3,
        scratch_shapes=[
            v((N_Z, FB, QC + KC), BF), v((N_Z, FB, KC), BF), v((N_Z, TOK, FB), BF), v((N_Z, TOK, FB), BF),
            v((3, 8, TOK), F32), v((8, HALF, FB), BF), v((6, HALF, FB), BF),
            v((2, 4, 4, 2) + half, BF), v((4, 4, 2) + half, BF),
            v((2, 3, 4) + half, BF), v((2, 4) + half, BF), v((2, 3) + half, BF),
            v((2,) + half, BF), v((2,) + half, BF),
            DMA((N_Z, 4)), DMA((6,)), DMA((6,)), DMA((4,)), DMA((4,)), DMA((4,)), DMA((4,)),
            DMA((2, 3)), DMA((2, 3)), DMA((2, 3)), DMA((2, 3)), DMA((1,)), DMA((1,))],
        compiler_params=params(collective_id=1),
    )(grads, outs, rows, cot, weights.reshape(2, N_Z, FB, QC + KC), dots, packed, gain, inv_b, adv_b)
    return pl.pallas_call(
        split_kernel,
        out_shape=(sds((TOK, FB)), sds((112, QC)), sds((112, KC)), sds((112, KC)), sds((112, QC))),
        in_specs=[VMEM] * 3, out_specs=(VMEM,) * 5, compiler_params=params(),
    )(result, low, high)


def solution(mesh):
    in_specs = (
        P("fsdp", None, "tp"), P("fsdp"), P("fsdp", None), P("fsdp"), P("fsdp", "tp"), P(),
        P("fsdp", "tp"), P("fsdp", "tp"), P("fsdp", "tp"), P("fsdp", "tp"),
    )
    out_specs = (P("fsdp", "tp"),) * 5
    return jax.shard_map(per_device, mesh=mesh, in_specs=in_specs, out_specs=out_specs, check_vma=False)
```

```python
import jax
import jax.numpy as jnp
import numpy as np
from jax import lax
from jax.experimental import pallas as pl
from jax.experimental.pallas import tpu as pltpu
from jax.sharding import PartitionSpec as P

HD = 128
GSIZE = 16
ROPE_BASE = 1000000.0
NORM_EPSILON = 1e-06
MESH = pl.DeviceIdType.MESH
BF = jnp.bfloat16
F32 = jnp.float32
HBM = pl.BlockSpec(memory_space=pl.ANY)
VMEM = pl.BlockSpec(memory_space=pltpu.VMEM)
SMEM = pl.BlockSpec(memory_space=pltpu.SMEM)
DMA = pltpu.SemaphoreType.DMA
LIMIT = 60 * 2**20

N_F = 32
N_Z = 4
SEQ = 32
MAXLEN = 72
TOK = 768
HALF = TOK // 2
FB = 896
FA = 512
SLAB = 80
D = 3584
QC = 512
KC = 128
TB = 128

CHIPS = [(0, 1), (1, 0), (0, 3), (3, 0), (1, 1), (3, 3), (1, 3), (3, 1),
         (0, 2), (2, 0), (1, 2), (2, 1), (3, 2), (2, 3), (2, 2)]
OFFSETS = [(0, 0, 1)] + [(a, b, c) for c in range(2) for a, b in CHIPS]


def nt(a, b):
    return lax.dot_general(a, b, (((1,), (1,)), ((), ())), preferred_element_type=F32)


def tn(a, b):
    return lax.dot_general(a, b, (((0,), (0,)), ((), ())), preferred_element_type=F32)


def nn(a, b):
    return lax.dot_general(a, b, (((1,), (0,)), ((), ())), preferred_element_type=F32)


def iota(shape, dim):
    return lax.broadcasted_iota(jnp.int32, shape, dim)


def diagonal(row, n):
    return jnp.sum(jnp.where(iota((n, n), 0) == iota((n, n), 1), row, 0.0), axis=1, keepdims=True)


def stage_kernel(dest_s, dest_r, clus_r, roll, send_a, send_b, meta):
    def place(s, c):
        at = pl.ds(pl.multiple_of((dest_s[s] // SEQ) * SLAB, 16), SLAB)
        v = jnp.concatenate([roll[s], jnp.zeros((SLAB - MAXLEN, FB), BF)], axis=0)
        send_a[at, :] = v[:, :FA]
        send_b[at, :] = v[:, FA:]
        return c

    lax.fori_loop(0, SEQ, place, 0)
    clus = clus_r[...].astype(F32)
    group = iota((SEQ, SEQ), 0) // GSIZE == iota((SEQ, SEQ), 1) // GSIZE
    same = jnp.where((diagonal(clus, SEQ) == clus) & group, 1.0 / GSIZE, 0.0)
    share_c = jnp.sum(same, axis=1, keepdims=True)
    share_r = jnp.sum(same, axis=0, keepdims=True)
    mean_r = jnp.sum(jnp.where(group, share_c, 0.0), axis=0, keepdims=True) * (1.0 / GSIZE)
    adv_r = (share_r - mean_r).astype(BF).astype(F32)
    rows = iota((SEQ * 8, SEQ), 0)
    dest_v = dest_r[...]
    hit = dest_v // SEQ == rows // 8
    what = jnp.where(rows % 8 < 4, (dest_v % SEQ).astype(F32), adv_r)
    meta[...] = jnp.broadcast_to(jnp.sum(jnp.where(hit, what, 0.0), axis=1, keepdims=True), (SEQ * 8, 128))


def remote(src, dst, ss, rs, who):
    return pltpu.make_async_remote_copy(
        src_ref=src, dst_ref=dst, send_sem=ss, recv_sem=rs, device_id=who, device_id_type=MESH)


class Ring:
    def __init__(self, own, dst, cols, z, ss, rs):
        self.own, self.dst, self.cols, self.z, self.ss, self.rs = own, dst, cols, z, ss, rs
        self.right, self.left, self.far = (lax.rem(z + d, N_Z) for d in (1, 3, 2))

    def copy(self, i, blk, src=None):
        half = (0, 1, 1, 0, 0, 1)[i]
        at = pl.ds(half * HALF, HALF)
        to = self.right if i % 2 == 0 else self.left
        src = self.own if src is None else src
        return remote(src.at[at, self.cols], self.dst.at[blk, at, self.cols], self.ss.at[i], self.rs.at[i], {"tp": to})

    def start(self):
        for i in range(4):
            self.copy(i, self.z).start()

    def hand_on(self):
        for i, blk in ((0, self.left), (1, self.right)):
            self.copy(i, blk).wait_recv()
            self.copy(i + 4, blk, self.dst.at[blk]).start()

    def near(self):
        self.copy(2, self.left).wait_recv()
        self.copy(3, self.right).wait_recv()

    def end(self):
        self.copy(4, self.far).wait_recv()
        self.copy(5, self.far).wait_recv()

    def sent(self):
        for i in range(4):
            self.copy(i, self.z).wait_send()
        self.copy(4, self.left, self.dst.at[self.left]).wait_send()
        self.copy(5, self.right, self.dst.at[self.right]).wait_send()


def unstack(v):
    return jnp.concatenate([v[h * TB:(h + 1) * TB] for h in range(4)], axis=1)


def stack(v):
    return jnp.concatenate([v[:, h * HD:(h + 1) * HD] for h in range(4)], axis=0)


def turn(v, cos, sin):
    return v * cos + jnp.concatenate([v[:, HD // 2:], v[:, :HD // 2]], axis=1) * sin


def turn_back(v, cos, sin):
    return v * cos - jnp.concatenate([v[:, HD // 2:], v[:, :HD // 2]], axis=1) * sin


def whole_kernel(send_a, send_b, meta, cot, len_r, gain, table, w_q, w_k, w_v, w_o,
                 result, low_out, high_out,
                 arr, meta_in, xv, cv, wsh, wv, sq, sq_all, sqc, rope, pos_b, grads, outs, inv_b, adv_b, dots,
                 dots_all, rbuf, pair, r1, r2, s2, fin,
                 lsem, as_, ar, bs, br, ms, mr, zs, zr, us, ur, vs, vr, qs, qr,
                 w0s, w0r, w1s, w1r, w2s, w2r, w3s, w3r,
                 gs, gr, ds_, dr, ps, pr, s1s, s1r, s2s, s2r, fs, fr):
    packed = result
    me = lax.axis_index("fsdp")
    z = lax.axis_index("tp")
    y, x, c = me // 8, (me // 2) % 4, me % 2
    other = 1 - c
    sib = {"fsdp": y * 8 + x * 2 + other}

    def peer(o, s):
        return lax.rem(y + s * o[0] + 4, 4) * 8 + lax.rem(x + s * o[1] + 4, 4) * 2 + lax.rem(c + s * o[2] + 2, 2)

    def on_x(d):
        return {"fsdp": peer((0, d, 0), 1)}

    def on_y(d):
        return {"fsdp": peer((d, 0, 0), 1)}

    cot_own = pltpu.make_async_copy(cot, cv.at[z], lsem.at[0])
    cot_own.start()
    barrier = pltpu.get_barrier_semaphore()
    for o in OFFSETS:
        pl.semaphore_signal(barrier, inc=1, device_id={"fsdp": peer(o, 1)}, device_id_type=MESH)
    for d in (1, 2, 3):
        pl.semaphore_signal(barrier, inc=1, device_id={"tp": lax.rem(z + d, N_Z)}, device_id_type=MESH)
    pl.semaphore_wait(barrier, len(OFFSETS) + 3)

    ring_c = Ring(cot, cv, pl.ds(0, FB), z, zs, zr)
    ring_a = Ring(xv.at[z], xv, pl.ds(0, FA), z, us, ur)
    ring_b = Ring(xv.at[z], xv, pl.ds(FA, FB - FA), z, vs, vr)
    ring_c.start()

    def slab(k):
        return pl.ds(pl.multiple_of(k * SLAB, 16), SLAB)

    def eight(k):
        return pl.ds(pl.multiple_of(k * 8, 8), 8)

    def part_a(i, frm, to, who):
        return remote(send_a.at[slab(frm)], arr.at[slab(to), pl.ds(0, FA)], as_.at[i], ar.at[i], {"fsdp": who})

    def part_b(i, frm, to, who):
        return remote(send_b.at[slab(frm)], arr.at[slab(to), pl.ds(FA, FB - FA)], bs.at[i], br.at[i], {"fsdp": who})

    def note(i, frm, to, who):
        return remote(meta.at[eight(frm)], meta_in.at[eight(to)], ms.at[i], mr.at[i], {"fsdp": who})

    for kind in (note, part_a, part_b):
        for i, o in enumerate(OFFSETS):
            t = peer(o, 1)
            kind(i, t, me, t).start()
    mine = [pltpu.make_async_copy(send_a.at[slab(me)], arr.at[slab(me), pl.ds(0, FA)], lsem.at[1]),
            pltpu.make_async_copy(send_b.at[slab(me)], arr.at[slab(me), pl.ds(FA, FB - FA)], lsem.at[2]),
            pltpu.make_async_copy(meta.at[eight(me)], meta_in.at[eight(me)], lsem.at[3])]
    for k in mine:
        k.start()

    wsh[0, :, :QC] = w_q[...]
    wsh[0, :, QC:] = w_k[...]
    wsh[1, :, :KC] = w_v[...]
    wsh[1, :, KC:] = w_o[...]
    wv[0, y, x, c] = wsh[0]
    wv[1, y, x, c] = wsh[1]
    w_pair = remote(wsh.at[other], wv.at[other, y, x, c], w0s.at[0], w0r.at[0], sib)
    w_pair.start()

    def w_near(p, d):
        return remote(wv.at[c, y, x, p], wv.at[c, y, x, p], w1s.at[p, d - 1], w1r.at[p, d - 1], on_y(d) if p else on_x(d))

    def w_next(p, d):
        blk = wv.at[c, :, x, 1] if p else wv.at[c, y, :, 0]
        return remote(blk, blk, w2s.at[p, d - 1], w2r.at[p, d - 1], on_x(d) if p else on_y(d))

    def w_last(d):
        if d < 3:
            blk = wv.at[c, lax.rem(y + d + 1, 4)]
        elif d < 6:
            blk = wv.at[c, y, lax.rem(x + d - 2, 4)]
        else:
            blk = wv.at[c, y, x, c]
        return remote(blk, blk, w3s.at[d], w3r.at[d], sib)

    hops = [(p, d) for d in (1, 2, 3) for p in (0, 1)]
    w_pair.wait_recv()
    for p, d in hops:
        w_near(p, d).start()

    lens = diagonal(len_r[...].astype(F32), SEQ)
    gain_own = gain[:, pl.ds(pl.multiple_of(z * FB, 128), FB)].astype(F32)
    lane = iota((SEQ, 128), 1)
    sub = iota((SEQ, 128), 0)
    ends = jnp.sum(jnp.where(sub <= lane, lens, 0.0), axis=0, keepdims=True)
    starts = jnp.sum(jnp.where(sub < lane, lens, 0.0), axis=0, keepdims=True)
    for i, o in enumerate(OFFSETS):
        note(i, peer(o, 1), peer(o, -1), peer(o, 1)).wait_recv()
    mine[2].wait()
    place = meta_in[pl.ds(0, SEQ, 8), :]
    share = meta_in[pl.ds(4, SEQ, 8), :]
    place_r = jnp.where(iota((1, 128), 1) < SEQ, jnp.sum(jnp.where(sub == lane, place, 0.0), axis=0, keepdims=True), -1.0)
    share_r = jnp.sum(jnp.where(sub == lane, share, 0.0), axis=0, keepdims=True)
    column = iota((SEQ, SEQ * SLAB), 1) - iota((SEQ, SEQ * SLAB), 0) * SLAB
    here = (column >= 0) & (column < SLAB)
    key = jnp.sum(jnp.where(here, place[:, :1] * 128.0 + column.astype(F32), 0.0), axis=0, keepdims=True)

    def packing(pick):
        def layout(b):
            at = pl.ds(b * TB, TB)
            i = (iota((TB, 128), 0) + b * TB).astype(F32)
            lane_f = iota((TB, 128), 1).astype(F32)
            hit = (i >= starts) & (i < ends)
            seg = jnp.sum(jnp.where(hit, lane_f, 0.0), axis=1, keepdims=True)
            pos = i - jnp.sum(jnp.where(hit, starts, 0.0), axis=1, keepdims=True)
            pos_b[at, :] = pos
            adv_b[at, :] = jnp.broadcast_to(
                jnp.sum(jnp.where(place_r == seg, share_r, 0.0), axis=1, keepdims=True), (TB, 128))
            rope[at, :] = lax.dot_general(
                jnp.where(pos == lane_f, 1.0, 0.0), table[...], (((1,), (0,)), ((), ())),
                precision=lax.Precision.HIGHEST, preferred_element_type=F32)
            pick[at, :] = jnp.where(seg * 128.0 + pos[:, :1] == key, 1.0, 0.0).astype(BF)

        for b in range(TOK // TB):
            layout(b)
        ring_c.hand_on()

        def pack(lo, hi):
            def rows(b, carry):
                at = pl.ds(pl.multiple_of(b * 256, 256), 256)
                took = nn(pick[at, :], arr[:, lo:hi])
                packed[at, lo:hi] = took.astype(BF)
                xv[z, at, lo:hi] = (took * gain_own[:, lo:hi]).astype(BF)
                square = took * took
                lanes = sum(square[:, k:k + 128] for k in range(0, hi - lo, 128))
                sqc[at, :] = lanes if lo == 0 else sqc[at, :] + lanes
                return carry

            lax.fori_loop(0, TOK // 256, rows, 0)

        for i, o in enumerate(OFFSETS):
            part_a(i, peer(o, 1), peer(o, -1), peer(o, 1)).wait_recv()
        mine[0].wait()
        pack(0, FA)
        ring_a.start()
        ring_c.near()
        ring_c.end()
        cot_own.wait()
        ring_a.hand_on()
        for i, o in enumerate(OFFSETS):
            part_b(i, peer(o, 1), peer(o, -1), peer(o, 1)).wait_recv()
        mine[1].wait()
        for p, d in hops:
            w_near(p, d).wait_recv()
        for p, d in hops:
            w_next(p, d).start()
        pack(FA, FB)
        ring_b.start()
    pl.run_scoped(packing, scratch((TOK, SEQ * SLAB)))
    for b in range(TOK // TB):
        square = jnp.sum(sqc[b * TB:(b + 1) * TB, :], axis=1, keepdims=True)
        sq[:, b * TB:(b + 1) * TB] = jnp.transpose(jnp.broadcast_to(square, (TB, 128)))[:8, :]

    def tell(d):
        return remote(sq, sq_all.at[d - 1], qs.at[d], qr.at[d], {"tp": lax.rem(z + d, N_Z)})

    for d in (1, 2, 3):
        tell(d).start()
    ring_b.hand_on()
    ring_a.near()
    ring_a.end()
    for d in (1, 2, 3):
        tell(d).wait_recv()
    inv_t = lax.rsqrt((sq[...] + sq_all[0] + sq_all[1] + sq_all[2]) * (1.0 / D) + NORM_EPSILON)
    for b in range(TOK // TB):
        inv_b[b * TB:(b + 1) * TB, :] = jnp.transpose(jnp.broadcast_to(inv_t[:1, b * TB:(b + 1) * TB], (128, TB)))
    for p, d in hops:
        w_next(p, d).wait_recv()
    for d in range(7):
        w_last(d).start()
    for d in range(7):
        w_last(d).wait_recv()

    def whole(h, blk):
        return wv[h, blk].reshape(FB, QC + KC)

    def attention(kbuf, vbuf, dk, dv, lin, ga, qrot, gab, mq):
        kbuf[:TB, :] = jnp.zeros((TB, HD), BF)
        vbuf[:TB, :] = jnp.zeros((TB, HD), BF)
        dk[...] = jnp.zeros_like(dk)
        dv[...] = jnp.zeros_like(dv)
        def project_c(d, carry):
            t = nn(cv[d], whole(1, d)[:, KC:])

            @pl.when(d == 0)
            def _():
                ga[...] = t

            @pl.when(d > 0)
            def _():
                ga[...] += t

            return carry

        lax.fori_loop(0, N_Z, project_c, 0)
        lin[...] = jnp.zeros_like(lin)

        def project_x(d, carry):
            blk = lax.rem(z + d, N_Z)
            lin[:, :QC + KC] += nn(xv[blk], whole(0, blk))
            lin[:, QC + KC:] += nn(xv[blk], whole(1, blk)[:, :KC])
            return carry

        project_x(0, 0)
        ring_b.near()
        lax.fori_loop(0, 2, lambda k, carry: project_x(1 + 2 * k, carry), 0)
        ring_b.end()
        project_x(2, 0)

        def ready(b, carry):
            at = pl.ds(pl.multiple_of(b * TB, TB), TB)
            up = pl.ds(pl.multiple_of(b * TB + TB, TB), TB)
            inv = inv_b[at, :]
            cos, sin = rope[at, :HD], rope[at, HD:]
            for h in range(4):
                qrot[at, h * HD:(h + 1) * HD] = turn(lin[at, h * HD:(h + 1) * HD] * inv, cos, sin).astype(BF)
                gab[at, h * HD:(h + 1) * HD] = (ga[at, h * HD:(h + 1) * HD] * adv_b[at, :]).astype(BF)
            kbuf[up, :] = turn(lin[at, QC:QC + KC] * inv, cos, sin).astype(BF)
            vbuf[up, :] = (lin[at, QC + KC:] * inv).astype(BF)
            return carry

        lax.fori_loop(0, TOK // TB, ready, 0)
        scale = HD ** (-0.5)

        def attend(b, carry):
            at = pl.ds(pl.multiple_of(b * TB, TB), TB)
            win = pl.ds(pl.multiple_of(b * TB, TB), 2 * TB)
            q = stack(qrot[at, :])
            g = stack(gab[at, :])
            k, v = kbuf[win, :], vbuf[win, :]
            back = iota((TB, 2 * TB), 0) + TB - iota((TB, 2 * TB), 1)
            ok = (back >= 0) & (back.astype(F32) <= pos_b[at, :1])
            ok = jnp.concatenate([ok] * 4, axis=0)
            s = jnp.where(ok, nt(q, k) * scale, -1e30)
            e = jnp.where(ok, jnp.exp(s - jnp.max(s, axis=1, keepdims=True)), 0.0)
            p = e / jnp.sum(e, axis=1, keepdims=True)
            pb = p.astype(BF)
            o = unstack(nn(pb, v))
            dp = nt(g, v)
            ds = (p * (dp - jnp.sum(p * dp, axis=1, keepdims=True)) * scale).astype(BF)
            dq = nn(ds, k)
            dk[win, :] += tn(ds, q)
            dv[win, :] += tn(pb, g)
            prod = dq * q.astype(F32)
            mq[at, :] = prod[:TB] + prod[TB:2 * TB] + prod[2 * TB:3 * TB] + prod[3 * TB:]
            dq = unstack(dq)
            inv = inv_b[at, :]
            cos, sin = rope[at, :HD], rope[at, HD:]
            for h in range(4):
                col = slice(h * HD, (h + 1) * HD)
                grads[at, col] = (turn_back(dq[:, col], cos, sin) * inv).astype(BF)
                outs[at, col] = (o[:, col] * adv_b[at, :]).astype(BF)
            return carry

        lax.fori_loop(0, TOK // TB, attend, 0)

        def finish(b, carry):
            at = pl.ds(pl.multiple_of(b * TB, TB), TB)
            up = pl.ds(pl.multiple_of(b * TB + TB, TB), TB)
            inv = inv_b[at, :]
            cos, sin = rope[at, :HD], rope[at, HD:]
            gk, gv = dk[up, :], dv[up, :]
            grads[at, QC:QC + KC] = (turn_back(gk, cos, sin) * inv).astype(BF)
            grads[at, QC + KC:] = (gv * inv).astype(BF)
            m = mq[at, :] + gk * kbuf[up, :].astype(F32) + gv * vbuf[up, :].astype(F32)
            m = jnp.sum(m, axis=1, keepdims=True) * inv
            dots[:, at] = jnp.transpose(jnp.broadcast_to(m, (TB, 128)))[:8, :]
            return carry

        lax.fori_loop(0, TOK // TB, finish, 0)
    v = scratch
    pl.run_scoped(attention, v((TOK + TB, HD)), v((TOK + TB, HD)), v((TOK + TB, HD), F32), v((TOK + TB, HD), F32),
                  v((TOK, WIDTH), F32), v((TOK, QC), F32), v((TOK, QC)), v((TOK, QC)), v((TOK, HD), F32))
    ring_c.sent()
    right, left, far = lax.rem(z + 1, N_Z), lax.rem(z + 3, N_Z), lax.rem(z + 2, N_Z)
    order = [far, right, left, z]

    def gradients(dw, s1):
        def dot_note(d):
            return remote(dots, dots_all.at[d - 1], ds_.at[d], dr.at[d], {"tp": lax.rem(z + d, N_Z)})

        for d in (1, 2, 3):
            dot_note(d).start()

        def ship(i):
            return remote(arr.at[pl.ds(i * HALF, HALF)], rbuf.at[i], gs.at[i], gr.at[i], {"tp": right if i % 2 == 0 else left})

        def share(i, h):
            at = slice(h * HALF, (h + 1) * HALF)
            return nt(grads[at, :QC + KC], whole(0, order[i])) + nt(grads[at, QC + KC:], whole(1, order[i])[:, :KC])

        def first(i, w, h):
            arr[i * HALF:(i + 1) * HALF, :] = share(w, h).astype(BF)
            ship(i).start()

        first(0, 0, 0)
        first(1, 0, 1)
        def swap(i):
            b = lax.rem(y + 1 + i, 4)
            return remote(dw.at[other, b], pair.at[b], ps.at[i], pr.at[i], sib)

        def terms(i, carry):
            b = lax.rem(y + 1 + i, 4)
            def place(h, cols, v):
                for j in range(8):
                    dw[h, b, j // 2, j % 2, :, cols] = v[112 * j:112 * (j + 1)]

            place(0, slice(0, QC), tn(xv[b], grads[:, :QC]).astype(BF))
            t = tn(xv[b], grads[:, QC:]).astype(BF)
            place(0, slice(QC, QC + KC), t[:, :KC])
            place(1, slice(0, KC), t[:, KC:])
            place(1, slice(KC, QC + KC), tn(cv[b], outs[...]).astype(BF))
            swap(i).start()
            return carry

        lax.fori_loop(0, 2, terms, 0)
        first(2, 1, 1)
        first(3, 2, 0)
        lax.fori_loop(2, 4, terms, 0)
        for i, w in ((4, 1), (5, 2)):
            a = share(w, i % 2)
            ship(i - 4).wait_recv()
            arr[i * HALF:(i + 1) * HALF, :] = (a + rbuf[i - 4].astype(F32)).astype(BF)
            ship(i).start()

        def hop_y(d):
            return remote(dw.at[c, lax.rem(y + d, 4), :, 1], r1.at[1, d - 1], s1s.at[1, d - 1], s1r.at[1, d - 1], on_y(d))

        def hop_x(d):
            return remote(dw.at[c, :, lax.rem(x + d, 4), 0], r1.at[0, d - 1], s1s.at[0, d - 1], s1r.at[0, d - 1], on_x(d))

        def chip_sum(i, carry):
            b = lax.rem(y + 1 + i, 4)
            swap(i).wait_recv()
            for j in range(4):
                dw[c, b, j] = (dw[c, b, j].astype(F32) + pair[b, j].astype(F32)).astype(BF)

            @pl.when(i < 3)
            def _():
                hop_y(i + 1).start()

            return carry

        lax.fori_loop(0, 4, chip_sum, 0)
        for d in (1, 2, 3):
            hop_x(d).start()
        for h in range(2):
            cv[right, h * HALF:(h + 1) * HALF, :] = share(3, h).astype(BF)
        for d in (1, 2, 3):
            dot_note(d).wait()
        m = (dots[...] + dots_all[0] + dots_all[1] + dots_all[2]) * (1.0 / D)

        for d in (1, 2, 3):
            hop_y(d).wait_recv()
            hop_x(d).wait_recv()
        for j in range(4):
            s1[1, j] = (dw[c, y, j, 1].astype(F32) + r1[1, 0, j].astype(F32) + r1[1, 1, j].astype(F32)
                        + r1[1, 2, j].astype(F32)).astype(BF)
            s1[0, j] = (dw[c, j, x, 0].astype(F32) + r1[0, 0, j].astype(F32) + r1[0, 1, j].astype(F32)
                        + r1[0, 2, j].astype(F32)).astype(BF)

        def last_x(d):
            return remote(s1.at[1, lax.rem(x + d, 4)], r2.at[1, d - 1], s2s.at[1, d - 1], s2r.at[1, d - 1], on_x(d))

        def last_y(d):
            return remote(s1.at[0, lax.rem(y + d, 4)], r2.at[0, d - 1], s2s.at[0, d - 1], s2r.at[0, d - 1], on_y(d))

        for d in (1, 2, 3):
            last_x(d).start()
            last_y(d).start()
        for d in (1, 2, 3):
            last_x(d).wait_recv()
            last_y(d).wait_recv()
        for p, own in ((0, s1[0, y]), (1, s1[1, x])):
            s2[p] = (own.astype(F32) + r2[p, 0].astype(F32) + r2[p, 1].astype(F32) + r2[p, 2].astype(F32)).astype(BF)
        trade = remote(s2.at[other], fin.at[c], fs.at[0], fr.at[0], sib)
        trade.start()
        for i in (2, 3, 4, 5):
            ship(i).wait_recv()
        gain_own = gain[:, pl.ds(pl.multiple_of(z * FB, 128), FB)].astype(F32)
        for b in range(TOK // TB):
            h, r = divmod(b * TB, HALF)
            at = slice(b * TB, (b + 1) * TB)
            hs = slice(r, r + TB)
            one, two = (4, 3) if h == 0 else (2, 5)
            s = cv[right, at, :].astype(F32) + rbuf[one, hs, :].astype(F32) + rbuf[two, hs, :].astype(F32)
            mc = jnp.transpose(jnp.broadcast_to(m[:1, at], (128, TB)))[:, :1]
            inv = inv_b[at, :1]
            result[at, :] = (adv_b[at, :1] * cv[z, at, :].astype(F32) + s * gain_own
                             - packed[at, :].astype(F32) * (inv * mc)).astype(BF)
        trade.wait()
        mine = s2[c]
        got = fin[other]
        low_out[...] = jnp.where(c == 0, mine, got)
        high_out[...] = jnp.where(c == 0, got, mine)
        for i in range(6):
            ship(i).wait_send()
        for i in range(4):
            swap(i).wait_send()
        for d in (1, 2, 3):
            hop_x(d).wait_send()
            hop_y(d).wait_send()
            last_x(d).wait_send()
            last_y(d).wait_send()

    pl.run_scoped(gradients, v((2, 4, 4, 2) + PART), v((2, 4) + PART))
    ring_a.sent()
    ring_b.sent()
    for kind in (note, part_a, part_b):
        for i, o in enumerate(OFFSETS):
            t = peer(o, 1)
            kind(i, t, me, t).wait_send()
    w_pair.wait_send()
    for p, d in hops:
        w_near(p, d).wait_send()
        w_next(p, d).wait_send()
    for d in range(7):
        w_last(d).wait_send()
    for d in (1, 2, 3):
        tell(d).wait_send()


def split_kernel(result, low, high, res, res_q, res_k, res_v, res_o):
    res[...] = result[...]
    res_q[...] = low[:, :QC]
    res_k[...] = low[:, QC:]
    res_v[...] = high[:, :KC]
    res_o[...] = high[:, KC:]


def sds(shape, dtype=BF):
    return jax.ShapeDtypeStruct(shape, dtype)


def params(**kw):
    return pltpu.CompilerParams(vmem_limit_bytes=LIMIT, has_side_effects=True, **kw)


def rope_table():
    i = np.arange(HD // 2, dtype=np.float32)
    frequency = np.float32(ROPE_BASE) ** (-(np.float32(2.0) * i) / np.float32(HD))
    angle = np.arange(128, dtype=np.float32)[:, None] * frequency[None, :]
    c, s = np.cos(angle), np.sin(angle)
    return np.concatenate([c, c, -s, s], axis=1).astype(np.float32)


N_O = len(OFFSETS)
WIDTH = QC + 2 * KC
PART = (112, QC + KC)


def scratch(shape, dtype=BF):
    return pltpu.VMEM(shape, dtype)


def stage(*args):
    return pl.pallas_call(
        stage_kernel, out_shape=(sds((SEQ * SLAB, FA)), sds((SEQ * SLAB, FB - FA)), sds((SEQ * 8, 128), F32)),
        in_specs=[SMEM, VMEM, VMEM, VMEM], out_specs=(VMEM,) * 3, compiler_params=params(),
    )(*args)


def whole(*args):
    v = scratch
    ring = [DMA((6,)), DMA((6,))]
    return pl.pallas_call(
        whole_kernel, out_shape=(sds((TOK, FB)), sds(PART), sds(PART)),
        in_specs=[HBM] * 4 + [VMEM] * 7, out_specs=(VMEM,) * 3,
        scratch_shapes=[
            v((SEQ * SLAB, FB)), v((SEQ * 8, 128), F32),
            v((N_Z, TOK, FB)), v((N_Z, TOK, FB)), v((2,) + PART), v((2, 4, 4, 2) + PART),
            v((8, TOK), F32), v((3, 8, TOK), F32), v((TOK, 128), F32), v((TOK, 2 * HD), F32), v((TOK, 128), F32),
            v((TOK, WIDTH)), v((TOK, QC)), v((TOK, 128), F32), v((TOK, 128), F32), v((8, TOK), F32),
            v((3, 8, TOK), F32), v((6, HALF, FB)), v((4, 4, 2) + PART), v((2, 3, 4) + PART), v((2, 3) + PART),
            v((2,) + PART), v((2,) + PART),
            DMA((4,))] + [DMA((N_O,))] * 6 + ring * 3 + [DMA((4,)), DMA((4,)), DMA((1,)), DMA((1,))]
        + [DMA((2, 3))] * 4 + [DMA((7,))] * 2
        + ring + [DMA((4,))] * 4 + [DMA((2, 3))] * 4 + [DMA((1,))] * 2,
        compiler_params=params(collective_id=0),
    )(*args)


def split(*args):
    return pl.pallas_call(
        split_kernel,
        out_shape=(sds((TOK, FB)), sds((112, QC)), sds((112, KC)), sds((112, KC)), sds((112, QC))),
        in_specs=[VMEM] * 3, out_specs=(VMEM,) * 5, compiler_params=params(),
    )(*args)


def per_device(roll_rows, dest, lengths, clusters, log_prob_grad, gain, w_q, w_k, w_v, w_o_t):
    gain = gain.reshape(1, D)
    send_a, send_b, meta = stage(dest, dest.reshape(1, SEQ), clusters.reshape(1, SEQ), roll_rows)
    return split(*whole(
        send_a, send_b, meta, log_prob_grad, lengths, gain, jnp.asarray(rope_table()), w_q, w_k, w_v, w_o_t))


def solution(mesh):
    in_specs = (
        P("fsdp", None, "tp"), P("fsdp"), P("fsdp", None), P("fsdp"), P("fsdp", "tp"), P(),
        P("fsdp", "tp"), P("fsdp", "tp"), P("fsdp", "tp"), P("fsdp", "tp"),
    )
    out_specs = (P("fsdp", "tp"),) * 5
    return jax.shard_map(per_device, mesh=mesh, in_specs=in_specs, out_specs=out_specs, check_vma=False)
```

```python
import jax
import jax.numpy as jnp
import numpy as np
from jax import lax
from jax.experimental import pallas as pl
from jax.experimental.pallas import tpu as pltpu
from jax.sharding import PartitionSpec as P

HD = 128
GSIZE = 16
ROPE_BASE = 1000000.0
NORM_EPSILON = 1e-06
MESH = pl.DeviceIdType.MESH
BF = jnp.bfloat16
F32 = jnp.float32
HBM = pl.BlockSpec(memory_space=pl.ANY)
VMEM = pl.BlockSpec(memory_space=pltpu.VMEM)
SMEM = pl.BlockSpec(memory_space=pltpu.SMEM)
DMA = pltpu.SemaphoreType.DMA
LIMIT = 60 * 2**20

N_F = 32
N_Z = 4
SEQ = 32
MAXLEN = 72
TOK = 768
HALF = TOK // 2
FB = 896
FA = 512
SLAB = 80
D = 3584
QC = 512
KC = 128
TB = 128

CHIPS = [(0, 1), (1, 0), (0, 3), (3, 0), (1, 1), (3, 3), (1, 3), (3, 1),
         (0, 2), (2, 0), (1, 2), (2, 1), (3, 2), (2, 3), (2, 2)]
OFFSETS = [(0, 0, 1)] + [(a, b, c) for c in range(2) for a, b in CHIPS]


def nt(a, b):
    return lax.dot_general(a, b, (((1,), (1,)), ((), ())), preferred_element_type=F32)


def tn(a, b):
    return lax.dot_general(a, b, (((0,), (0,)), ((), ())), preferred_element_type=F32)


def nn(a, b):
    return lax.dot_general(a, b, (((1,), (0,)), ((), ())), preferred_element_type=F32)


def iota(shape, dim):
    return lax.broadcasted_iota(jnp.int32, shape, dim)


def diagonal(row, n):
    return jnp.sum(jnp.where(iota((n, n), 0) == iota((n, n), 1), row, 0.0), axis=1, keepdims=True)


def stage_kernel(dest_s, dest_r, clus_r, roll, send_a, send_b, meta):
    def place(s, c):
        at = pl.ds(pl.multiple_of((dest_s[s] // SEQ) * SLAB, 16), SLAB)
        v = jnp.concatenate([roll[s], jnp.zeros((SLAB - MAXLEN, FB), BF)], axis=0)
        send_a[at, :] = v[:, :FA]
        send_b[at, :] = v[:, FA:]
        return c

    lax.fori_loop(0, SEQ, place, 0)
    clus = clus_r[...].astype(F32)
    group = iota((SEQ, SEQ), 0) // GSIZE == iota((SEQ, SEQ), 1) // GSIZE
    same = jnp.where((diagonal(clus, SEQ) == clus) & group, 1.0 / GSIZE, 0.0)
    share_c = jnp.sum(same, axis=1, keepdims=True)
    share_r = jnp.sum(same, axis=0, keepdims=True)
    mean_r = jnp.sum(jnp.where(group, share_c, 0.0), axis=0, keepdims=True) * (1.0 / GSIZE)
    adv_r = (share_r - mean_r).astype(BF).astype(F32)
    rows = iota((SEQ * 8, SEQ), 0)
    dest_v = dest_r[...]
    hit = dest_v // SEQ == rows // 8
    what = jnp.where(rows % 8 < 4, (dest_v % SEQ).astype(F32), adv_r)
    meta[...] = jnp.broadcast_to(jnp.sum(jnp.where(hit, what, 0.0), axis=1, keepdims=True), (SEQ * 8, 128))


def remote(src, dst, ss, rs, who):
    return pltpu.make_async_remote_copy(
        src_ref=src, dst_ref=dst, send_sem=ss, recv_sem=rs, device_id=who, device_id_type=MESH)


class Ring:
    def __init__(self, own, dst, cols, z, ss, rs):
        self.own, self.dst, self.cols, self.z, self.ss, self.rs = own, dst, cols, z, ss, rs
        self.right, self.left, self.far = (lax.rem(z + d, N_Z) for d in (1, 3, 2))

    def copy(self, i, blk, src=None):
        half = (0, 1, 1, 0, 0, 1)[i]
        at = pl.ds(half * HALF, HALF)
        to = self.right if i % 2 == 0 else self.left
        src = self.own if src is None else src
        return remote(src.at[at, self.cols], self.dst.at[blk, at, self.cols], self.ss.at[i], self.rs.at[i], {"tp": to})

    def start(self):
        for i in range(4):
            self.copy(i, self.z).start()

    def hand_on(self):
        for i, blk in ((0, self.left), (1, self.right)):
            self.copy(i, blk).wait_recv()
            self.copy(i + 4, blk, self.source(blk)).start()

    def near(self):
        self.copy(2, self.left).wait_recv()
        self.copy(3, self.right).wait_recv()

    def end(self):
        self.copy(4, self.far).wait_recv()
        self.copy(5, self.far).wait_recv()

    def sent(self):
        for i in range(4):
            self.copy(i, self.z).wait_send()
        self.copy(4, self.left, self.source(self.left)).wait_send()
        self.copy(5, self.right, self.source(self.right)).wait_send()

    def source(self, blk):
        return self.dst.at[blk]


class Loop(Ring):
    def __init__(self, ref, k, to, ss, rs):
        self.ref, self.z, self.to, self.ss, self.rs = ref, k, to, ss, rs
        self.right, self.left, self.far = (lax.rem(k + d, 4) for d in (1, 3, 2))

    def copy(self, i, blk, src=None):
        at = self.ref(blk, (0, 1, 1, 0, 0, 1)[i])
        return remote(at, at, self.ss.at[i], self.rs.at[i], self.to(1 if i % 2 == 0 else 3))

    def source(self, blk):
        return None


def unstack(v):
    return jnp.concatenate([v[h * TB:(h + 1) * TB] for h in range(4)], axis=1)


def stack(v):
    return jnp.concatenate([v[:, h * HD:(h + 1) * HD] for h in range(4)], axis=0)


def turn(v, cos, sin):
    return v * cos + jnp.concatenate([v[:, HD // 2:], v[:, :HD // 2]], axis=1) * sin


def turn_back(v, cos, sin):
    return v * cos - jnp.concatenate([v[:, HD // 2:], v[:, :HD // 2]], axis=1) * sin


def whole_kernel(send_a, send_b, meta, cot, len_r, gain, table, w_q, w_k, w_v, w_o,
                 result, low_out, high_out,
                 arr, meta_in, xv, cv, wsh, wv, sq, sq_all, sqc, rope, pos_b, grads, outs, inv_b, adv_b, dots,
                 dots_all, rbuf, pair, r1, r2, s2, fin,
                 lsem, as_, ar, bs, br, ms, mr, zs, zr, us, ur, vs, vr, qs, qr,
                 w0s, w0r, w1s, w1r, w3s, w3r, w2s, w2r, w4s, w4r,
                 gs, gr, ds_, dr, ps, pr, s1s, s1r, hs, hr, s2s, s2r, fs, fr):
    packed = result
    me = lax.axis_index("fsdp")
    z = lax.axis_index("tp")
    y, x, c = me // 8, (me // 2) % 4, me % 2
    other = 1 - c
    sib = {"fsdp": y * 8 + x * 2 + other}

    def peer(o, s):
        return lax.rem(y + s * o[0] + 4, 4) * 8 + lax.rem(x + s * o[1] + 4, 4) * 2 + lax.rem(c + s * o[2] + 2, 2)

    def on_x(d):
        return {"fsdp": peer((0, d, 0), 1)}

    def on_y(d):
        return {"fsdp": peer((d, 0, 0), 1)}

    cot_own = pltpu.make_async_copy(cot, cv.at[z], lsem.at[0])
    cot_own.start()
    barrier = pltpu.get_barrier_semaphore()
    for o in OFFSETS:
        pl.semaphore_signal(barrier, inc=1, device_id={"fsdp": peer(o, 1)}, device_id_type=MESH)
    for d in (1, 2, 3):
        pl.semaphore_signal(barrier, inc=1, device_id={"tp": lax.rem(z + d, N_Z)}, device_id_type=MESH)
    pl.semaphore_wait(barrier, len(OFFSETS) + 3)

    ring_c = Ring(cot, cv, pl.ds(0, FB), z, zs, zr)
    ring_a = Ring(xv.at[z], xv, pl.ds(0, FA), z, us, ur)
    ring_b = Ring(xv.at[z], xv, pl.ds(FA, FB - FA), z, vs, vr)
    ring_c.start()

    def slab(k):
        return pl.ds(pl.multiple_of(k * SLAB, 16), SLAB)

    def eight(k):
        return pl.ds(pl.multiple_of(k * 8, 8), 8)

    def part_a(i, frm, to, who):
        return remote(send_a.at[slab(frm)], arr.at[slab(to), pl.ds(0, FA)], as_.at[i], ar.at[i], {"fsdp": who})

    def part_b(i, frm, to, who):
        return remote(send_b.at[slab(frm)], arr.at[slab(to), pl.ds(FA, FB - FA)], bs.at[i], br.at[i], {"fsdp": who})

    def note(i, frm, to, who):
        return remote(meta.at[eight(frm)], meta_in.at[eight(to)], ms.at[i], mr.at[i], {"fsdp": who})

    for kind in (note, part_a, part_b):
        for i, o in enumerate(OFFSETS):
            t = peer(o, 1)
            kind(i, t, me, t).start()
    mine = [pltpu.make_async_copy(send_a.at[slab(me)], arr.at[slab(me), pl.ds(0, FA)], lsem.at[1]),
            pltpu.make_async_copy(send_b.at[slab(me)], arr.at[slab(me), pl.ds(FA, FB - FA)], lsem.at[2]),
            pltpu.make_async_copy(meta.at[eight(me)], meta_in.at[eight(me)], lsem.at[3])]
    for k in mine:
        k.start()

    wsh[0, :, :QC] = w_q[...]
    wsh[0, :, QC:] = w_k[...]
    wsh[1, :, :KC] = w_v[...]
    wsh[1, :, KC:] = w_o[...]
    wv[0, y, x, c] = wsh[0]
    wv[1, y, x, c] = wsh[1]
    w_pair = remote(wsh.at[other], wv.at[other, y, x, c], w0s.at[0], w0r.at[0], sib)
    w_pair.start()

    def w_near(p, d):
        return remote(wv.at[c, y, x, p], wv.at[c, y, x, p], w1s.at[p, d - 1], w1r.at[p, d - 1], on_y(d) if p else on_x(d))

    loops = [Loop(lambda k, h: wv.at[c, k, pl.ds(2 * h, 2), 0], y, on_y, w2s, w2r),
             Loop(lambda k, h: wv.at[c, pl.ds(2 * h, 2), k, 1], x, on_x, w4s, w4r)]

    def w_last(d):
        if d < 3:
            blk = wv.at[c, lax.rem(y + d + 1, 4)]
        elif d < 6:
            blk = wv.at[c, y, lax.rem(x + d - 2, 4)]
        else:
            blk = wv.at[c, y, x, c]
        return remote(blk, blk, w3s.at[d], w3r.at[d], sib)

    hops = [(p, d) for d in (1, 2, 3) for p in (0, 1)]
    w_pair.wait_recv()
    for p, d in hops:
        w_near(p, d).start()

    lens = diagonal(len_r[...].astype(F32), SEQ)
    gain_own = gain[:, pl.ds(pl.multiple_of(z * FB, 128), FB)].astype(F32)
    lane = iota((SEQ, 128), 1)
    sub = iota((SEQ, 128), 0)
    ends = jnp.sum(jnp.where(sub <= lane, lens, 0.0), axis=0, keepdims=True)
    starts = jnp.sum(jnp.where(sub < lane, lens, 0.0), axis=0, keepdims=True)
    for i, o in enumerate(OFFSETS):
        note(i, peer(o, 1), peer(o, -1), peer(o, 1)).wait_recv()
    mine[2].wait()
    place = meta_in[pl.ds(0, SEQ, 8), :]
    share = meta_in[pl.ds(4, SEQ, 8), :]
    place_r = jnp.where(iota((1, 128), 1) < SEQ, jnp.sum(jnp.where(sub == lane, place, 0.0), axis=0, keepdims=True), -1.0)
    share_r = jnp.sum(jnp.where(sub == lane, share, 0.0), axis=0, keepdims=True)
    column = iota((SEQ, SEQ * SLAB), 1) - iota((SEQ, SEQ * SLAB), 0) * SLAB
    here = (column >= 0) & (column < SLAB)
    key = jnp.sum(jnp.where(here, place[:, :1] * 128.0 + column.astype(F32), 0.0), axis=0, keepdims=True)

    def packing(pick):
        def layout(b):
            at = pl.ds(b * TB, TB)
            i = (iota((TB, 128), 0) + b * TB).astype(F32)
            lane_f = iota((TB, 128), 1).astype(F32)
            hit = (i >= starts) & (i < ends)
            seg = jnp.sum(jnp.where(hit, lane_f, 0.0), axis=1, keepdims=True)
            pos = i - jnp.sum(jnp.where(hit, starts, 0.0), axis=1, keepdims=True)
            pos_b[at, :] = pos
            adv_b[at, :] = jnp.broadcast_to(
                jnp.sum(jnp.where(place_r == seg, share_r, 0.0), axis=1, keepdims=True), (TB, 128))
            rope[at, :] = lax.dot_general(
                jnp.where(pos == lane_f, 1.0, 0.0), table[...], (((1,), (0,)), ((), ())),
                precision=lax.Precision.HIGHEST, preferred_element_type=F32)
            pick[at, :] = jnp.where(seg * 128.0 + pos[:, :1] == key, 1.0, 0.0).astype(BF)

        for b in range(TOK // TB):
            layout(b)
        ring_c.hand_on()

        def pack(lo, hi):
            def rows(b, carry):
                at = pl.ds(pl.multiple_of(b * 256, 256), 256)
                took = nn(pick[at, :], arr[:, lo:hi])
                packed[at, lo:hi] = took.astype(BF)
                xv[z, at, lo:hi] = (took * gain_own[:, lo:hi]).astype(BF)
                square = took * took
                lanes = sum(square[:, k:k + 128] for k in range(0, hi - lo, 128))
                sqc[at, :] = lanes if lo == 0 else sqc[at, :] + lanes
                return carry

            lax.fori_loop(0, TOK // 256, rows, 0)

        for i, o in enumerate(OFFSETS):
            part_a(i, peer(o, 1), peer(o, -1), peer(o, 1)).wait_recv()
        mine[0].wait()
        pack(0, FA)
        ring_a.start()
        ring_c.near()
        ring_c.end()
        cot_own.wait()
        ring_a.hand_on()
        for i, o in enumerate(OFFSETS):
            part_b(i, peer(o, 1), peer(o, -1), peer(o, 1)).wait_recv()
        mine[1].wait()
        for p, d in hops:
            w_near(p, d).wait_recv()
        for loop in loops:
            loop.start()
        pack(FA, FB)
        ring_b.start()
    pl.run_scoped(packing, scratch((TOK, SEQ * SLAB)))
    for b in range(TOK // TB):
        square = jnp.sum(sqc[b * TB:(b + 1) * TB, :], axis=1, keepdims=True)
        sq[:, b * TB:(b + 1) * TB] = jnp.transpose(jnp.broadcast_to(square, (TB, 128)))[:8, :]

    def tell(d):
        return remote(sq, sq_all.at[d - 1], qs.at[d], qr.at[d], {"tp": lax.rem(z + d, N_Z)})

    for d in (1, 2, 3):
        tell(d).start()
    for loop in loops:
        loop.hand_on()
    ring_b.hand_on()
    ring_a.near()
    ring_a.end()
    for d in (1, 2, 3):
        tell(d).wait_recv()
    inv_t = lax.rsqrt((sq[...] + sq_all[0] + sq_all[1] + sq_all[2]) * (1.0 / D) + NORM_EPSILON)
    for b in range(TOK // TB):
        inv_b[b * TB:(b + 1) * TB, :] = jnp.transpose(jnp.broadcast_to(inv_t[:1, b * TB:(b + 1) * TB], (128, TB)))
    for loop in loops:
        loop.near()
        loop.end()
    for d in range(7):
        w_last(d).start()
    for d in range(7):
        w_last(d).wait_recv()

    def whole(h, blk):
        return wv[h, blk].reshape(FB, QC + KC)

    def attention(kbuf, vbuf, dk, dv, lin, ga, qrot, gab, mq):
        kbuf[:TB, :] = jnp.zeros((TB, HD), BF)
        vbuf[:TB, :] = jnp.zeros((TB, HD), BF)
        dk[...] = jnp.zeros_like(dk)
        dv[...] = jnp.zeros_like(dv)
        def project_c(d, carry):
            t = nn(cv[d], whole(1, d)[:, KC:])

            @pl.when(d == 0)
            def _():
                ga[...] = t

            @pl.when(d > 0)
            def _():
                ga[...] += t

            return carry

        lax.fori_loop(0, N_Z, project_c, 0)
        lin[...] = jnp.zeros_like(lin)

        def project_x(d, carry):
            blk = lax.rem(z + d, N_Z)
            lin[:, :QC + KC] += nn(xv[blk], whole(0, blk))
            lin[:, QC + KC:] += nn(xv[blk], whole(1, blk)[:, :KC])
            return carry

        project_x(0, 0)
        ring_b.near()
        lax.fori_loop(0, 2, lambda k, carry: project_x(1 + 2 * k, carry), 0)
        ring_b.end()
        project_x(2, 0)

        def ready(b, carry):
            at = pl.ds(pl.multiple_of(b * TB, TB), TB)
            up = pl.ds(pl.multiple_of(b * TB + TB, TB), TB)
            inv = inv_b[at, :]
            cos, sin = rope[at, :HD], rope[at, HD:]
            for h in range(4):
                qrot[at, h * HD:(h + 1) * HD] = turn(lin[at, h * HD:(h + 1) * HD] * inv, cos, sin).astype(BF)
                gab[at, h * HD:(h + 1) * HD] = (ga[at, h * HD:(h + 1) * HD] * adv_b[at, :]).astype(BF)
            kbuf[up, :] = turn(lin[at, QC:QC + KC] * inv, cos, sin).astype(BF)
            vbuf[up, :] = (lin[at, QC + KC:] * inv).astype(BF)
            return carry

        lax.fori_loop(0, TOK // TB, ready, 0)
        scale = HD ** (-0.5)

        def attend(b, carry):
            at = pl.ds(pl.multiple_of(b * TB, TB), TB)
            win = pl.ds(pl.multiple_of(b * TB, TB), 2 * TB)
            q = stack(qrot[at, :])
            g = stack(gab[at, :])
            k, v = kbuf[win, :], vbuf[win, :]
            back = iota((TB, 2 * TB), 0) + TB - iota((TB, 2 * TB), 1)
            ok = (back >= 0) & (back.astype(F32) <= pos_b[at, :1])
            ok = jnp.concatenate([ok] * 4, axis=0)
            s = jnp.where(ok, nt(q, k) * scale, -1e30)
            e = jnp.where(ok, jnp.exp(s - jnp.max(s, axis=1, keepdims=True)), 0.0)
            p = e / jnp.sum(e, axis=1, keepdims=True)
            pb = p.astype(BF)
            o = unstack(nn(pb, v))
            dp = nt(g, v)
            ds = (p * (dp - jnp.sum(p * dp, axis=1, keepdims=True)) * scale).astype(BF)
            dq = nn(ds, k)
            dk[win, :] += tn(ds, q)
            dv[win, :] += tn(pb, g)
            prod = dq * q.astype(F32)
            mq[at, :] = prod[:TB] + prod[TB:2 * TB] + prod[2 * TB:3 * TB] + prod[3 * TB:]
            dq = unstack(dq)
            inv = inv_b[at, :]
            cos, sin = rope[at, :HD], rope[at, HD:]
            for h in range(4):
                col = slice(h * HD, (h + 1) * HD)
                grads[at, col] = (turn_back(dq[:, col], cos, sin) * inv).astype(BF)
                outs[at, col] = (o[:, col] * adv_b[at, :]).astype(BF)
            return carry

        lax.fori_loop(0, TOK // TB, attend, 0, unroll=True)

        def finish(b, carry):
            at = pl.ds(pl.multiple_of(b * TB, TB), TB)
            up = pl.ds(pl.multiple_of(b * TB + TB, TB), TB)
            inv = inv_b[at, :]
            cos, sin = rope[at, :HD], rope[at, HD:]
            gk, gv = dk[up, :], dv[up, :]
            grads[at, QC:QC + KC] = (turn_back(gk, cos, sin) * inv).astype(BF)
            grads[at, QC + KC:] = (gv * inv).astype(BF)
            m = mq[at, :] + gk * kbuf[up, :].astype(F32) + gv * vbuf[up, :].astype(F32)
            m = jnp.sum(m, axis=1, keepdims=True) * inv
            dots[:, at] = jnp.transpose(jnp.broadcast_to(m, (TB, 128)))[:8, :]
            return carry

        lax.fori_loop(0, TOK // TB, finish, 0)
    v = scratch
    pl.run_scoped(attention, v((TOK + TB, HD)), v((TOK + TB, HD)), v((TOK + TB, HD), F32), v((TOK + TB, HD), F32),
                  v((TOK, WIDTH), F32), v((TOK, QC), F32), v((TOK, QC)), v((TOK, QC)), v((TOK, HD), F32))
    ring_c.sent()
    right, left, far = lax.rem(z + 1, N_Z), lax.rem(z + 3, N_Z), lax.rem(z + 2, N_Z)
    order = [far, right, left, z]

    def gradients(dw, s1):
        def dot_note(d):
            return remote(dots, dots_all.at[d - 1], ds_.at[d], dr.at[d], {"tp": lax.rem(z + d, N_Z)})

        for d in (1, 2, 3):
            dot_note(d).start()

        def ship(i):
            return remote(arr.at[pl.ds(i * HALF, HALF)], rbuf.at[i], gs.at[i], gr.at[i], {"tp": right if i % 2 == 0 else left})

        def share(i, h):
            at = slice(h * HALF, (h + 1) * HALF)
            return nt(grads[at, :QC + KC], whole(0, order[i])) + nt(grads[at, QC + KC:], whole(1, order[i])[:, :KC])

        def first(i, w, h):
            arr[i * HALF:(i + 1) * HALF, :] = share(w, h).astype(BF)
            ship(i).start()

        first(0, 0, 0)
        first(1, 0, 1)
        def swap(i):
            b = lax.rem(y + 1 + i, 4)
            return remote(dw.at[other, b], pair.at[b], ps.at[i], pr.at[i], sib)

        def terms(i, carry):
            b = lax.rem(y + 1 + i, 4)
            def place(h, cols, v):
                for j in range(8):
                    dw[h, b, j // 2, j % 2, :, cols] = v[112 * j:112 * (j + 1)]

            place(0, slice(0, QC), tn(xv[b], grads[:, :QC]).astype(BF))
            t = tn(xv[b], grads[:, QC:]).astype(BF)
            place(0, slice(QC, QC + KC), t[:, :KC])
            place(1, slice(0, KC), t[:, KC:])
            place(1, slice(KC, QC + KC), tn(cv[b], outs[...]).astype(BF))
            swap(i).start()
            return carry

        def hop_y(d):
            return remote(dw.at[c, lax.rem(y + d, 4), :, 1], r1.at[1, d - 1], s1s.at[1, d - 1], s1r.at[1, d - 1], on_y(d))

        def hop_x(i, d):
            b = lax.rem(y + 1 + i, 4)
            return remote(dw.at[c, b, lax.rem(x + d, 4), 0], r1.at[0, d - 1, b], hs.at[i, d - 1], hr.at[i, d - 1], on_x(d))

        def chip_sum(i, carry):
            b = lax.rem(y + 1 + i, 4)
            swap(i).wait_recv()
            for j in range(4):
                dw[c, b, j] = (dw[c, b, j].astype(F32) + pair[b, j].astype(F32)).astype(BF)

            def along_y():
                hop_y(i + 1).start()

            if not isinstance(i, int):
                pl.when(i < 3)(along_y)

            for d in (1, 2, 3):
                hop_x(i, d).start()

        def step(i, carry):
            terms(i, carry)

            @pl.when(i > 0)
            def _():
                chip_sum(i - 1, carry)

            return carry

        lax.fori_loop(0, 2, step, 0)
        first(2, 1, 1)
        first(3, 2, 0)
        lax.fori_loop(2, 4, step, 0)
        chip_sum(3, 0)
        for i, w in ((4, 1), (5, 2)):
            a = share(w, i % 2)
            ship(i - 4).wait_recv()
            arr[i * HALF:(i + 1) * HALF, :] = (a + rbuf[i - 4].astype(F32)).astype(BF)
            ship(i).start()
        for h in range(2):
            cv[right, h * HALF:(h + 1) * HALF, :] = share(3, h).astype(BF)
        for d in (1, 2, 3):
            dot_note(d).wait()
        m = (dots[...] + dots_all[0] + dots_all[1] + dots_all[2]) * (1.0 / D)

        for d in (1, 2, 3):
            hop_y(d).wait_recv()
            for i in range(4):
                hop_x(i, d).wait_recv()
        for j in range(4):
            s1[1, j] = (dw[c, y, j, 1].astype(F32) + r1[1, 0, j].astype(F32) + r1[1, 1, j].astype(F32)
                        + r1[1, 2, j].astype(F32)).astype(BF)
            s1[0, j] = (dw[c, j, x, 0].astype(F32) + r1[0, 0, j].astype(F32) + r1[0, 1, j].astype(F32)
                        + r1[0, 2, j].astype(F32)).astype(BF)

        def last_x(d):
            return remote(s1.at[1, lax.rem(x + d, 4)], r2.at[1, d - 1], s2s.at[1, d - 1], s2r.at[1, d - 1], on_x(d))

        def last_y(d):
            return remote(s1.at[0, lax.rem(y + d, 4)], r2.at[0, d - 1], s2s.at[0, d - 1], s2r.at[0, d - 1], on_y(d))

        for d in (1, 2, 3):
            last_x(d).start()
            last_y(d).start()
        for d in (1, 2, 3):
            last_x(d).wait_recv()
            last_y(d).wait_recv()
        for p, own in ((0, s1[0, y]), (1, s1[1, x])):
            s2[p] = (own.astype(F32) + r2[p, 0].astype(F32) + r2[p, 1].astype(F32) + r2[p, 2].astype(F32)).astype(BF)
        trade = remote(s2.at[other], fin.at[c], fs.at[0], fr.at[0], sib)
        trade.start()
        for i in (2, 3, 4, 5):
            ship(i).wait_recv()
        gain_own = gain[:, pl.ds(pl.multiple_of(z * FB, 128), FB)].astype(F32)
        for b in range(TOK // TB):
            h, r = divmod(b * TB, HALF)
            at = slice(b * TB, (b + 1) * TB)
            rows = slice(r, r + TB)
            one, two = (4, 3) if h == 0 else (2, 5)
            s = cv[right, at, :].astype(F32) + rbuf[one, rows, :].astype(F32) + rbuf[two, rows, :].astype(F32)
            mc = jnp.transpose(jnp.broadcast_to(m[:1, at], (128, TB)))[:, :1]
            inv = inv_b[at, :1]
            result[at, :] = (adv_b[at, :1] * cv[z, at, :].astype(F32) + s * gain_own
                             - packed[at, :].astype(F32) * (inv * mc)).astype(BF)
        trade.wait()
        mine = s2[c]
        got = fin[other]
        low_out[...] = jnp.where(c == 0, mine, got)
        high_out[...] = jnp.where(c == 0, got, mine)
        for i in range(6):
            ship(i).wait_send()
        for i in range(4):
            swap(i).wait_send()
        for d in (1, 2, 3):
            for i in range(4):
                hop_x(i, d).wait_send()
            hop_y(d).wait_send()
            last_x(d).wait_send()
            last_y(d).wait_send()

    pl.run_scoped(gradients, v((2, 4, 4, 2) + PART), v((2, 4) + PART))
    ring_a.sent()
    ring_b.sent()
    for kind in (note, part_a, part_b):
        for i, o in enumerate(OFFSETS):
            t = peer(o, 1)
            kind(i, t, me, t).wait_send()
    w_pair.wait_send()
    for p, d in hops:
        w_near(p, d).wait_send()
    for loop in loops:
        loop.sent()
    for d in range(7):
        w_last(d).wait_send()
    for d in (1, 2, 3):
        tell(d).wait_send()


def split_kernel(result, low, high, res, res_q, res_k, res_v, res_o):
    res[...] = result[...]
    res_q[...] = low[:, :QC]
    res_k[...] = low[:, QC:]
    res_v[...] = high[:, :KC]
    res_o[...] = high[:, KC:]


def sds(shape, dtype=BF):
    return jax.ShapeDtypeStruct(shape, dtype)


def params(**kw):
    return pltpu.CompilerParams(vmem_limit_bytes=LIMIT, has_side_effects=True, **kw)


def rope_table():
    i = np.arange(HD // 2, dtype=np.float32)
    frequency = np.float32(ROPE_BASE) ** (-(np.float32(2.0) * i) / np.float32(HD))
    angle = np.arange(128, dtype=np.float32)[:, None] * frequency[None, :]
    c, s = np.cos(angle), np.sin(angle)
    return np.concatenate([c, c, -s, s], axis=1).astype(np.float32)


N_O = len(OFFSETS)
WIDTH = QC + 2 * KC
PART = (112, QC + KC)


def scratch(shape, dtype=BF):
    return pltpu.VMEM(shape, dtype)


def stage(*args):
    return pl.pallas_call(
        stage_kernel, out_shape=(sds((SEQ * SLAB, FA)), sds((SEQ * SLAB, FB - FA)), sds((SEQ * 8, 128), F32)),
        in_specs=[SMEM, VMEM, VMEM, VMEM], out_specs=(VMEM,) * 3, compiler_params=params(),
    )(*args)


def whole(*args):
    v = scratch
    ring = [DMA((6,)), DMA((6,))]
    return pl.pallas_call(
        whole_kernel, out_shape=(sds((TOK, FB)), sds(PART), sds(PART)),
        in_specs=[HBM] * 4 + [VMEM] * 7, out_specs=(VMEM,) * 3,
        scratch_shapes=[
            v((SEQ * SLAB, FB)), v((SEQ * 8, 128), F32),
            v((N_Z, TOK, FB)), v((N_Z, TOK, FB)), v((2,) + PART), v((2, 4, 4, 2) + PART),
            v((8, TOK), F32), v((3, 8, TOK), F32), v((TOK, 128), F32), v((TOK, 2 * HD), F32), v((TOK, 128), F32),
            v((TOK, WIDTH)), v((TOK, QC)), v((TOK, 128), F32), v((TOK, 128), F32), v((8, TOK), F32),
            v((3, 8, TOK), F32), v((6, HALF, FB)), v((4, 4, 2) + PART), v((2, 3, 4) + PART), v((2, 3) + PART),
            v((2,) + PART), v((2,) + PART),
            DMA((4,))] + [DMA((N_O,))] * 6 + ring * 3 + [DMA((4,)), DMA((4,)), DMA((1,)), DMA((1,))]
        + [DMA((2, 3))] * 2 + [DMA((7,))] * 2 + ring * 2
        + ring + [DMA((4,))] * 4 + [DMA((2, 3))] * 2 + [DMA((4, 3))] * 2 + [DMA((2, 3))] * 2 + [DMA((1,))] * 2,
        compiler_params=params(collective_id=0),
    )(*args)


def split(*args):
    return pl.pallas_call(
        split_kernel,
        out_shape=(sds((TOK, FB)), sds((112, QC)), sds((112, KC)), sds((112, KC)), sds((112, QC))),
        in_specs=[VMEM] * 3, out_specs=(VMEM,) * 5, compiler_params=params(),
    )(*args)


def per_device(roll_rows, dest, lengths, clusters, log_prob_grad, gain, w_q, w_k, w_v, w_o_t):
    gain = gain.reshape(1, D)
    send_a, send_b, meta = stage(dest, dest.reshape(1, SEQ), clusters.reshape(1, SEQ), roll_rows)
    return split(*whole(
        send_a, send_b, meta, log_prob_grad, lengths, gain, jnp.asarray(rope_table()), w_q, w_k, w_v, w_o_t))


def solution(mesh):
    in_specs = (
        P("fsdp", None, "tp"), P("fsdp"), P("fsdp", None), P("fsdp"), P("fsdp", "tp"), P(),
        P("fsdp", "tp"), P("fsdp", "tp"), P("fsdp", "tp"), P("fsdp", "tp"),
    )
    out_specs = (P("fsdp", "tp"),) * 5
    return jax.shard_map(per_device, mesh=mesh, in_specs=in_specs, out_specs=out_specs, check_vma=False)
```

```python
import jax
import jax.numpy as jnp
import numpy as np
from jax import lax
from jax.experimental import pallas as pl
from jax.experimental.pallas import tpu as pltpu
from jax.sharding import PartitionSpec as P

HD = 128
GSIZE = 16
ROPE_BASE = 1000000.0
NORM_EPSILON = 1e-06
MESH = pl.DeviceIdType.MESH
BF = jnp.bfloat16
F32 = jnp.float32
HBM = pl.BlockSpec(memory_space=pl.ANY)
VMEM = pl.BlockSpec(memory_space=pltpu.VMEM)
SMEM = pl.BlockSpec(memory_space=pltpu.SMEM)
DMA = pltpu.SemaphoreType.DMA
LIMIT = 60 * 2**20

N_F = 32
N_Z = 4
SEQ = 32
MAXLEN = 72
TOK = 768
HALF = TOK // 2
FB = 896
FA = 512
SLAB = 80
D = 3584
QC = 512
KC = 128
TB = 128

CHIPS = [(0, 1), (1, 0), (0, 3), (3, 0), (1, 1), (3, 3), (1, 3), (3, 1),
         (0, 2), (2, 0), (1, 2), (2, 1), (3, 2), (2, 3), (2, 2)]
OFFSETS = [(0, 0, 1)] + [(a, b, c) for c in range(2) for a, b in CHIPS]


def nt(a, b):
    return lax.dot_general(a, b, (((1,), (1,)), ((), ())), preferred_element_type=F32)


def tn(a, b):
    return lax.dot_general(a, b, (((0,), (0,)), ((), ())), preferred_element_type=F32)


def nn(a, b):
    return lax.dot_general(a, b, (((1,), (0,)), ((), ())), preferred_element_type=F32)


def iota(shape, dim):
    return lax.broadcasted_iota(jnp.int32, shape, dim)


def diagonal(row, n):
    return jnp.sum(jnp.where(iota((n, n), 0) == iota((n, n), 1), row, 0.0), axis=1, keepdims=True)


def stage_kernel(dest_s, dest_r, clus_r, roll, send_a, send_b, meta):
    def place(s, c):
        at = pl.ds(pl.multiple_of((dest_s[s] // SEQ) * SLAB, 16), SLAB)
        v = jnp.concatenate([roll[s], jnp.zeros((SLAB - MAXLEN, FB), BF)], axis=0)
        send_a[at, :] = v[:, :FA]
        send_b[at, :] = v[:, FA:]
        return c

    lax.fori_loop(0, SEQ, place, 0)
    clus = clus_r[...].astype(F32)
    group = iota((SEQ, SEQ), 0) // GSIZE == iota((SEQ, SEQ), 1) // GSIZE
    same = jnp.where((diagonal(clus, SEQ) == clus) & group, 1.0 / GSIZE, 0.0)
    share_c = jnp.sum(same, axis=1, keepdims=True)
    share_r = jnp.sum(same, axis=0, keepdims=True)
    mean_r = jnp.sum(jnp.where(group, share_c, 0.0), axis=0, keepdims=True) * (1.0 / GSIZE)
    adv_r = (share_r - mean_r).astype(BF).astype(F32)
    rows = iota((SEQ * 8, SEQ), 0)
    dest_v = dest_r[...]
    hit = dest_v // SEQ == rows // 8
    what = jnp.where(rows % 8 < 4, (dest_v % SEQ).astype(F32), adv_r)
    meta[...] = jnp.broadcast_to(jnp.sum(jnp.where(hit, what, 0.0), axis=1, keepdims=True), (SEQ * 8, 128))


def remote(src, dst, ss, rs, who):
    return pltpu.make_async_remote_copy(
        src_ref=src, dst_ref=dst, send_sem=ss, recv_sem=rs, device_id=who, device_id_type=MESH)


class Ring:
    def __init__(self, own, dst, cols, z, ss, rs):
        self.own, self.dst, self.cols, self.z, self.ss, self.rs = own, dst, cols, z, ss, rs
        self.right, self.left, self.far = (lax.rem(z + d, N_Z) for d in (1, 3, 2))

    def copy(self, i, blk, src=None):
        half = (0, 1, 1, 0, 0, 1)[i]
        at = pl.ds(half * HALF, HALF)
        to = self.right if i % 2 == 0 else self.left
        src = self.own if src is None else src
        return remote(src.at[at, self.cols], self.dst.at[blk, at, self.cols], self.ss.at[i], self.rs.at[i], {"tp": to})

    def start(self):
        for i in range(4):
            self.copy(i, self.z).start()

    def hand_on(self):
        for i, blk in ((0, self.left), (1, self.right)):
            self.copy(i, blk).wait_recv()
            self.copy(i + 4, blk, self.source(blk)).start()

    def near(self):
        self.copy(2, self.left).wait_recv()
        self.copy(3, self.right).wait_recv()

    def end(self):
        self.copy(4, self.far).wait_recv()
        self.copy(5, self.far).wait_recv()

    def sent(self):
        for i in range(4):
            self.copy(i, self.z).wait_send()
        self.copy(4, self.left, self.source(self.left)).wait_send()
        self.copy(5, self.right, self.source(self.right)).wait_send()

    def source(self, blk):
        return self.dst.at[blk]


class Loop(Ring):
    def __init__(self, ref, k, to, ss, rs):
        self.ref, self.z, self.to, self.ss, self.rs = ref, k, to, ss, rs
        self.right, self.left, self.far = (lax.rem(k + d, 4) for d in (1, 3, 2))

    def copy(self, i, blk, src=None):
        at = self.ref(blk, (0, 1, 1, 0, 0, 1)[i])
        return remote(at, at, self.ss.at[i], self.rs.at[i], self.to(1 if i % 2 == 0 else 3))

    def source(self, blk):
        return None


def unstack(v):
    return jnp.concatenate([v[h * TB:(h + 1) * TB] for h in range(4)], axis=1)


def stack(v):
    return jnp.concatenate([v[:, h * HD:(h + 1) * HD] for h in range(4)], axis=0)


def turn(v, cos, sin):
    return v * cos + jnp.concatenate([v[:, HD // 2:], v[:, :HD // 2]], axis=1) * sin


def turn_back(v, cos, sin):
    return v * cos - jnp.concatenate([v[:, HD // 2:], v[:, :HD // 2]], axis=1) * sin


def whole_kernel(send_a, send_b, meta, cot, len_r, gain, table, w_q, w_k, w_v, w_o,
                 result, low_out, high_out,
                 arr, meta_in, xv, cv, wsh, wv, sq, sq_all, sqc, rope, pos_b, grads, outs, inv_b, adv_b, dots,
                 dots_all, rbuf, pair, r1, r2, s2, fin,
                 lsem, as_, ar, bs, br, ms, mr, zs, zr, us, ur, vs, vr, qs, qr,
                 w0s, w0r, w1s, w1r, w3s, w3r, w2s, w2r, w4s, w4r,
                 gs, gr, ds_, dr, ps, pr, s1s, s1r, hs, hr, s2s, s2r, fs, fr):
    packed = result
    me = lax.axis_index("fsdp")
    z = lax.axis_index("tp")
    y, x, c = me // 8, (me // 2) % 4, me % 2
    other = 1 - c
    sib = {"fsdp": y * 8 + x * 2 + other}

    def peer(o, s):
        return lax.rem(y + s * o[0] + 4, 4) * 8 + lax.rem(x + s * o[1] + 4, 4) * 2 + lax.rem(c + s * o[2] + 2, 2)

    def on_x(d):
        return {"fsdp": peer((0, d, 0), 1)}

    def on_y(d):
        return {"fsdp": peer((d, 0, 0), 1)}

    cot_own = pltpu.make_async_copy(cot, cv.at[z], lsem.at[0])
    cot_own.start()
    barrier = pltpu.get_barrier_semaphore()
    for o in OFFSETS:
        pl.semaphore_signal(barrier, inc=1, device_id={"fsdp": peer(o, 1)}, device_id_type=MESH)
    for d in (1, 2, 3):
        pl.semaphore_signal(barrier, inc=1, device_id={"tp": lax.rem(z + d, N_Z)}, device_id_type=MESH)
    pl.semaphore_wait(barrier, len(OFFSETS) + 3)

    def own_gain():
        g = gain[...].astype(F32).reshape(1, D)
        return sum(jnp.where(z == k, g[:, k * FB:(k + 1) * FB], 0.0) for k in range(N_Z))

    ring_c = Ring(cot, cv, pl.ds(0, FB), z, zs, zr)
    ring_a = Ring(xv.at[z], xv, pl.ds(0, FA), z, us, ur)
    ring_b = Ring(xv.at[z], xv, pl.ds(FA, FB - FA), z, vs, vr)
    ring_c.start()

    def slab(k):
        return pl.ds(pl.multiple_of(k * SLAB, 16), SLAB)

    def eight(k):
        return pl.ds(pl.multiple_of(k * 8, 8), 8)

    def part_a(i, frm, to, who):
        return remote(send_a.at[slab(frm)], arr.at[slab(to), pl.ds(0, FA)], as_.at[i], ar.at[i], {"fsdp": who})

    def part_b(i, frm, to, who):
        return remote(send_b.at[slab(frm)], arr.at[slab(to), pl.ds(FA, FB - FA)], bs.at[i], br.at[i], {"fsdp": who})

    def note(i, frm, to, who):
        return remote(meta.at[eight(frm)], meta_in.at[eight(to)], ms.at[i], mr.at[i], {"fsdp": who})

    for kind in (note, part_a, part_b):
        for i, o in enumerate(OFFSETS):
            t = peer(o, 1)
            kind(i, t, me, t).start()
    mine = [pltpu.make_async_copy(send_a.at[slab(me)], arr.at[slab(me), pl.ds(0, FA)], lsem.at[1]),
            pltpu.make_async_copy(send_b.at[slab(me)], arr.at[slab(me), pl.ds(FA, FB - FA)], lsem.at[2]),
            pltpu.make_async_copy(meta.at[eight(me)], meta_in.at[eight(me)], lsem.at[3])]
    for k in mine:
        k.start()

    wsh[0, :, :QC] = w_q[...]
    wsh[0, :, QC:] = w_k[...]
    wsh[1, :, :KC] = w_v[...]
    wsh[1, :, KC:] = w_o[...]
    wv[0, y, x, c] = wsh[0]
    wv[1, y, x, c] = wsh[1]
    w_pair = remote(wsh.at[other], wv.at[other, y, x, c], w0s.at[0], w0r.at[0], sib)
    w_pair.start()

    def w_near(p, d):
        return remote(wv.at[c, y, x, p], wv.at[c, y, x, p], w1s.at[p, d - 1], w1r.at[p, d - 1], on_y(d) if p else on_x(d))

    loops = [Loop(lambda k, h: wv.at[c, k, pl.ds(2 * h, 2), 0], y, on_y, w2s, w2r),
             Loop(lambda k, h: wv.at[c, pl.ds(2 * h, 2), k, 1], x, on_x, w4s, w4r)]

    def w_last(d):
        if d < 3:
            blk = wv.at[c, lax.rem(y + d + 1, 4)]
        elif d < 6:
            blk = wv.at[c, y, lax.rem(x + d - 2, 4)]
        else:
            blk = wv.at[c, y, x, c]
        return remote(blk, blk, w3s.at[d], w3r.at[d], sib)

    hops = [(p, d) for d in (1, 2, 3) for p in (0, 1)]
    w_pair.wait_recv()
    for p, d in hops:
        w_near(p, d).start()

    lens = diagonal(len_r[...].astype(F32), SEQ)
    gain_own = own_gain()
    lane = iota((SEQ, 128), 1)
    sub = iota((SEQ, 128), 0)
    ends = jnp.sum(jnp.where(sub <= lane, lens, 0.0), axis=0, keepdims=True)
    starts = jnp.sum(jnp.where(sub < lane, lens, 0.0), axis=0, keepdims=True)
    for i, o in enumerate(OFFSETS):
        note(i, peer(o, 1), peer(o, -1), peer(o, 1)).wait_recv()
    mine[2].wait()
    place = meta_in[pl.ds(0, SEQ, 8), :]
    share = meta_in[pl.ds(4, SEQ, 8), :]
    place_r = jnp.where(iota((1, 128), 1) < SEQ, jnp.sum(jnp.where(sub == lane, place, 0.0), axis=0, keepdims=True), -1.0)
    share_r = jnp.sum(jnp.where(sub == lane, share, 0.0), axis=0, keepdims=True)
    column = iota((SEQ, SEQ * SLAB), 1) - iota((SEQ, SEQ * SLAB), 0) * SLAB
    here = (column >= 0) & (column < SLAB)
    key = jnp.sum(jnp.where(here, place[:, :1] * 128.0 + column.astype(F32), 0.0), axis=0, keepdims=True)

    def packing(pick):
        def layout(b):
            at = pl.ds(b * TB, TB)
            i = (iota((TB, 128), 0) + b * TB).astype(F32)
            lane_f = iota((TB, 128), 1).astype(F32)
            hit = (i >= starts) & (i < ends)
            seg = jnp.sum(jnp.where(hit, lane_f, 0.0), axis=1, keepdims=True)
            pos = i - jnp.sum(jnp.where(hit, starts, 0.0), axis=1, keepdims=True)
            pos_b[at, :] = pos
            adv_b[at, :] = jnp.broadcast_to(
                jnp.sum(jnp.where(place_r == seg, share_r, 0.0), axis=1, keepdims=True), (TB, 128))
            rope[at, :] = lax.dot_general(
                jnp.where(pos == lane_f, 1.0, 0.0), table[...], (((1,), (0,)), ((), ())),
                precision=lax.Precision.HIGHEST, preferred_element_type=F32)
            pick[at, :] = jnp.where(seg * 128.0 + pos[:, :1] == key, 1.0, 0.0).astype(BF)

        for b in range(TOK // TB):
            layout(b)
        ring_c.hand_on()

        def pack(lo, hi):
            def rows(b, carry):
                at = pl.ds(pl.multiple_of(b * 256, 256), 256)
                took = nn(pick[at, :], arr[:, lo:hi])
                packed[at, lo:hi] = took.astype(BF)
                xv[z, at, lo:hi] = (took * gain_own[:, lo:hi]).astype(BF)
                square = took * took
                lanes = sum(square[:, k:k + 128] for k in range(0, hi - lo, 128))
                sqc[at, :] = lanes if lo == 0 else sqc[at, :] + lanes
                return carry

            lax.fori_loop(0, TOK // 256, rows, 0)

        for i, o in enumerate(OFFSETS):
            part_a(i, peer(o, 1), peer(o, -1), peer(o, 1)).wait_recv()
        mine[0].wait()
        pack(0, FA)
        ring_a.start()
        ring_c.near()
        ring_c.end()
        cot_own.wait()
        ring_a.hand_on()
        for i, o in enumerate(OFFSETS):
            part_b(i, peer(o, 1), peer(o, -1), peer(o, 1)).wait_recv()
        mine[1].wait()
        for p, d in hops:
            w_near(p, d).wait_recv()
        for loop in loops:
            loop.start()
        pack(FA, FB)
        ring_b.start()
    pl.run_scoped(packing, scratch((TOK, SEQ * SLAB)))
    for b in range(TOK // TB):
        square = jnp.sum(sqc[b * TB:(b + 1) * TB, :], axis=1, keepdims=True)
        sq[:, b * TB:(b + 1) * TB] = jnp.transpose(jnp.broadcast_to(square, (TB, 128)))[:8, :]

    def tell(d):
        return remote(sq, sq_all.at[d - 1], qs.at[d], qr.at[d], {"tp": lax.rem(z + d, N_Z)})

    for d in (1, 2, 3):
        tell(d).start()
    for loop in loops:
        loop.hand_on()
    ring_b.hand_on()
    ring_a.near()
    ring_a.end()
    for d in (1, 2, 3):
        tell(d).wait_recv()
    inv_t = lax.rsqrt((sq[...] + sq_all[0] + sq_all[1] + sq_all[2]) * (1.0 / D) + NORM_EPSILON)
    for b in range(TOK // TB):
        inv_b[b * TB:(b + 1) * TB, :] = jnp.transpose(jnp.broadcast_to(inv_t[:1, b * TB:(b + 1) * TB], (128, TB)))
    for loop in loops:
        loop.near()
        loop.end()
    for d in range(7):
        w_last(d).start()
    for kind in (note, part_a, part_b):
        for i, o in enumerate(OFFSETS):
            t = peer(o, 1)
            kind(i, t, me, t).wait_send()
    w_pair.wait_send()
    for p, d in hops:
        w_near(p, d).wait_send()
    for d in range(7):
        w_last(d).wait_recv()

    def whole(h, blk):
        return wv[h, blk].reshape(FB, QC + KC)

    def attention(kbuf, vbuf, dk, dv, lin, ga, qrot, gab, mq):
        kbuf[:TB, :] = jnp.zeros((TB, HD), BF)
        vbuf[:TB, :] = jnp.zeros((TB, HD), BF)
        dk[...] = jnp.zeros_like(dk)
        dv[...] = jnp.zeros_like(dv)
        def project_c(d, carry):
            t = nn(cv[d], whole(1, d)[:, KC:])

            @pl.when(d == 0)
            def _():
                ga[...] = t

            @pl.when(d > 0)
            def _():
                ga[...] += t

            return carry

        lax.fori_loop(0, N_Z, project_c, 0)
        lin[...] = jnp.zeros_like(lin)

        def project_x(d, carry):
            blk = lax.rem(z + d, N_Z)
            lin[:, :QC + KC] += nn(xv[blk], whole(0, blk))
            lin[:, QC + KC:] += nn(xv[blk], whole(1, blk)[:, :KC])
            return carry

        project_x(0, 0)
        ring_b.near()
        lax.fori_loop(0, 2, lambda k, carry: project_x(1 + 2 * k, carry), 0)
        ring_b.end()
        project_x(2, 0)

        def ready(b, carry):
            at = pl.ds(pl.multiple_of(b * TB, TB), TB)
            up = pl.ds(pl.multiple_of(b * TB + TB, TB), TB)
            inv = inv_b[at, :]
            cos, sin = rope[at, :HD], rope[at, HD:]
            for h in range(4):
                qrot[at, h * HD:(h + 1) * HD] = turn(lin[at, h * HD:(h + 1) * HD] * inv, cos, sin).astype(BF)
                gab[at, h * HD:(h + 1) * HD] = (ga[at, h * HD:(h + 1) * HD] * adv_b[at, :]).astype(BF)
            kbuf[up, :] = turn(lin[at, QC:QC + KC] * inv, cos, sin).astype(BF)
            vbuf[up, :] = (lin[at, QC + KC:] * inv).astype(BF)
            return carry

        lax.fori_loop(0, TOK // TB, ready, 0)
        scale = HD ** (-0.5)

        def attend(b, carry):
            at = pl.ds(pl.multiple_of(b * TB, TB), TB)
            win = pl.ds(pl.multiple_of(b * TB, TB), 2 * TB)
            q = stack(qrot[at, :])
            g = stack(gab[at, :])
            k, v = kbuf[win, :], vbuf[win, :]
            back = iota((TB, 2 * TB), 0) + TB - iota((TB, 2 * TB), 1)
            ok = (back >= 0) & (back.astype(F32) <= pos_b[at, :1])
            ok = jnp.concatenate([ok] * 4, axis=0)
            s = jnp.where(ok, nt(q, k) * scale, -1e30)
            e = jnp.where(ok, jnp.exp(s - jnp.max(s, axis=1, keepdims=True)), 0.0)
            p = e / jnp.sum(e, axis=1, keepdims=True)
            pb = p.astype(BF)
            o = unstack(nn(pb, v))
            dp = nt(g, v)
            ds = (p * (dp - jnp.sum(p * dp, axis=1, keepdims=True)) * scale).astype(BF)
            dq = nn(ds, k)
            dk[win, :] += tn(ds, q)
            dv[win, :] += tn(pb, g)
            prod = dq * q.astype(F32)
            mq[at, :] = prod[:TB] + prod[TB:2 * TB] + prod[2 * TB:3 * TB] + prod[3 * TB:]
            dq = unstack(dq)
            inv = inv_b[at, :]
            cos, sin = rope[at, :HD], rope[at, HD:]
            for h in range(4):
                col = slice(h * HD, (h + 1) * HD)
                grads[at, col] = (turn_back(dq[:, col], cos, sin) * inv).astype(BF)
                outs[at, col] = (o[:, col] * adv_b[at, :]).astype(BF)
            return carry

        lax.fori_loop(0, TOK // TB, attend, 0, unroll=True)

        def finish(b, carry):
            at = pl.ds(pl.multiple_of(b * TB, TB), TB)
            up = pl.ds(pl.multiple_of(b * TB + TB, TB), TB)
            inv = inv_b[at, :]
            cos, sin = rope[at, :HD], rope[at, HD:]
            gk, gv = dk[up, :], dv[up, :]
            grads[at, QC:QC + KC] = (turn_back(gk, cos, sin) * inv).astype(BF)
            grads[at, QC + KC:] = (gv * inv).astype(BF)
            m = mq[at, :] + gk * kbuf[up, :].astype(F32) + gv * vbuf[up, :].astype(F32)
            m = jnp.sum(m, axis=1, keepdims=True) * inv
            dots[:, at] = jnp.transpose(jnp.broadcast_to(m, (TB, 128)))[:8, :]
            return carry

        lax.fori_loop(0, TOK // TB, finish, 0)
    v = scratch
    pl.run_scoped(attention, v((TOK + TB, HD)), v((TOK + TB, HD)), v((TOK + TB, HD), F32), v((TOK + TB, HD), F32),
                  v((TOK, WIDTH), F32), v((TOK, QC), F32), v((TOK, QC)), v((TOK, QC)), v((TOK, HD), F32))
    ring_c.sent()
    right, left, far = lax.rem(z + 1, N_Z), lax.rem(z + 3, N_Z), lax.rem(z + 2, N_Z)
    order = [far, right, left, z]

    def gradients(dw, s1):
        def dot_note(d):
            return remote(dots, dots_all.at[d - 1], ds_.at[d], dr.at[d], {"tp": lax.rem(z + d, N_Z)})

        for d in (1, 2, 3):
            dot_note(d).start()

        def ship(i):
            return remote(arr.at[pl.ds(i * HALF, HALF)], rbuf.at[i], gs.at[i], gr.at[i], {"tp": right if i % 2 == 0 else left})

        def share(i, h):
            at = slice(h * HALF, (h + 1) * HALF)
            return nt(grads[at, :QC + KC], whole(0, order[i])) + nt(grads[at, QC + KC:], whole(1, order[i])[:, :KC])

        def first(i, w, h):
            arr[i * HALF:(i + 1) * HALF, :] = share(w, h).astype(BF)
            ship(i).start()

        first(0, 0, 0)
        first(1, 0, 1)
        def swap(i):
            b = lax.rem(y + 1 + i, 4)
            return remote(dw.at[other, b], pair.at[b], ps.at[i], pr.at[i], sib)

        def terms(i, carry):
            b = lax.rem(y + 1 + i, 4)
            def place(h, cols, v):
                for j in range(8):
                    dw[h, b, j // 2, j % 2, :, cols] = v[112 * j:112 * (j + 1)]

            place(0, slice(0, QC), tn(xv[b], grads[:, :QC]).astype(BF))
            t = tn(xv[b], grads[:, QC:]).astype(BF)
            place(0, slice(QC, QC + KC), t[:, :KC])
            place(1, slice(0, KC), t[:, KC:])
            place(1, slice(KC, QC + KC), tn(cv[b], outs[...]).astype(BF))
            swap(i).start()
            return carry

        def hop_y(d):
            return remote(dw.at[c, lax.rem(y + d, 4), :, 1], r1.at[1, d - 1], s1s.at[1, d - 1], s1r.at[1, d - 1], on_y(d))

        def hop_x(i, d):
            b = lax.rem(y + 1 + i, 4)
            return remote(dw.at[c, b, lax.rem(x + d, 4), 0], r1.at[0, d - 1, b], hs.at[i, d - 1], hr.at[i, d - 1], on_x(d))

        def chip_sum(i, carry):
            b = lax.rem(y + 1 + i, 4)
            swap(i).wait_recv()
            for j in range(4):
                dw[c, b, j] = (dw[c, b, j].astype(F32) + pair[b, j].astype(F32)).astype(BF)

            def along_y():
                hop_y(i + 1).start()

            if not isinstance(i, int):
                pl.when(i < 3)(along_y)

            for d in (1, 2, 3):
                hop_x(i, d).start()

        def step(i, carry):
            terms(i, carry)

            @pl.when(i > 0)
            def _():
                chip_sum(i - 1, carry)

            return carry

        lax.fori_loop(0, 2, step, 0)
        first(2, 1, 1)
        first(3, 2, 0)
        lax.fori_loop(2, 4, step, 0)
        chip_sum(3, 0)
        for i, w in ((4, 1), (5, 2)):
            a = share(w, i % 2)
            ship(i - 4).wait_recv()
            arr[i * HALF:(i + 1) * HALF, :] = (a + rbuf[i - 4].astype(F32)).astype(BF)
            ship(i).start()
        for h in range(2):
            cv[right, h * HALF:(h + 1) * HALF, :] = share(3, h).astype(BF)
        for d in (1, 2, 3):
            dot_note(d).wait()
        m = (dots[...] + dots_all[0] + dots_all[1] + dots_all[2]) * (1.0 / D)

        for d in (1, 2, 3):
            hop_y(d).wait_recv()
            for i in range(4):
                hop_x(i, d).wait_recv()
        for j in range(4):
            s1[1, j] = (dw[c, y, j, 1].astype(F32) + r1[1, 0, j].astype(F32) + r1[1, 1, j].astype(F32)
                        + r1[1, 2, j].astype(F32)).astype(BF)
            s1[0, j] = (dw[c, j, x, 0].astype(F32) + r1[0, 0, j].astype(F32) + r1[0, 1, j].astype(F32)
                        + r1[0, 2, j].astype(F32)).astype(BF)

        def last_x(d):
            return remote(s1.at[1, lax.rem(x + d, 4)], r2.at[1, d - 1], s2s.at[1, d - 1], s2r.at[1, d - 1], on_x(d))

        def last_y(d):
            return remote(s1.at[0, lax.rem(y + d, 4)], r2.at[0, d - 1], s2s.at[0, d - 1], s2r.at[0, d - 1], on_y(d))

        for d in (1, 2, 3):
            last_x(d).start()
            last_y(d).start()
        for d in (1, 2, 3):
            last_x(d).wait_recv()
            last_y(d).wait_recv()
        for p, own in ((0, s1[0, y]), (1, s1[1, x])):
            s2[p] = (own.astype(F32) + r2[p, 0].astype(F32) + r2[p, 1].astype(F32) + r2[p, 2].astype(F32)).astype(BF)
        trade = remote(s2.at[other], fin.at[c], fs.at[0], fr.at[0], sib)
        trade.start()
        for i in (2, 3, 4, 5):
            ship(i).wait_recv()
        gain_own = own_gain()
        for b in range(TOK // TB):
            h, r = divmod(b * TB, HALF)
            at = slice(b * TB, (b + 1) * TB)
            rows = slice(r, r + TB)
            one, two = (4, 3) if h == 0 else (2, 5)
            s = cv[right, at, :].astype(F32) + rbuf[one, rows, :].astype(F32) + rbuf[two, rows, :].astype(F32)
            mc = jnp.transpose(jnp.broadcast_to(m[:1, at], (128, TB)))[:, :1]
            inv = inv_b[at, :1]
            result[at, :] = (adv_b[at, :1] * cv[z, at, :].astype(F32) + s * gain_own
                             - packed[at, :].astype(F32) * (inv * mc)).astype(BF)
        trade.wait()
        mine = s2[c]
        got = fin[other]
        low_out[...] = jnp.where(c == 0, mine, got)
        high_out[...] = jnp.where(c == 0, got, mine)
        for i in range(6):
            ship(i).wait_send()
        for i in range(4):
            swap(i).wait_send()
        for d in (1, 2, 3):
            for i in range(4):
                hop_x(i, d).wait_send()
            hop_y(d).wait_send()
            last_x(d).wait_send()
            last_y(d).wait_send()

    pl.run_scoped(gradients, v((2, 4, 4, 2) + PART), v((2, 4) + PART))
    ring_a.sent()
    ring_b.sent()
    for loop in loops:
        loop.sent()
    for d in range(7):
        w_last(d).wait_send()
    for d in (1, 2, 3):
        tell(d).wait_send()


def split_kernel(result, low, high, res, res_q, res_k, res_v, res_o):
    res[...] = result[...]
    res_q[...] = low[:, :QC]
    res_k[...] = low[:, QC:]
    res_v[...] = high[:, :KC]
    res_o[...] = high[:, KC:]


def sds(shape, dtype=BF):
    return jax.ShapeDtypeStruct(shape, dtype)


def params(**kw):
    return pltpu.CompilerParams(vmem_limit_bytes=LIMIT, has_side_effects=True, **kw)


def rope_table():
    i = np.arange(HD // 2, dtype=np.float32)
    frequency = np.float32(ROPE_BASE) ** (-(np.float32(2.0) * i) / np.float32(HD))
    angle = np.arange(128, dtype=np.float32)[:, None] * frequency[None, :]
    c, s = np.cos(angle), np.sin(angle)
    return np.concatenate([c, c, -s, s], axis=1).astype(np.float32)


N_O = len(OFFSETS)
WIDTH = QC + 2 * KC
PART = (112, QC + KC)


def scratch(shape, dtype=BF):
    return pltpu.VMEM(shape, dtype)


def stage(*args):
    return pl.pallas_call(
        stage_kernel, out_shape=(sds((SEQ * SLAB, FA)), sds((SEQ * SLAB, FB - FA)), sds((SEQ * 8, 128), F32)),
        in_specs=[SMEM, VMEM, VMEM, VMEM], out_specs=(VMEM,) * 3, compiler_params=params(),
    )(*args)


def whole(*args):
    v = scratch
    ring = [DMA((6,)), DMA((6,))]
    return pl.pallas_call(
        whole_kernel, out_shape=(sds((TOK, FB)), sds(PART), sds(PART)),
        in_specs=[HBM] * 4 + [VMEM] * 7, out_specs=(VMEM,) * 3,
        scratch_shapes=[
            v((SEQ * SLAB, FB)), v((SEQ * 8, 128), F32),
            v((N_Z, TOK, FB)), v((N_Z, TOK, FB)), v((2,) + PART), v((2, 4, 4, 2) + PART),
            v((8, TOK), F32), v((3, 8, TOK), F32), v((TOK, 128), F32), v((TOK, 2 * HD), F32), v((TOK, 128), F32),
            v((TOK, WIDTH)), v((TOK, QC)), v((TOK, 128), F32), v((TOK, 128), F32), v((8, TOK), F32),
            v((3, 8, TOK), F32), v((6, HALF, FB)), v((4, 4, 2) + PART), v((2, 3, 4) + PART), v((2, 3) + PART),
            v((2,) + PART), v((2,) + PART),
            DMA((4,))] + [DMA((N_O,))] * 6 + ring * 3 + [DMA((4,)), DMA((4,)), DMA((1,)), DMA((1,))]
        + [DMA((2, 3))] * 2 + [DMA((7,))] * 2 + ring * 2
        + ring + [DMA((4,))] * 4 + [DMA((2, 3))] * 2 + [DMA((4, 3))] * 2 + [DMA((2, 3))] * 2 + [DMA((1,))] * 2,
        compiler_params=params(collective_id=0),
    )(*args)


def split(*args):
    return pl.pallas_call(
        split_kernel,
        out_shape=(sds((TOK, FB)), sds((112, QC)), sds((112, KC)), sds((112, KC)), sds((112, QC))),
        in_specs=[VMEM] * 3, out_specs=(VMEM,) * 5, compiler_params=params(),
    )(*args)


def per_device(roll_rows, dest, lengths, clusters, log_prob_grad, gain, w_q, w_k, w_v, w_o_t):
    send_a, send_b, meta = stage(dest, dest.reshape(1, SEQ), clusters.reshape(1, SEQ), roll_rows)
    return split(*whole(
        send_a, send_b, meta, log_prob_grad, lengths, gain, jnp.asarray(rope_table()), w_q, w_k, w_v, w_o_t))


def solution(mesh):
    in_specs = (
        P("fsdp", None, "tp"), P("fsdp"), P("fsdp", None), P("fsdp"), P("fsdp", "tp"), P(),
        P("fsdp", "tp"), P("fsdp", "tp"), P("fsdp", "tp"), P("fsdp", "tp"),
    )
    out_specs = (P("fsdp", "tp"),) * 5
    return jax.shard_map(per_device, mesh=mesh, in_specs=in_specs, out_specs=out_specs, check_vma=False)
```
